256 devices in a mesh: gx: 8 (over z), gy: 32 (over y, x, core).
Axes of the slice: x: 4, y: 4, z: 8, core: 2. Of those that a mesh axis runs over, the one named last changes fastest.
Arguments:
- tokens: bfloat16 [768, 16384], P(None, ('gx', 'gy')), may hold values from -24 to 24
- norm_attn: bfloat16 [16384], P(('gx', 'gy')), may hold values from 0.099609375 to 1.8984375
- w_query: bfloat16 [16384, 8192], P('gx', 'gy')
- w_key: bfloat16 [16384, 512], P('gx', 'gy')
- w_value: bfloat16 [16384, 512], P('gx', 'gy'), may hold values from -0.046875 to 0.046875
- w_out: bfloat16 [8192, 16384], P('gy', 'gx'), may hold values from -0.0625 to 0.0625
- norm_ffn: bfloat16 [16384], P(('gx', 'gy')), may hold values from 0.099609375 to 1.8984375
- w_gate: bfloat16 [16384, 26624], P('gx', 'gy'), may hold values from -0.046875 to 0.046875
- w_up: bfloat16 [16384, 26624], P('gx', 'gy'), may hold values from -0.046875 to 0.046875
- w_down: bfloat16 [26624, 16384], P('gy', 'gx'), may hold values from -0.0390625 to 0.0390625
- lengths: int32 [8], P('gx'), may hold values from 32 to 96
- segments: int32 [768], P('gx'), may hold values from 0 to 6, as said below
Outputs:
- block_out: bfloat16 [768, 16384], P(None, ('gx', 'gy'))
The draws below stay inside these ranges and needn't reach their ends.
Inputs may be any that keep to these rules, and one draw needn't show every extreme that they name: `segments`: within each row of 96 tokens the segment ids start at 0 and never fall.
All inputs are finite; a program needn't handle non-finite values.
Results may differ from the reference program's by a relative error of at most 0.023.
Values may be sent and summed in bfloat16 or wider, within the bound.
No kernel may reach another device: no remote copies, remote signals or barrier semaphores. Data moves between devices by JAX's collectives and lax.ppermute only.
A program may use at most 128 MiB of HBM per device.

```python
import math
import jax
import jax.numpy as jnp
from jax import lax

D = 16384
HEADS = 64
KV_HEADS = 4
HEAD_DIM = 128
FF = 26624
SEQ = 96
ROWS = 8
TOKENS = 768


def draw_tokens(key, part):
    key = jax.random.fold_in(key, 11)
    key_rows, key_cols, key_base = jax.random.split(key, 3)
    row_scale = jnp.exp(jax.random.uniform(key_rows, (TOKENS, 1), minval=-1.15, maxval=1.15))
    col_scale = jnp.exp(jnp.arange(D, dtype=jnp.float32) * (1.1 / D) + jax.random.uniform(key_cols, (1, D), minval=-0.5, maxval=0.5))
    base = jnp.clip(jax.random.normal(key_base, (TOKENS, D)), -4.0, 4.0)
    return (base * row_scale * col_scale * 0.35).astype(jnp.bfloat16)


def head_weights(key, heads_count):
    key_base = jax.random.fold_in(key, 0)
    base = jnp.clip(jax.random.normal(key_base, (D, heads_count, HEAD_DIM)), -4.0, 4.0)
    return (base * D ** (-0.5)).reshape(D, heads_count * HEAD_DIM).astype(jnp.bfloat16)


def draw_w_query(key, part):
    key = jax.random.fold_in(key, 23)
    return head_weights(key, HEADS)


def draw_w_key(key, part):
    key = jax.random.fold_in(key, 29)
    return head_weights(key, KV_HEADS)


def draw_lengths(key, part):
    key = jax.random.fold_in(key, 37)
    key_len, key_order = jax.random.split(key)
    base = jax.random.randint(key_len, (ROWS,), SEQ // 3, SEQ + 1)
    order = jax.random.permutation(key_order, ROWS)
    place = jnp.arange(ROWS, dtype=jnp.int32)
    base = jnp.where(place == order[0], SEQ, base)
    base = jnp.where(place == order[1], SEQ // 3, base)
    return base.astype(jnp.int32)


def draw_segments(key, part):
    key = jax.random.fold_in(key, 41)
    key_coin, key_pick = jax.random.split(key)
    coins = jax.random.randint(key_coin, (ROWS, SEQ), 0, 16)
    chosen = jax.random.randint(key_pick, (), 0, ROWS)
    place = jnp.arange(SEQ, dtype=jnp.int32)[None, :]
    row_ids = jnp.arange(ROWS, dtype=jnp.int32)[:, None]
    forced = (row_ids == chosen) & (place % 8 == 4)
    starts = jnp.where((coins == 0) & (place > 0) | forced, 1, 0).astype(jnp.int32)
    ids = jnp.minimum(jnp.cumsum(starts, axis=1), SEQ // 16)
    return ids.astype(jnp.int32).reshape(TOKENS)


def shard_levels(own_key, shape, cuts, low, top_value):
    def one(dim, parts):
        heights = jax.random.uniform(jax.random.fold_in(jax.random.fold_in(own_key, 6), dim), (parts,), jnp.float32, low / len(cuts), top_value / len(cuts))
        return jnp.repeat(jnp.exp(heights), shape[dim] // parts).reshape((-1,) + (1,) * (len(shape) - dim - 1))

    level = one(*cuts[0])
    for cut in cuts[1:]:
        level = level * one(*cut)
    return level


def centred(own_key, extent, deviation, reach, pieces=(), kind=jnp.bfloat16):
    loudness = shard_levels(own_key, extent, pieces, -0.22, 0.18) if pieces else 1.0
    entries = jax.random.normal(own_key, extent, jnp.float32) * deviation * loudness
    return jnp.minimum(jnp.maximum(entries, -reach), reach).astype(kind)


def setup_inputs(seed: int = 0) -> dict:
    key_of = jax.random.split(jax.random.key(seed), 13)
    return {
        "tokens": draw_tokens(jax.random.fold_in(key_of[12], 71), 0),
        "norm_attn": jnp.clip(1.0 + 0.18 * jax.random.normal(key_of[1], (D,), jnp.float32), 0.099609375, 1.8984375).astype(jnp.bfloat16),
        "w_query": draw_w_query(jax.random.fold_in(key_of[12], 71), 0),
        "w_key": draw_w_key(jax.random.fold_in(key_of[12], 71), 0),
        "w_value": centred(key_of[4], (D, KV_HEADS * HEAD_DIM), D ** -0.5, 0.046875, ((0, 8), (1, 32))),
        "w_out": centred(key_of[5], (HEADS * HEAD_DIM, D), (HEADS * HEAD_DIM) ** -0.5, 0.0625, ((0, 32), (1, 8))),
        "norm_ffn": jnp.clip(1.0 + 0.18 * jax.random.normal(key_of[6], (D,), jnp.float32), 0.099609375, 1.8984375).astype(jnp.bfloat16),
        "w_gate": centred(key_of[7], (D, FF), D ** -0.5, 0.046875, ((0, 8), (1, 32))),
        "w_up": centred(key_of[8], (D, FF), D ** -0.5, 0.046875, ((0, 8), (1, 32))),
        "w_down": centred(key_of[9], (FF, D), FF ** -0.5, 0.0390625, ((0, 32), (1, 8))),
        "lengths": draw_lengths(jax.random.fold_in(key_of[12], 71), 0),
        "segments": draw_segments(jax.random.fold_in(key_of[12], 71), 0),
    }


EPS = 1e-05
ROPE_BASE = 500000.0

def rms_norm(values, gain):
    wide = values.astype(jnp.float32)
    inv_rms = lax.rsqrt(lax.optimization_barrier(jnp.sum(wide * wide, axis=1, keepdims=True)) / D + EPS)
    return (wide * inv_rms * gain.astype(jnp.float32)[None, :]).astype(jnp.bfloat16)

def rotate_pairs(heads_block, positions):
    half_dim = HEAD_DIM // 2
    inv_freq = jnp.power(ROPE_BASE, -(jnp.arange(half_dim, dtype=jnp.float32) * 2.0 / HEAD_DIM))
    angles = positions.astype(jnp.float32)[:, None] * inv_freq[None, :]
    cosine = jnp.cos(angles)[:, None, :]
    sine_part = jnp.sin(angles)[:, None, :]
    first_half = heads_block[..., :half_dim]
    second_half = heads_block[..., half_dim:]
    return jnp.concatenate([first_half * cosine - second_half * sine_part, second_half * cosine + first_half * sine_part], axis=-1)

def one_row(packed):
    query, keys, values, seg_row, length = packed
    group = HEADS // KV_HEADS
    keys_all = jnp.repeat(keys, group, axis=1).astype(jnp.float32)
    values_all = jnp.repeat(values, group, axis=1).astype(jnp.float32)
    scores = jnp.einsum('qhd,khd->hqk', query.astype(jnp.float32), keys_all) * (1.0 / math.sqrt(HEAD_DIM))
    place = jnp.arange(SEQ, dtype=jnp.int32)
    allowed = (seg_row[:, None] == seg_row[None, :]) & (place[None, :] <= place[:, None]) & (place[None, :] < length)
    allowed = allowed | (place[None, :] == place[:, None])
    scores = jnp.where(allowed[None, :, :], scores, jnp.float32(-1e+30))
    row_max = lax.optimization_barrier(jnp.max(scores, axis=-1, keepdims=True))
    expo = jnp.exp(scores - row_max)
    soft = (expo / lax.optimization_barrier(jnp.sum(expo, axis=-1, keepdims=True))).astype(jnp.bfloat16)
    return jnp.einsum('hqk,khd->qhd', soft.astype(jnp.float32), values_all).astype(jnp.bfloat16)

def reference(tokens, norm_attn, w_query, w_key, w_value, w_out, norm_ffn, w_gate, w_up, w_down, lengths, segments):
    normed_a = rms_norm(tokens, norm_attn)
    query_raw = jnp.dot(normed_a, w_query, preferred_element_type=jnp.float32)
    key_raw = jnp.dot(normed_a, w_key, preferred_element_type=jnp.float32)
    value_raw = jnp.dot(normed_a, w_value, preferred_element_type=jnp.float32)
    positions = jnp.arange(TOKENS, dtype=jnp.int32) % SEQ
    query = rotate_pairs(query_raw.reshape(TOKENS, HEADS, HEAD_DIM), positions).astype(jnp.bfloat16)
    keys = rotate_pairs(key_raw.reshape(TOKENS, KV_HEADS, HEAD_DIM), positions).astype(jnp.bfloat16)
    values = value_raw.astype(jnp.bfloat16).reshape(TOKENS, KV_HEADS, HEAD_DIM)
    attended = lax.map(one_row, (query.reshape(ROWS, SEQ, HEADS, HEAD_DIM), keys.reshape(ROWS, SEQ, KV_HEADS, HEAD_DIM), values.reshape(ROWS, SEQ, KV_HEADS, HEAD_DIM), segments.reshape(ROWS, SEQ), lengths))
    attended = attended.reshape(TOKENS, HEADS * HEAD_DIM)
    residual = (tokens.astype(jnp.float32) + jnp.dot(attended, w_out, preferred_element_type=jnp.float32)).astype(jnp.bfloat16)
    normed_f = rms_norm(residual, norm_ffn)
    gate_sum = jnp.dot(normed_f, w_gate, preferred_element_type=jnp.float32)
    up_sum = jnp.dot(normed_f, w_up, preferred_element_type=jnp.float32)
    hidden = (jax.nn.silu(gate_sum) * up_sum).astype(jnp.bfloat16)
    return (residual.astype(jnp.float32) + jnp.dot(hidden, w_down, preferred_element_type=jnp.float32)).astype(jnp.bfloat16)
```

```python
import math

import jax
import jax.numpy as jnp
import numpy as np
from jax import lax
from jax.experimental import pallas as pl
from jax.experimental.pallas import tpu as pltpu
from jax.sharding import PartitionSpec as P

D = 16384
HEADS = 64
KV_HEADS = 4
HEAD_DIM = 128
SEQ = 96
EPS = 1e-05
ROPE_BASE = 500000.0

BF = jnp.bfloat16
F32 = jnp.float32

TOK = 768
HALF = 384
CHIPS = 16
LANE = 128
ROWS = 8
KSTEP = 4
FFL = 832
MAIN = 640
REST = FFL - MAIN
SIDE = 512
UP_AT = 256
CHIP_GROUPS = [[2 * i + c for i in range(CHIPS)] for c in range(2)]
KV_GROUPS = [list(range(8 * i, 8 * i + 8)) for i in range(4)]
VMEM = 48 * 1024 * 1024


def swap(x):
    return lax.ppermute(x, "gy", [(i, i ^ 1) for i in range(32)])


def over_chips(x):
    return lax.all_to_all(x, "gy", 0, 0, axis_index_groups=CHIP_GROUPS, tiled=True)


def over_rows(x):
    return lax.all_to_all(x, "gx", 0, 0, tiled=True)


def params(**kw):
    return pltpu.CompilerParams(vmem_limit_bytes=VMEM, **kw)


def nt(a, b):
    return lax.dot_general(a, b, (((1,), (1,)), ((), ())), preferred_element_type=F32)


def nn(a, b):
    return jnp.dot(a, b, preferred_element_type=F32)


def fold_squares(wide):
    total = None
    for j in range(wide.shape[1] // LANE):
        part = wide[:, j * LANE : (j + 1) * LANE]
        total = part * part if total is None else total + part * part
    return total


def split_two(total):
    high = total.astype(BF).astype(F32)
    return high, total - high


def qkv_kernel(h_ref, x_ref, g_ref, wq_ref, wk_ref, wv_ref, *rest):
    out_ref, acc_q, acc_kv, acc_sq = rest[-4:]
    k = pl.program_id(0)

    @pl.when(k == 0)
    def _():
        acc_q[...] = jnp.zeros_like(acc_q)
        acc_kv[...] = jnp.zeros_like(acc_kv)
        acc_sq[...] = jnp.zeros_like(acc_sq)

    wide = jnp.concatenate([x_ref[j] for j in range(x_ref.shape[0])], axis=1).astype(F32)
    acc_sq[...] += fold_squares(wide)
    gained = (wide * g_ref[...]).astype(BF)
    acc_q[...] += nn(gained, wq_ref[...])
    depth = gained.shape[1]
    kv = jnp.concatenate([wk_ref[...], wv_ref[...], jnp.zeros((LANE - 32, depth), BF)], axis=0)
    acc_kv[...] += nt(gained, kv)

    @pl.when(k == pl.num_programs(0) - 1)
    def _():
        high, low = split_two(jnp.sum(acc_sq[...], axis=1, keepdims=True))
        lane = lax.broadcasted_iota(jnp.int32, (HALF, LANE), 1)
        tail = jnp.where(lane == 32, high, jnp.where(lane == 33, low, acc_kv[...]))
        out_ref[:, :256] = acc_q[...].astype(BF)
        out_ref[:, 256:] = tail.astype(BF)


def qkv_half(h, x, gain, wq, wk_t, wv_t, held=None):
    depth = 2048 // KSTEP
    in_specs = [
        pl.BlockSpec((CHIPS // KSTEP, HALF, LANE), lambda k, h: (k, 0, 0)),
        pl.BlockSpec((1, depth), lambda k, h: (0, k)),
        pl.BlockSpec((depth, 256), lambda k, h: (k, 0)),
        pl.BlockSpec((16, depth), lambda k, h: (0, k)),
        pl.BlockSpec((16, depth), lambda k, h: (0, k)),
    ]
    operands = [h, x, gain, wq, wk_t, wv_t]
    aliases = {}
    if held is not None:
        in_specs.append(pl.BlockSpec(memory_space=pl.ANY))
        operands.append(held)
        aliases = {6: 0}
    return pl.pallas_call(
        qkv_kernel,
        grid_spec=pltpu.PrefetchScalarGridSpec(
            num_scalar_prefetch=1,
            grid=(KSTEP,),
            in_specs=in_specs,
            out_specs=pl.BlockSpec((HALF, 384), lambda k, h: (h[0], 0)),
            scratch_shapes=[
                pltpu.VMEM((HALF, 256), F32),
                pltpu.VMEM((HALF, LANE), F32),
                pltpu.VMEM((HALF, LANE), F32),
            ],
        ),
        out_shape=jax.ShapeDtypeStruct((TOK, 384), BF),
        input_output_aliases=aliases,
        compiler_params=params(),
        cost_estimate=pl.CostEstimate(
            flops=2 * HALF * 2048 * 384, bytes_accessed=4 * 1024 * 1024, transcendentals=0
        ),
        name="qkv_half",
    )(*operands)


def qkv_sum_kernel(p_ref, q_ref, kv_ref):
    total = p_ref[0].astype(F32)
    for j in range(1, ROWS):
        total = total + p_ref[j].astype(F32)
    tail = total[:, 256:]
    squares = tail[:, 32:33] + tail[:, 33:34]
    inv = lax.rsqrt(squares / D + EPS)
    q_ref[...] = total[:, :256] * inv
    kv = tail[:, :32] * inv
    for j in range(8):
        kv_ref[j] = kv


def qkv_sum(parts):
    return pl.pallas_call(
        qkv_sum_kernel,
        out_shape=(
            jax.ShapeDtypeStruct((SEQ, 256), F32),
            jax.ShapeDtypeStruct((8, SEQ, 32), F32),
        ),
        compiler_params=params(),
        name="qkv_sum",
    )(parts)


def attend_kernel(len_ref, q_ref, kv_ref, segr_ref, segc_ref, cos_ref, sin_ref, out_ref):
    def rotate(x):
        return (x * cos_ref[...] + pltpu.roll(x, 64, 1) * sin_ref[...]).astype(BF)

    keys = rotate(jnp.concatenate([kv_ref[j][:, :16] for j in range(8)], axis=1))
    values = jnp.concatenate([kv_ref[j][:, 16:32] for j in range(8)], axis=1).astype(BF)
    q_at = lax.broadcasted_iota(jnp.int32, (SEQ, SEQ), 0)
    k_at = lax.broadcasted_iota(jnp.int32, (SEQ, SEQ), 1)
    allowed = (segr_ref[...] == segc_ref[...]) & (k_at <= q_at) & (k_at < len_ref[0])
    allowed = allowed | (k_at == q_at)
    for head in range(2):
        query = rotate(q_ref[:, head * HEAD_DIM : (head + 1) * HEAD_DIM])
        scores = nt(query, keys) * (1.0 / math.sqrt(HEAD_DIM))
        scores = jnp.where(allowed, scores, F32(-1e30))
        expo = jnp.exp(scores - jnp.max(scores, axis=1, keepdims=True))
        soft = (expo / jnp.sum(expo, axis=1, keepdims=True)).astype(BF)
        attended = nn(soft, values).astype(BF)
        for j in range(ROWS):
            out_ref[j, :, head * HEAD_DIM : (head + 1) * HEAD_DIM] = attended


def attend(lengths, q, kv, segments, cos, sin):
    vmem = pl.BlockSpec(memory_space=pltpu.VMEM)
    return pl.pallas_call(
        attend_kernel,
        in_specs=[pl.BlockSpec(memory_space=pltpu.SMEM)] + [vmem] * 6,
        out_specs=vmem,
        out_shape=jax.ShapeDtypeStruct((ROWS, SEQ, 256), BF),
        compiler_params=params(),
        name="attend",
    )(lengths, q, kv, segments.reshape(1, SEQ), segments.reshape(SEQ, 1), cos, sin)


def proj_kernel(h_ref, x_ref, w_ref, out_ref):
    result = nn(x_ref[...], w_ref[...]).astype(out_ref.dtype)
    for j in range(out_ref.shape[0]):
        out_ref[j] = result[:, j * LANE : (j + 1) * LANE]


def proj_half(h, x, w, dtype):
    depth = x.shape[1]
    steps = 4
    wide = 2048 // steps
    return pl.pallas_call(
        proj_kernel,
        grid_spec=pltpu.PrefetchScalarGridSpec(
            num_scalar_prefetch=1,
            grid=(steps,),
            in_specs=[
                pl.BlockSpec((HALF, depth), lambda i, h: (h[0], 0)),
                pl.BlockSpec((depth, wide), lambda i, h: (0, i)),
            ],
            out_specs=pl.BlockSpec((wide // LANE, HALF, LANE), lambda i, h: (i, 0, 0)),
        ),
        out_shape=jax.ShapeDtypeStruct((CHIPS, HALF, LANE), dtype),
        compiler_params=params(),
        cost_estimate=pl.CostEstimate(
            flops=2 * HALF * 2048 * depth, bytes_accessed=4 * 1024 * 1024, transcendentals=0
        ),
        name="proj_half",
    )(h, x, w)


def project_out(c, x, w):
    given = proj_half(1 - c, x, w, BF)
    got = swap(given)
    kept = proj_half(c, x, w, F32)
    return over_chips((kept + got.astype(F32)).astype(BF))


def residual_kernel(base_ref, p_ref, out_ref, copies_ref):
    total = p_ref[0].astype(F32)
    for j in range(1, CHIPS):
        total = total + p_ref[j].astype(F32)
    result = (base_ref[...].astype(F32) + total).astype(BF)
    out_ref[...] = result
    for j in range(CHIPS):
        copies_ref[j] = result


def residual_copies(base, parts):
    return pl.pallas_call(
        residual_kernel,
        out_shape=(
            jax.ShapeDtypeStruct((HALF, LANE), BF),
            jax.ShapeDtypeStruct((CHIPS, HALF, LANE), BF),
        ),
        compiler_params=params(),
        name="residual_copies",
    )(base, parts)


def final_kernel(base_ref, p_ref, out_ref):
    total = p_ref[0].astype(F32)
    for j in range(1, CHIPS):
        total = total + p_ref[j].astype(F32)
    out_ref[...] = (base_ref[...].astype(F32) + total).astype(BF)


def final_sum(base, parts):
    return pl.pallas_call(
        final_kernel,
        out_shape=jax.ShapeDtypeStruct((HALF, LANE), BF),
        compiler_params=params(),
        name="final_sum",
    )(base, parts)


def gate_up_kernel(h_ref, x_ref, g_ref, wg_ref, wu_ref, *rest):
    main_ref, side_ref, acc_g, acc_u, acc_sq = rest[-5:]
    k = pl.program_id(0)

    @pl.when(k == 0)
    def _():
        acc_g[...] = jnp.zeros_like(acc_g)
        acc_u[...] = jnp.zeros_like(acc_u)
        acc_sq[...] = jnp.zeros_like(acc_sq)

    wide = jnp.concatenate([x_ref[j] for j in range(x_ref.shape[0])], axis=1).astype(F32)
    acc_sq[...] += fold_squares(wide)
    gained = (wide * g_ref[...]).astype(BF)
    acc_g[...] += nt(gained, wg_ref[...])
    acc_u[...] += nt(gained, wu_ref[...])

    @pl.when(k == pl.num_programs(0) - 1)
    def _():
        high, low = split_two(jnp.sum(acc_sq[...], axis=1, keepdims=True))
        main_ref[:, :MAIN] = acc_g[:, :MAIN].astype(BF)
        main_ref[:, MAIN:] = acc_u[:, :MAIN].astype(BF)
        lane = lax.broadcasted_iota(jnp.int32, (HALF, 64), 1)
        extra = jnp.where(lane == 0, high, jnp.where(lane == 1, low, 0.0))
        side_ref[:, :UP_AT] = jnp.concatenate([acc_g[:, MAIN:], extra], axis=1).astype(BF)
        side_ref[:, UP_AT:] = jnp.concatenate(
            [acc_u[:, MAIN:], jnp.zeros((HALF, 64), F32)], axis=1
        ).astype(BF)


def gate_up_half(h, x, gain, wg_t, wu_t, held=None):
    depth = 2048 // KSTEP
    in_specs = [
        pl.BlockSpec((CHIPS // KSTEP, HALF, LANE), lambda k, h: (k, 0, 0)),
        pl.BlockSpec((1, depth), lambda k, h: (0, k)),
        pl.BlockSpec((FFL, depth), lambda k, h: (0, k)),
        pl.BlockSpec((FFL, depth), lambda k, h: (0, k)),
    ]
    operands = [h, x, gain, wg_t, wu_t]
    aliases = {}
    if held is not None:
        in_specs += [pl.BlockSpec(memory_space=pl.ANY)] * 2
        operands += list(held)
        aliases = {5: 0, 6: 1}
    return pl.pallas_call(
        gate_up_kernel,
        grid_spec=pltpu.PrefetchScalarGridSpec(
            num_scalar_prefetch=1,
            grid=(KSTEP,),
            in_specs=in_specs,
            out_specs=[
                pl.BlockSpec((HALF, 2 * MAIN), lambda k, h: (h[0], 0)),
                pl.BlockSpec((HALF, SIDE), lambda k, h: (h[0], 0)),
            ],
            scratch_shapes=[
                pltpu.VMEM((HALF, FFL), F32),
                pltpu.VMEM((HALF, FFL), F32),
                pltpu.VMEM((HALF, LANE), F32),
            ],
        ),
        out_shape=(
            jax.ShapeDtypeStruct((TOK, 2 * MAIN), BF),
            jax.ShapeDtypeStruct((TOK, SIDE), BF),
        ),
        input_output_aliases=aliases,
        compiler_params=params(),
        cost_estimate=pl.CostEstimate(
            flops=2 * HALF * 2048 * 2 * FFL, bytes_accessed=10 * 1024 * 1024, transcendentals=0
        ),
        name="gate_up_half",
    )(*operands)


def hidden_kernel(main_ref, side_ref, out_ref):
    side = side_ref[0].astype(F32)
    for j in range(1, ROWS):
        side = side + side_ref[j].astype(F32)
    squares = side[:, REST : REST + 1] + side[:, REST + 1 : REST + 2]
    inv = lax.rsqrt(squares / D + EPS)

    def gated(gate, up):
        gate, up = gate * inv, up * inv
        return (gate / (1.0 + jnp.exp(-gate)) * up).astype(BF)

    first = gated(main_ref[:, :MAIN].astype(F32), main_ref[:, MAIN:].astype(F32))
    second = gated(side[:, :REST], side[:, UP_AT : UP_AT + REST])
    for j in range(ROWS):
        out_ref[j, :, :MAIN] = first
        out_ref[j, :, MAIN:] = second


def hidden_copies(main, side):
    return pl.pallas_call(
        hidden_kernel,
        out_shape=jax.ShapeDtypeStruct((ROWS, SEQ, FFL), BF),
        compiler_params=params(),
        name="hidden_copies",
    )(main, side)


def rope_tables():
    inv_freq = np.power(
        np.float32(ROPE_BASE), -(np.arange(64, dtype=np.float32) * np.float32(2.0 / HEAD_DIM))
    ).astype(np.float32)
    angles = np.arange(SEQ, dtype=np.float32)[:, None] * inv_freq[None, :]
    cos, sin = np.cos(angles.astype(np.float64)), np.sin(angles.astype(np.float64))
    return (
        np.concatenate([cos, cos], axis=1).astype(np.float32),
        np.concatenate([-sin, sin], axis=1).astype(np.float32),
    )


def per_device(
    tokens,
    norm_attn,
    w_query,
    w_key,
    w_value,
    w_out,
    norm_ffn,
    w_gate,
    w_up,
    w_down,
    lengths,
    segments,
):
    core = lax.axis_index("gy") % 2
    c = jnp.reshape(core, (1,)).astype(jnp.int32)
    gains = lax.all_gather(jnp.stack([norm_attn, norm_ffn]), "gy", axis=1, tiled=True).astype(F32)
    gain_a, gain_f = gains[0:1], gains[1:2]
    cos, sin = rope_tables()

    mine = lax.dynamic_slice_in_dim(tokens, core * HALF, HALF, 0)
    theirs = swap(lax.dynamic_slice_in_dim(tokens, (1 - core) * HALF, HALF, 0))
    base = jnp.where(
        core == 0,
        jnp.concatenate([mine, theirs], axis=1),
        jnp.concatenate([theirs, mine], axis=1),
    )

    own = over_chips(jnp.broadcast_to(base[None], (CHIPS, HALF, LANE)))
    other = swap(own)
    held = qkv_half(c, own, gain_a, w_query, w_key.T, w_value.T)
    parts = qkv_half(1 - c, other, gain_a, w_query, w_key.T, w_value.T, held)
    q, kv = qkv_sum(over_rows(parts.reshape(ROWS, SEQ, 384)))
    kv = lax.all_to_all(kv, "gy", 0, 0, axis_index_groups=KV_GROUPS, tiled=True)
    attended = attend(lengths, q, kv, segments, cos, sin)
    attended = over_rows(attended).reshape(TOK, 256)
    residual, copies = residual_copies(base, project_out(c, attended, w_out))

    own = over_chips(copies)
    other = swap(own)
    held = gate_up_half(c, own, gain_f, w_gate.T, w_up.T)
    main, side = gate_up_half(1 - c, other, gain_f, w_gate.T, w_up.T, held)
    main = lax.psum_scatter(main, "gx", scatter_dimension=0, tiled=True)
    side = over_rows(side.reshape(ROWS, SEQ, SIDE))
    hidden = over_rows(hidden_copies(main, side)).reshape(TOK, FFL)
    done = final_sum(residual, project_out(c, hidden, w_down))

    keep = lax.dynamic_slice_in_dim(done, core * 64, 64, 1)
    got = swap(lax.dynamic_slice_in_dim(done, (1 - core) * 64, 64, 1))
    return jnp.where(
        core == 0,
        jnp.concatenate([keep, got], axis=0),
        jnp.concatenate([got, keep], axis=0),
    )


def solution(mesh):
    in_specs = (
        P(None, ("gx", "gy")),
        P(("gx", "gy")),
        P("gx", "gy"),
        P("gx", "gy"),
        P("gx", "gy"),
        P("gy", "gx"),
        P(("gx", "gy")),
        P("gx", "gy"),
        P("gx", "gy"),
        P("gy", "gx"),
        P("gx"),
        P("gx"),
    )
    out_specs = P(None, ("gx", "gy"))
    return jax.shard_map(
        per_device, mesh=mesh, in_specs=in_specs, out_specs=out_specs, check_vma=False
    )
```

```python
import functools
import math

import jax
import jax.numpy as jnp
import numpy as np
from jax import lax
from jax.experimental import pallas as pl
from jax.experimental.pallas import tpu as pltpu
from jax.sharding import PartitionSpec as P

D = 16384
HEADS = 64
KV_HEADS = 4
HEAD_DIM = 128
SEQ = 96
EPS = 1e-05
ROPE_BASE = 500000.0

BF = jnp.bfloat16
F32 = jnp.float32

TOK = 768
HALF = 384
CHIPS = 16
LANE = 128
ROWS = 8
KSTEP = 4
FFL = 832
MAIN = 512
REST = FFL - MAIN
SIDE = 768
CHIP_GROUPS = [[2 * i + c for i in range(CHIPS)] for c in range(2)]
KV_GROUPS = [list(range(8 * i, 8 * i + 8)) for i in range(4)]
VMEM = 48 * 1024 * 1024


def swap(x):
    return lax.ppermute(x, "gy", [(i, i ^ 1) for i in range(32)])


def over_chips(x):
    return lax.all_to_all(x, "gy", 0, 0, axis_index_groups=CHIP_GROUPS, tiled=True)


def over_rows(x):
    return lax.all_to_all(x, "gx", 0, 0, tiled=True)


def params(**kw):
    return pltpu.CompilerParams(vmem_limit_bytes=VMEM, **kw)


def nt(a, b):
    return lax.dot_general(a, b, (((1,), (1,)), ((), ())), preferred_element_type=F32)


def nn(a, b):
    return jnp.dot(a, b, preferred_element_type=F32)


def fold_squares(wide):
    total = None
    for j in range(wide.shape[1] // LANE):
        part = wide[:, j * LANE : (j + 1) * LANE]
        total = part * part if total is None else total + part * part
    return total


def split_two(total):
    high = total.astype(BF).astype(F32)
    return high, total - high


def gained_block(x_ref, g_ref, row):
    chips = range(x_ref.shape[0])
    wide = jnp.concatenate([x_ref[j, :HALF] for j in chips], axis=1).astype(F32)
    gain = jnp.concatenate([g_ref[j, row : row + 1] for j in chips], axis=1).astype(F32)
    return wide, (wide * gain).astype(BF)


def qkv_kernel(h_ref, x_ref, g_ref, wq_ref, wk_ref, wv_ref, *rest):
    out_ref, acc_q, acc_kv, acc_sq = rest[-4:]
    k = pl.program_id(0)

    @pl.when(k == 0)
    def _():
        acc_q[...] = jnp.zeros_like(acc_q)
        acc_kv[...] = jnp.zeros_like(acc_kv)
        acc_sq[...] = jnp.zeros_like(acc_sq)

    wide, gained = gained_block(x_ref, g_ref, 0)
    acc_sq[...] += fold_squares(wide)
    acc_q[...] += nn(gained, wq_ref[...])
    acc_kv[...] += nt(jnp.concatenate([wk_ref[...], wv_ref[...]], axis=0), gained)

    @pl.when(k == pl.num_programs(0) - 1)
    def _():
        high, low = split_two(jnp.sum(jnp.transpose(acc_sq[...]), axis=0, keepdims=True))
        at = lax.broadcasted_iota(jnp.int32, (16, SEQ), 0)
        gap = jnp.zeros((16, LANE - SEQ), F32)
        for r in range(HALF // SEQ):
            here = slice(r * SEQ, (r + 1) * SEQ)
            out_ref[r, :SEQ] = acc_q[here].astype(BF)
            kv = acc_kv[:, here]
            sums = jnp.where(at == 0, high[:, here], jnp.where(at == 1, low[:, here], 0.0))
            top = jnp.concatenate([kv[:16], gap, kv[16:], gap], axis=1)
            bottom = jnp.concatenate([sums, gap, sums, gap], axis=1)
            out_ref[r, SEQ:] = jnp.concatenate([top, bottom], axis=0).astype(BF)


def qkv_half(h, x, gains, wq, wk_t, wv_t, held=None):
    depth = 2048 // KSTEP
    chips = CHIPS // KSTEP
    in_specs = [
        pl.BlockSpec((chips, HALF, LANE), lambda k, h: (k, 0, 0)),
        pl.BlockSpec((chips, 16, LANE), lambda k, h: (k, HALF // 16, 0)),
        pl.BlockSpec((depth, 256), lambda k, h: (k, 0)),
        pl.BlockSpec((16, depth), lambda k, h: (0, k)),
        pl.BlockSpec((16, depth), lambda k, h: (0, k)),
    ]
    operands = [h, x, gains, wq, wk_t, wv_t]
    aliases = {}
    if held is not None:
        in_specs.append(pl.BlockSpec(memory_space=pl.ANY))
        operands.append(held)
        aliases = {6: 0}
    return pl.pallas_call(
        qkv_kernel,
        grid_spec=pltpu.PrefetchScalarGridSpec(
            num_scalar_prefetch=1,
            grid=(KSTEP,),
            in_specs=in_specs,
            out_specs=pl.BlockSpec((HALF // SEQ, 128, 256), lambda k, h: (h[0], 0, 0)),
            scratch_shapes=[
                pltpu.VMEM((HALF, 256), F32),
                pltpu.VMEM((32, HALF), F32),
                pltpu.VMEM((HALF, LANE), F32),
            ],
        ),
        out_shape=jax.ShapeDtypeStruct((ROWS, 128, 256), BF),
        input_output_aliases=aliases,
        compiler_params=params(),
        cost_estimate=pl.CostEstimate(
            flops=2 * HALF * 2048 * 384, bytes_accessed=4 * 1024 * 1024, transcendentals=0
        ),
        name="qkv_half",
    )(*operands)


def qkv_sum_kernel(p_ref, q_ref, kv_ref):
    total = p_ref[0].astype(F32)
    for j in range(1, ROWS):
        total = total + p_ref[j].astype(F32)
    squares = total[112:113, :LANE] + total[113:114, :LANE]
    inv = lax.rsqrt(squares / D + EPS)
    down = jnp.transpose(jnp.broadcast_to(inv, (LANE, LANE)))[:SEQ]
    q_ref[...] = total[:SEQ] * jnp.concatenate([down, down], axis=1)
    kv = jnp.concatenate([total[96:112, :SEQ], total[96:112, LANE : LANE + SEQ]], axis=0)
    kv = kv * inv[:, :SEQ]
    for j in range(8):
        kv_ref[j] = kv


def qkv_sum(parts):
    return pl.pallas_call(
        qkv_sum_kernel,
        out_shape=(
            jax.ShapeDtypeStruct((SEQ, 256), F32),
            jax.ShapeDtypeStruct((8, 32, SEQ), F32),
        ),
        compiler_params=params(),
        name="qkv_sum",
    )(parts)


def attend_kernel(
    len_ref, q_ref, kv_ref, segr_ref, segc_ref, cos_ref, sin_ref, cost_ref, sint_ref, out_ref
):
    keys = jnp.concatenate([kv_ref[j, :16] for j in range(8)], axis=0)
    turned = jnp.concatenate([keys[64:], keys[:64]], axis=0)
    keys = (keys * cost_ref[...] + turned * sint_ref[...]).astype(BF)
    values = jnp.concatenate([kv_ref[j, 16:] for j in range(8)], axis=0).astype(BF)
    q_at = lax.broadcasted_iota(jnp.int32, (SEQ, SEQ), 0)
    k_at = lax.broadcasted_iota(jnp.int32, (SEQ, SEQ), 1)
    allowed = (segr_ref[...] == segc_ref[...]) & (k_at <= q_at) & (k_at < len_ref[0])
    allowed = allowed | (k_at == q_at)
    for head in range(2):
        query = q_ref[:, head * HEAD_DIM : (head + 1) * HEAD_DIM]
        query = (query * cos_ref[...] + pltpu.roll(query, 64, 1) * sin_ref[...]).astype(BF)
        scores = nn(query, keys) * (1.0 / math.sqrt(HEAD_DIM))
        scores = jnp.where(allowed, scores, F32(-1e30))
        expo = jnp.exp(scores - jnp.max(scores, axis=1, keepdims=True))
        soft = (expo / jnp.sum(expo, axis=1, keepdims=True)).astype(BF)
        attended = nt(soft, values).astype(BF)
        for j in range(ROWS):
            out_ref[j, :, head * HEAD_DIM : (head + 1) * HEAD_DIM] = attended


def attend(lengths, q, kv, segments):
    cos, sin = rope_tables()
    vmem = pl.BlockSpec(memory_space=pltpu.VMEM)
    return pl.pallas_call(
        attend_kernel,
        in_specs=[pl.BlockSpec(memory_space=pltpu.SMEM)] + [vmem] * 8,
        out_specs=vmem,
        out_shape=jax.ShapeDtypeStruct((ROWS, SEQ, 256), BF),
        compiler_params=params(),
        name="attend",
    )(
        lengths,
        q,
        kv,
        segments.reshape(1, SEQ),
        segments.reshape(SEQ, 1),
        cos,
        sin,
        np.ascontiguousarray(cos.T),
        np.ascontiguousarray(sin.T),
    )


def proj_kernel(h_ref, x_ref, w_ref, out_ref):
    result = nn(x_ref[...], w_ref[...]).astype(out_ref.dtype)
    for j in range(out_ref.shape[0]):
        out_ref[j] = result[:, j * LANE : (j + 1) * LANE]


def proj_half(h, x, w, dtype):
    depth = x.shape[1]
    steps = 4
    wide = 2048 // steps
    return pl.pallas_call(
        proj_kernel,
        grid_spec=pltpu.PrefetchScalarGridSpec(
            num_scalar_prefetch=1,
            grid=(steps,),
            in_specs=[
                pl.BlockSpec((HALF, depth), lambda i, h: (h[0], 0)),
                pl.BlockSpec((depth, wide), lambda i, h: (0, i)),
            ],
            out_specs=pl.BlockSpec((wide // LANE, HALF, LANE), lambda i, h: (i, 0, 0)),
        ),
        out_shape=jax.ShapeDtypeStruct((CHIPS, HALF, LANE), dtype),
        compiler_params=params(),
        cost_estimate=pl.CostEstimate(
            flops=2 * HALF * 2048 * depth, bytes_accessed=4 * 1024 * 1024, transcendentals=0
        ),
        name="proj_half",
    )(h, x, w)


def project_out(c, x, w):
    given = proj_half(1 - c, x, w, BF)
    got = swap(given)
    kept = proj_half(c, x, w, F32)
    return over_chips((kept + got.astype(F32)).astype(BF))


def residual_kernel(base_ref, p_ref, out_ref, copies_ref):
    total = p_ref[0].astype(F32)
    for j in range(1, CHIPS):
        total = total + p_ref[j].astype(F32)
    result = (base_ref[:HALF].astype(F32) + total).astype(BF)
    out_ref[...] = result
    for j in range(CHIPS):
        copies_ref[j] = result


def residual_copies(base, parts):
    return pl.pallas_call(
        residual_kernel,
        out_shape=(
            jax.ShapeDtypeStruct((HALF, LANE), BF),
            jax.ShapeDtypeStruct((CHIPS, HALF, LANE), BF),
        ),
        compiler_params=params(),
        name="residual_copies",
    )(base, parts)


def final_kernel(base_ref, p_ref, out_ref):
    total = p_ref[0].astype(F32)
    for j in range(1, CHIPS):
        total = total + p_ref[j].astype(F32)
    out_ref[...] = (base_ref[...].astype(F32) + total).astype(BF)


def final_sum(base, parts):
    return pl.pallas_call(
        final_kernel,
        out_shape=jax.ShapeDtypeStruct((HALF, LANE), BF),
        compiler_params=params(),
        name="final_sum",
    )(base, parts)


def gate_up_kernel(with_sums, h_ref, x_ref, g_ref, wg_ref, wu_ref, *rest):
    if with_sums:
        out_ref, acc_g, acc_u, acc_sq = rest[-4:]
    else:
        out_ref, acc_g, acc_u = rest[-3:]
    k = pl.program_id(0)

    @pl.when(k == 0)
    def _():
        acc_g[...] = jnp.zeros_like(acc_g)
        acc_u[...] = jnp.zeros_like(acc_u)
        if with_sums:
            acc_sq[...] = jnp.zeros_like(acc_sq)

    wide, gained = gained_block(x_ref, g_ref, 1)
    acc_g[...] += nt(gained, wg_ref[...])
    acc_u[...] += nt(gained, wu_ref[...])
    if with_sums:
        acc_sq[...] += fold_squares(wide)

    @pl.when(k == pl.num_programs(0) - 1)
    def _():
        half = out_ref.shape[1] // 2
        if with_sums:
            high, low = split_two(jnp.sum(acc_sq[...], axis=1, keepdims=True))
            lane = lax.broadcasted_iota(jnp.int32, (HALF, half - REST), 1)
            extra = jnp.where(lane == 0, high, jnp.where(lane == 1, low, 0.0))
            blank = jnp.zeros_like(extra)
            out_ref[:, :half] = jnp.concatenate([acc_g[...], extra], axis=1).astype(BF)
            out_ref[:, half:] = jnp.concatenate([acc_u[...], blank], axis=1).astype(BF)
        else:
            out_ref[:, :half] = acc_g[...].astype(BF)
            out_ref[:, half:] = acc_u[...].astype(BF)


def gate_up_half(h, x, gains, wg_t, wu_t, with_sums, held=None):
    depth = 2048 // KSTEP
    chips = CHIPS // KSTEP
    at, width, out_width = (MAIN, REST, SIDE) if with_sums else (0, MAIN, 2 * MAIN)
    weight_spec = pl.BlockSpec((pl.Element(width), pl.Element(depth)), lambda k, h: (at, k * depth))
    in_specs = [
        pl.BlockSpec((chips, HALF, LANE), lambda k, h: (k, 0, 0)),
        pl.BlockSpec((chips, 16, LANE), lambda k, h: (k, HALF // 16, 0)),
        weight_spec,
        weight_spec,
    ]
    operands = [h, x, gains, wg_t, wu_t]
    aliases = {}
    if held is not None:
        in_specs.append(pl.BlockSpec(memory_space=pl.ANY))
        operands.append(held)
        aliases = {5: 0}
    scratch = [pltpu.VMEM((HALF, width), F32), pltpu.VMEM((HALF, width), F32)]
    if with_sums:
        scratch.append(pltpu.VMEM((HALF, LANE), F32))
    return pl.pallas_call(
        functools.partial(gate_up_kernel, with_sums),
        grid_spec=pltpu.PrefetchScalarGridSpec(
            num_scalar_prefetch=1,
            grid=(KSTEP,),
            in_specs=in_specs,
            out_specs=pl.BlockSpec((HALF, out_width), lambda k, h: (h[0], 0)),
            scratch_shapes=scratch,
        ),
        out_shape=jax.ShapeDtypeStruct((TOK, out_width), BF),
        input_output_aliases=aliases,
        compiler_params=params(),
        cost_estimate=pl.CostEstimate(
            flops=2 * HALF * 2048 * 2 * width,
            bytes_accessed=4 * 2048 * width + 2 * 1024 * 1024,
            transcendentals=0,
        ),
        name="gate_up_side" if with_sums else "gate_up_main",
    )(*operands)


def hidden_kernel(main_ref, side_ref, out_ref):
    side = side_ref[0].astype(F32)
    for j in range(1, ROWS):
        side = side + side_ref[j].astype(F32)
    squares = side[:, REST : REST + 1] + side[:, REST + 1 : REST + 2]
    inv = lax.rsqrt(squares / D + EPS)

    def gated(gate, up):
        gate, up = gate * inv, up * inv
        return (gate / (1.0 + jnp.exp(-gate)) * up).astype(BF)

    first = gated(main_ref[:, :MAIN].astype(F32), main_ref[:, MAIN:].astype(F32))
    second = gated(side[:, :REST], side[:, SIDE // 2 : SIDE // 2 + REST])
    for j in range(ROWS):
        out_ref[j, :, :MAIN] = first
        out_ref[j, :, MAIN:] = second


def hidden_copies(main, side):
    return pl.pallas_call(
        hidden_kernel,
        out_shape=jax.ShapeDtypeStruct((ROWS, SEQ, FFL), BF),
        compiler_params=params(),
        name="hidden_copies",
    )(main, side)


def rope_tables():
    inv_freq = np.power(
        np.float32(ROPE_BASE), -(np.arange(64, dtype=np.float32) * np.float32(2.0 / HEAD_DIM))
    ).astype(np.float32)
    angles = np.arange(SEQ, dtype=np.float32)[:, None] * inv_freq[None, :]
    cos, sin = np.cos(angles.astype(np.float64)), np.sin(angles.astype(np.float64))
    return (
        np.concatenate([cos, cos], axis=1).astype(np.float32),
        np.concatenate([-sin, sin], axis=1).astype(np.float32),
    )


def per_device(
    tokens,
    norm_attn,
    w_query,
    w_key,
    w_value,
    w_out,
    norm_ffn,
    w_gate,
    w_up,
    w_down,
    lengths,
    segments,
):
    core = lax.axis_index("gy") % 2
    c = jnp.reshape(core, (1,)).astype(jnp.int32)

    gains = jnp.concatenate([norm_attn[None], norm_ffn[None], jnp.zeros((14, 64), BF)], axis=0)

    def with_gains(start):
        return jnp.concatenate([lax.dynamic_slice_in_dim(tokens, start, HALF, 0), gains], axis=0)

    mine = with_gains(core * HALF)
    theirs = swap(with_gains((1 - core) * HALF))
    base = jnp.where(
        core == 0,
        jnp.concatenate([mine, theirs], axis=1),
        jnp.concatenate([theirs, mine], axis=1),
    )

    first = over_chips(jnp.broadcast_to(base[None], (CHIPS,) + base.shape))
    other = swap(first)
    held = qkv_half(c, first, first, w_query, w_key.T, w_value.T)
    parts = qkv_half(1 - c, other, first, w_query, w_key.T, w_value.T, held)
    q, kv = qkv_sum(over_rows(parts))
    kv = lax.all_to_all(kv, "gy", 0, 0, axis_index_groups=KV_GROUPS, tiled=True)
    attended = over_rows(attend(lengths, q, kv, segments)).reshape(TOK, 256)
    residual, copies = residual_copies(base, project_out(c, attended, w_out))

    own = over_chips(copies)
    other = swap(own)
    weights = (w_gate.T, w_up.T)
    held = gate_up_half(c, own, first, *weights, False)
    main = gate_up_half(1 - c, other, first, *weights, False, held)
    own, other, later = lax.optimization_barrier((own, other, main))
    main = lax.psum_scatter(later, "gx", scatter_dimension=0, tiled=True)
    held = gate_up_half(c, own, first, *weights, True)
    side = gate_up_half(1 - c, other, first, *weights, True, held)
    side = over_rows(side.reshape(ROWS, SEQ, SIDE))
    hidden = over_rows(hidden_copies(main, side)).reshape(TOK, FFL)
    done = final_sum(residual, project_out(c, hidden, w_down))

    keep = lax.dynamic_slice_in_dim(done, core * 64, 64, 1)
    got = swap(lax.dynamic_slice_in_dim(done, (1 - core) * 64, 64, 1))
    return jnp.where(
        core == 0,
        jnp.concatenate([keep, got], axis=0),
        jnp.concatenate([got, keep], axis=0),
    )


def solution(mesh):
    in_specs = (
        P(None, ("gx", "gy")),
        P(("gx", "gy")),
        P("gx", "gy"),
        P("gx", "gy"),
        P("gx", "gy"),
        P("gy", "gx"),
        P(("gx", "gy")),
        P("gx", "gy"),
        P("gx", "gy"),
        P("gy", "gx"),
        P("gx"),
        P("gx"),
    )
    out_specs = P(None, ("gx", "gy"))
    return jax.shard_map(
        per_device, mesh=mesh, in_specs=in_specs, out_specs=out_specs, check_vma=False
    )
```

```python
import functools
import math

import jax
import jax.numpy as jnp
import numpy as np
from jax import lax
from jax.experimental import pallas as pl
from jax.experimental.pallas import tpu as pltpu
from jax.sharding import PartitionSpec as P

D = 16384
HEADS = 64
KV_HEADS = 4
HEAD_DIM = 128
SEQ = 96
EPS = 1e-05
ROPE_BASE = 500000.0

BF = jnp.bfloat16
F32 = jnp.float32

TOK = 768
HALF = 384
CHIPS = 16
LANE = 128
ROWS = 8
KSTEP = 4
FFL = 832
MAIN = 512
REST = FFL - MAIN
SIDE = 768
CHIP_GROUPS = [[2 * i + c for i in range(CHIPS)] for c in range(2)]
KV_GROUPS = [list(range(8 * i, 8 * i + 8)) for i in range(4)]


def swap(x):
    return lax.ppermute(x, "gy", [(i, i ^ 1) for i in range(32)])


def over_chips(x):
    return lax.all_to_all(x, "gy", 0, 0, axis_index_groups=CHIP_GROUPS, tiled=True)


def over_rows(x):
    return lax.all_to_all(x, "gx", 0, 0, tiled=True)


def params(mib=16):
    return pltpu.CompilerParams(vmem_limit_bytes=mib * 1024 * 1024)


def nt(a, b):
    return lax.dot_general(a, b, (((1,), (1,)), ((), ())), preferred_element_type=F32)


def nn(a, b):
    return jnp.dot(a, b, preferred_element_type=F32)


def fold_squares(wide):
    total = None
    for j in range(wide.shape[1] // LANE):
        part = wide[:, j * LANE : (j + 1) * LANE]
        total = part * part if total is None else total + part * part
    return total


def split_two(total):
    high = total.astype(BF).astype(F32)
    return high, total - high


def gained_block(x_ref, g_ref, row):
    chips = range(x_ref.shape[0])
    wide = jnp.concatenate([x_ref[j, :HALF] for j in chips], axis=1).astype(F32)
    gain = jnp.concatenate([g_ref[j, row : row + 1] for j in chips], axis=1).astype(F32)
    return wide, (wide * gain).astype(BF)


def qkv_kernel(h_ref, x_ref, g_ref, wq_ref, wk_ref, wv_ref, *rest):
    out_ref, acc_q, acc_kv, acc_sq = rest[-4:]
    k = pl.program_id(0)

    @pl.when(k == 0)
    def _():
        acc_q[...] = jnp.zeros_like(acc_q)
        acc_kv[...] = jnp.zeros_like(acc_kv)
        acc_sq[...] = jnp.zeros_like(acc_sq)

    wide, gained = gained_block(x_ref, g_ref, 0)
    acc_sq[...] += fold_squares(wide)
    acc_q[...] += nn(gained, wq_ref[...])
    acc_kv[...] += nt(jnp.concatenate([wk_ref[...], wv_ref[...]], axis=0), gained)

    @pl.when(k == pl.num_programs(0) - 1)
    def _():
        high, low = split_two(jnp.sum(jnp.transpose(acc_sq[...]), axis=0, keepdims=True))
        at = lax.broadcasted_iota(jnp.int32, (16, SEQ), 0)
        gap = jnp.zeros((16, LANE - SEQ), F32)
        for r in range(HALF // SEQ):
            here = slice(r * SEQ, (r + 1) * SEQ)
            out_ref[r, :SEQ] = acc_q[here].astype(BF)
            kv = acc_kv[:, here]
            sums = jnp.where(at == 0, high[:, here], jnp.where(at == 1, low[:, here], 0.0))
            top = jnp.concatenate([kv[:16], gap, kv[16:], gap], axis=1)
            bottom = jnp.concatenate([sums, gap, sums, gap], axis=1)
            out_ref[r, SEQ:] = jnp.concatenate([top, bottom], axis=0).astype(BF)


def qkv_half(h, x, gains, wq, wk_t, wv_t, held=None):
    depth = 2048 // KSTEP
    chips = CHIPS // KSTEP
    in_specs = [
        pl.BlockSpec((chips, HALF, LANE), lambda k, h: (k, 0, 0)),
        pl.BlockSpec((chips, 16, LANE), lambda k, h: (k, HALF // 16, 0)),
        pl.BlockSpec((depth, 256), lambda k, h: (k, 0)),
        pl.BlockSpec((16, depth), lambda k, h: (0, k)),
        pl.BlockSpec((16, depth), lambda k, h: (0, k)),
    ]
    operands = [h, x, gains, wq, wk_t, wv_t]
    aliases = {}
    if held is not None:
        in_specs.append(pl.BlockSpec(memory_space=pl.ANY))
        operands.append(held)
        aliases = {6: 0}
    return pl.pallas_call(
        qkv_kernel,
        grid_spec=pltpu.PrefetchScalarGridSpec(
            num_scalar_prefetch=1,
            grid=(KSTEP,),
            in_specs=in_specs,
            out_specs=pl.BlockSpec((HALF // SEQ, 128, 256), lambda k, h: (h[0], 0, 0)),
            scratch_shapes=[
                pltpu.VMEM((HALF, 256), F32),
                pltpu.VMEM((32, HALF), F32),
                pltpu.VMEM((HALF, LANE), F32),
            ],
        ),
        out_shape=jax.ShapeDtypeStruct((ROWS, 128, 256), BF),
        input_output_aliases=aliases,
        compiler_params=params(),
        cost_estimate=pl.CostEstimate(
            flops=2 * HALF * 2048 * 384, bytes_accessed=4 * 1024 * 1024, transcendentals=0
        ),
        name="qkv_half",
    )(*operands)


def qkv_sum_kernel(p_ref, q_ref, kv_ref):
    total = p_ref[0].astype(F32)
    for j in range(1, ROWS):
        total = total + p_ref[j].astype(F32)
    squares = total[112:113, :LANE] + total[113:114, :LANE]
    inv = lax.rsqrt(squares / D + EPS)
    down = jnp.transpose(jnp.broadcast_to(inv, (LANE, LANE)))[:SEQ]
    q_ref[...] = total[:SEQ] * jnp.concatenate([down, down], axis=1)
    kv = jnp.concatenate([total[96:112, :SEQ], total[96:112, LANE : LANE + SEQ]], axis=0)
    kv = kv * inv[:, :SEQ]
    for j in range(8):
        kv_ref[j] = kv


def qkv_sum(parts):
    return pl.pallas_call(
        qkv_sum_kernel,
        out_shape=(
            jax.ShapeDtypeStruct((SEQ, 256), F32),
            jax.ShapeDtypeStruct((8, 32, SEQ), F32),
        ),
        compiler_params=params(),
        name="qkv_sum",
    )(parts)


def attend_kernel(
    len_ref, q_ref, kv_ref, segr_ref, segc_ref, cos_ref, sin_ref, cost_ref, sint_ref, out_ref
):
    keys = jnp.concatenate([kv_ref[j, :16] for j in range(8)], axis=0)
    turned = jnp.concatenate([keys[64:], keys[:64]], axis=0)
    keys = (keys * cost_ref[...] + turned * sint_ref[...]).astype(BF)
    values = jnp.concatenate([kv_ref[j, 16:] for j in range(8)], axis=0).astype(BF)
    q_at = lax.broadcasted_iota(jnp.int32, (SEQ, SEQ), 0)
    k_at = lax.broadcasted_iota(jnp.int32, (SEQ, SEQ), 1)
    allowed = (segr_ref[...] == segc_ref[...]) & (k_at <= q_at) & (k_at < len_ref[0])
    allowed = allowed | (k_at == q_at)
    for head in range(2):
        query = q_ref[:, head * HEAD_DIM : (head + 1) * HEAD_DIM]
        query = (query * cos_ref[...] + pltpu.roll(query, 64, 1) * sin_ref[...]).astype(BF)
        scores = nn(query, keys) * (1.0 / math.sqrt(HEAD_DIM))
        scores = jnp.where(allowed, scores, F32(-1e30))
        expo = jnp.exp(scores - jnp.max(scores, axis=1, keepdims=True))
        soft = (expo / jnp.sum(expo, axis=1, keepdims=True)).astype(BF)
        attended = nt(soft, values).astype(BF)
        for j in range(ROWS):
            out_ref[j, :, head * HEAD_DIM : (head + 1) * HEAD_DIM] = attended


def attend(lengths, q, kv, segments):
    cos, sin = rope_tables()
    vmem = pl.BlockSpec(memory_space=pltpu.VMEM)
    return pl.pallas_call(
        attend_kernel,
        in_specs=[pl.BlockSpec(memory_space=pltpu.SMEM)] + [vmem] * 8,
        out_specs=vmem,
        out_shape=jax.ShapeDtypeStruct((ROWS, SEQ, 256), BF),
        compiler_params=params(),
        name="attend",
    )(
        lengths,
        q,
        kv,
        segments.reshape(1, SEQ),
        segments.reshape(SEQ, 1),
        cos,
        sin,
        np.ascontiguousarray(cos.T),
        np.ascontiguousarray(sin.T),
    )


def proj_kernel(h_ref, x_ref, w_ref, out_ref):
    result = nn(x_ref[...], w_ref[...]).astype(out_ref.dtype)
    for j in range(out_ref.shape[0]):
        out_ref[j] = result[:, j * LANE : (j + 1) * LANE]


def proj_half(h, x, w, dtype):
    depth = x.shape[1]
    steps = 2
    wide = 2048 // steps
    return pl.pallas_call(
        proj_kernel,
        grid_spec=pltpu.PrefetchScalarGridSpec(
            num_scalar_prefetch=1,
            grid=(steps,),
            in_specs=[
                pl.BlockSpec((HALF, depth), lambda i, h: (h[0], 0)),
                pl.BlockSpec((depth, wide), lambda i, h: (0, i)),
            ],
            out_specs=pl.BlockSpec((wide // LANE, HALF, LANE), lambda i, h: (i, 0, 0)),
        ),
        out_shape=jax.ShapeDtypeStruct((CHIPS, HALF, LANE), dtype),
        compiler_params=params(),
        cost_estimate=pl.CostEstimate(
            flops=2 * HALF * 2048 * depth, bytes_accessed=4 * 1024 * 1024, transcendentals=0
        ),
        name="proj_half",
    )(h, x, w)


def project_out(c, x, w):
    given = proj_half(1 - c, x, w, BF)
    got = swap(given)
    kept = proj_half(c, x, w, F32)
    return over_chips((kept + got.astype(F32)).astype(BF))


def residual_kernel(base_ref, p_ref, out_ref, copies_ref):
    total = p_ref[0].astype(F32)
    for j in range(1, CHIPS):
        total = total + p_ref[j].astype(F32)
    result = (base_ref[0, :HALF].astype(F32) + total).astype(BF)
    out_ref[...] = result
    for j in range(CHIPS):
        copies_ref[j] = result


def residual_copies(base, parts):
    return pl.pallas_call(
        residual_kernel,
        out_shape=(
            jax.ShapeDtypeStruct((HALF, LANE), BF),
            jax.ShapeDtypeStruct((CHIPS, HALF, LANE), BF),
        ),
        compiler_params=params(),
        name="residual_copies",
    )(base, parts)


def final_kernel(h_ref, base_ref, p_ref, keep_ref, give_ref):
    total = p_ref[0].astype(F32)
    for j in range(1, CHIPS):
        total = total + p_ref[j].astype(F32)
    done = (base_ref[...].astype(F32) + total).astype(BF)
    first, second = done[:, :64], done[:, 64:]
    keep_ref[...] = jnp.where(h_ref[0] == 0, first, second)
    give_ref[...] = jnp.where(h_ref[0] == 0, second, first)


def final_sum(h, base, parts):
    vmem = pl.BlockSpec(memory_space=pltpu.VMEM)
    return pl.pallas_call(
        final_kernel,
        in_specs=[pl.BlockSpec(memory_space=pltpu.SMEM), vmem, vmem],
        out_specs=(vmem, vmem),
        out_shape=(jax.ShapeDtypeStruct((HALF, 64), BF),) * 2,
        compiler_params=params(),
        name="final_sum",
    )(h, base, parts)


def place_kernel(h_ref, keep_ref, got_ref, out_ref):
    keep, got = keep_ref[...], got_ref[...]
    out_ref[:, :HALF] = jnp.transpose(jnp.where(h_ref[0] == 0, keep, got))
    out_ref[:, HALF:] = jnp.transpose(jnp.where(h_ref[0] == 0, got, keep))


def place_halves(h, keep, got):
    vmem = pl.BlockSpec(memory_space=pltpu.VMEM)
    return pl.pallas_call(
        place_kernel,
        in_specs=[pl.BlockSpec(memory_space=pltpu.SMEM), vmem, vmem],
        out_specs=vmem,
        out_shape=jax.ShapeDtypeStruct((64, TOK), BF),
        compiler_params=params(),
        name="place_halves",
    )(h, keep, got).T


def cut_kernel(h_ref, t_ref, ga_ref, gf_ref, keep_ref, give_ref):
    row = lax.broadcasted_iota(jnp.int32, (16, 64), 0)
    ga, gf = ga_ref[...].astype(F32), gf_ref[...].astype(F32)
    gains = jnp.where(row == 0, ga, jnp.where(row == 1, gf, 0.0)).astype(BF)
    keep_ref[HALF:] = gains
    give_ref[HALF:] = gains
    first = jnp.transpose(t_ref[:, :HALF])
    second = jnp.transpose(t_ref[:, HALF:])
    keep_ref[:HALF] = jnp.where(h_ref[0] == 0, first, second)
    give_ref[:HALF] = jnp.where(h_ref[0] == 0, second, first)


def cut_tokens(h, tokens_t, norm_attn, norm_ffn):
    vmem = pl.BlockSpec(memory_space=pltpu.VMEM)
    return pl.pallas_call(
        cut_kernel,
        in_specs=[pl.BlockSpec(memory_space=pltpu.SMEM), vmem, vmem, vmem],
        out_specs=(vmem, vmem),
        out_shape=(jax.ShapeDtypeStruct((HALF + 16, 64), BF),) * 2,
        compiler_params=params(),
        name="cut_tokens",
    )(h, tokens_t, norm_attn.reshape(1, 64), norm_ffn.reshape(1, 64))


def join_kernel(h_ref, keep_ref, got_ref, copies_ref):
    keep, got = keep_ref[...], got_ref[...]
    mine_first = jnp.concatenate([keep, got], axis=1)
    mine_last = jnp.concatenate([got, keep], axis=1)
    base = jnp.where(h_ref[0] == 0, mine_first, mine_last)
    for j in range(CHIPS):
        copies_ref[j] = base


def join_copies(h, keep, got):
    vmem = pl.BlockSpec(memory_space=pltpu.VMEM)
    return pl.pallas_call(
        join_kernel,
        in_specs=[pl.BlockSpec(memory_space=pltpu.SMEM), vmem, vmem],
        out_specs=vmem,
        out_shape=jax.ShapeDtypeStruct((CHIPS, HALF + 16, LANE), BF),
        compiler_params=params(),
        name="join_copies",
    )(h, keep, got)


def gained_rows(x_ref, g_ref, xs):
    for j in range(CHIPS):
        gain = g_ref[j, 1:2].astype(F32)
        xs[:, j * LANE : (j + 1) * LANE] = (x_ref[j].astype(F32) * gain).astype(BF)


def gate_up_main_kernel(h_ref, x_ref, g_ref, wg_ref, wu_ref, *rest):
    out_ref, xs = rest[-2:]
    step = pl.program_id(0)

    @pl.when(step == 0)
    def _():
        gained_rows(x_ref, g_ref, xs)

    wide = wg_ref.shape[0]
    at = pl.multiple_of(step * wide, wide)
    out_ref[:, pl.ds(at, wide)] = nt(xs[...], wg_ref[...]).astype(BF)
    out_ref[:, pl.ds(MAIN + at, wide)] = nt(xs[...], wu_ref[...]).astype(BF)


def gate_up_main(h, x, gains, wg_t, wu_t, held=None):
    steps = 2
    wide = MAIN // steps
    in_specs = [
        pl.BlockSpec((CHIPS, HALF, LANE), lambda i, h: (0, 0, 0)),
        pl.BlockSpec((CHIPS, 16, LANE), lambda i, h: (0, HALF // 16, 0)),
        pl.BlockSpec((wide, 2048), lambda i, h: (i, 0)),
        pl.BlockSpec((wide, 2048), lambda i, h: (i, 0)),
    ]
    operands = [h, x, gains, wg_t, wu_t]
    aliases = {}
    if held is not None:
        in_specs.append(pl.BlockSpec(memory_space=pl.ANY))
        operands.append(held)
        aliases = {5: 0}
    return pl.pallas_call(
        gate_up_main_kernel,
        grid_spec=pltpu.PrefetchScalarGridSpec(
            num_scalar_prefetch=1,
            grid=(steps,),
            in_specs=in_specs,
            out_specs=pl.BlockSpec((HALF, 2 * MAIN), lambda i, h: (h[0], 0)),
            scratch_shapes=[pltpu.VMEM((HALF, 2048), BF)],
        ),
        out_shape=jax.ShapeDtypeStruct((TOK, 2 * MAIN), BF),
        input_output_aliases=aliases,
        compiler_params=params(24),
        cost_estimate=pl.CostEstimate(
            flops=4 * HALF * 2048 * MAIN,
            bytes_accessed=8 * 1024 * 1024,
            transcendentals=0,
        ),
        name="gate_up_main",
    )(*operands)


def gate_up_side_kernel(h_ref, own_ref, other_ref, g_ref, wg_ref, wu_ref, out_ref, xs):
    lane = lax.broadcasted_iota(jnp.int32, (HALF, SIDE // 2 - REST), 1)
    for x_ref, half in ((own_ref, h_ref[0]), (other_ref, 1 - h_ref[0])):
        gained_rows(x_ref, g_ref, xs)
        squares = None
        for j in range(CHIPS):
            wide = x_ref[j].astype(F32)
            squares = wide * wide if squares is None else squares + wide * wide
        high, low = split_two(jnp.sum(squares, axis=1, keepdims=True))
        extra = jnp.where(lane == 0, high, jnp.where(lane == 1, low, 0.0))
        rows = pl.ds(pl.multiple_of(half * HALF, HALF), HALF)
        gate = jnp.concatenate([nt(xs[...], wg_ref[...]), extra], axis=1)
        out_ref[rows, : SIDE // 2] = gate.astype(BF)
        up = jnp.concatenate([nt(xs[...], wu_ref[...]), jnp.zeros_like(extra)], axis=1)
        out_ref[rows, SIDE // 2 :] = up.astype(BF)


def gate_up_side(h, own, other, gains, wg_t, wu_t):
    x_spec = pl.BlockSpec((CHIPS, HALF, LANE), lambda i, h: (0, 0, 0))
    w_spec = pl.BlockSpec((pl.Element(REST), pl.Element(2048)), lambda i, h: (MAIN, 0))
    return pl.pallas_call(
        gate_up_side_kernel,
        grid_spec=pltpu.PrefetchScalarGridSpec(
            num_scalar_prefetch=1,
            grid=(1,),
            in_specs=[
                x_spec,
                x_spec,
                pl.BlockSpec((CHIPS, 16, LANE), lambda i, h: (0, HALF // 16, 0)),
                w_spec,
                w_spec,
            ],
            out_specs=pl.BlockSpec((TOK, SIDE), lambda i, h: (0, 0)),
            scratch_shapes=[pltpu.VMEM((HALF, 2048), BF)],
        ),
        out_shape=jax.ShapeDtypeStruct((TOK, SIDE), BF),
        compiler_params=params(24),
        cost_estimate=pl.CostEstimate(
            flops=4 * TOK * 2048 * REST, bytes_accessed=6 * 1024 * 1024, transcendentals=0
        ),
        name="gate_up_side",
    )(h, own, other, gains, wg_t, wu_t)


def hidden_kernel(main_ref, side_ref, out_ref):
    side = side_ref[0].astype(F32)
    for j in range(1, ROWS):
        side = side + side_ref[j].astype(F32)
    squares = side[:, REST : REST + 1] + side[:, REST + 1 : REST + 2]
    inv = lax.rsqrt(squares / D + EPS)

    def gated(gate, up):
        gate, up = gate * inv, up * inv
        return (gate / (1.0 + jnp.exp(-gate)) * up).astype(BF)

    first = gated(main_ref[:, :MAIN].astype(F32), main_ref[:, MAIN:].astype(F32))
    second = gated(side[:, :REST], side[:, SIDE // 2 : SIDE // 2 + REST])
    for j in range(ROWS):
        out_ref[j, :, :MAIN] = first
        out_ref[j, :, MAIN:] = second


def hidden_copies(main, side):
    return pl.pallas_call(
        hidden_kernel,
        out_shape=jax.ShapeDtypeStruct((ROWS, SEQ, FFL), BF),
        compiler_params=params(),
        name="hidden_copies",
    )(main, side)


def rope_tables():
    inv_freq = np.power(
        np.float32(ROPE_BASE), -(np.arange(64, dtype=np.float32) * np.float32(2.0 / HEAD_DIM))
    ).astype(np.float32)
    angles = np.arange(SEQ, dtype=np.float32)[:, None] * inv_freq[None, :]
    cos, sin = np.cos(angles.astype(np.float64)), np.sin(angles.astype(np.float64))
    return (
        np.concatenate([cos, cos], axis=1).astype(np.float32),
        np.concatenate([-sin, sin], axis=1).astype(np.float32),
    )


def per_device(
    tokens,
    norm_attn,
    w_query,
    w_key,
    w_value,
    w_out,
    norm_ffn,
    w_gate,
    w_up,
    w_down,
    lengths,
    segments,
):
    core = lax.axis_index("gy") % 2
    c = jnp.reshape(core, (1,)).astype(jnp.int32)

    keep, give = cut_tokens(c, tokens.T, norm_attn, norm_ffn)
    base = join_copies(c, keep, swap(give))
    first = over_chips(base)
    other = swap(first)
    held = qkv_half(c, first, first, w_query, w_key.T, w_value.T)
    parts = qkv_half(1 - c, other, first, w_query, w_key.T, w_value.T, held)
    q, kv = qkv_sum(over_rows(parts))
    kv = lax.all_to_all(kv, "gy", 0, 0, axis_index_groups=KV_GROUPS, tiled=True)
    attended = over_rows(attend(lengths, q, kv, segments)).reshape(TOK, 256)
    residual, copies = residual_copies(base, project_out(c, attended, w_out))

    own = over_chips(copies)
    other = swap(own)
    weights = (w_gate.T, w_up.T)
    held = gate_up_main(c, own, first, *weights)
    main = gate_up_main(1 - c, other, first, *weights, held)
    own, other, later = lax.optimization_barrier((own, other, main))
    main = lax.psum_scatter(later, "gx", scatter_dimension=0, tiled=True)
    side = gate_up_side(c, own, other, first, *weights)
    side = over_rows(side.reshape(ROWS, SEQ, SIDE))
    hidden = over_rows(hidden_copies(main, side)).reshape(TOK, FFL)
    keep, give = final_sum(c, residual, project_out(c, hidden, w_down))
    return place_halves(c, keep, swap(give))


def solution(mesh):
    in_specs = (
        P(None, ("gx", "gy")),
        P(("gx", "gy")),
        P("gx", "gy"),
        P("gx", "gy"),
        P("gx", "gy"),
        P("gy", "gx"),
        P(("gx", "gy")),
        P("gx", "gy"),
        P("gx", "gy"),
        P("gy", "gx"),
        P("gx"),
        P("gx"),
    )
    out_specs = P(None, ("gx", "gy"))
    return jax.shard_map(
        per_device, mesh=mesh, in_specs=in_specs, out_specs=out_specs, check_vma=False
    )
```

```python
import functools
import math

import jax
import jax.numpy as jnp
import numpy as np
from jax import lax
from jax.experimental import pallas as pl
from jax.experimental.pallas import tpu as pltpu
from jax.sharding import PartitionSpec as P

D = 16384
HEADS = 64
KV_HEADS = 4
HEAD_DIM = 128
SEQ = 96
EPS = 1e-05
ROPE_BASE = 500000.0

BF = jnp.bfloat16
F32 = jnp.float32

TOK = 768
HALF = 384
CHIPS = 16
LANE = 128
ROWS = 8
KSTEP = 4
FFL = 832
MAIN = 640
REST = FFL - MAIN
SIDE = 512
CHIP_GROUPS = [[2 * i + c for i in range(CHIPS)] for c in range(2)]
KV_GROUPS = [list(range(8 * i, 8 * i + 8)) for i in range(4)]


def swap(x):
    return lax.ppermute(x, "gy", [(i, i ^ 1) for i in range(32)])


def over_chips(x):
    return lax.all_to_all(x, "gy", 0, 0, axis_index_groups=CHIP_GROUPS, tiled=True)


def over_rows(x):
    return lax.all_to_all(x, "gx", 0, 0, tiled=True)


def params(mib=16):
    return pltpu.CompilerParams(vmem_limit_bytes=mib * 1024 * 1024)


def nt(a, b):
    return lax.dot_general(a, b, (((1,), (1,)), ((), ())), preferred_element_type=F32)


def nn(a, b):
    return jnp.dot(a, b, preferred_element_type=F32)


def fold_squares(wide):
    total = None
    for j in range(wide.shape[1] // LANE):
        part = wide[:, j * LANE : (j + 1) * LANE]
        total = part * part if total is None else total + part * part
    return total


def split_two(total):
    high = total.astype(BF).astype(F32)
    return high, total - high


def gained_block(x_ref, g_ref, row):
    chips = range(x_ref.shape[0])
    wide = jnp.concatenate([x_ref[j, :HALF] for j in chips], axis=1).astype(F32)
    gain = jnp.concatenate([g_ref[j, row : row + 1] for j in chips], axis=1).astype(F32)
    return wide, (wide * gain).astype(BF)


def qkv_kernel(h_ref, x_ref, g_ref, wq_ref, wk_ref, wv_ref, *rest):
    out_ref, acc_q, acc_kv, acc_sq = rest[-4:]
    k = pl.program_id(0)

    @pl.when(k == 0)
    def _():
        acc_q[...] = jnp.zeros_like(acc_q)
        acc_kv[...] = jnp.zeros_like(acc_kv)
        acc_sq[...] = jnp.zeros_like(acc_sq)

    wide, gained = gained_block(x_ref, g_ref, 0)
    acc_sq[...] += fold_squares(wide)
    acc_q[...] += nn(gained, wq_ref[...])
    acc_kv[...] += nt(jnp.concatenate([wk_ref[...], wv_ref[...]], axis=0), gained)

    @pl.when(k == pl.num_programs(0) - 1)
    def _():
        high, low = split_two(jnp.sum(jnp.transpose(acc_sq[...]), axis=0, keepdims=True))
        at = lax.broadcasted_iota(jnp.int32, (16, SEQ), 0)
        gap = jnp.zeros((16, LANE - SEQ), F32)
        for r in range(HALF // SEQ):
            here = slice(r * SEQ, (r + 1) * SEQ)
            out_ref[r, :SEQ] = acc_q[here].astype(BF)
            kv = acc_kv[:, here]
            sums = jnp.where(at == 0, high[:, here], jnp.where(at == 1, low[:, here], 0.0))
            top = jnp.concatenate([kv[:16], gap, kv[16:], gap], axis=1)
            bottom = jnp.concatenate([sums, gap, sums, gap], axis=1)
            out_ref[r, SEQ:] = jnp.concatenate([top, bottom], axis=0).astype(BF)


def qkv_half(h, x, gains, wq, wk_t, wv_t, held=None):
    depth = 2048 // KSTEP
    chips = CHIPS // KSTEP
    in_specs = [
        pl.BlockSpec((chips, HALF, LANE), lambda k, h: (k, 0, 0)),
        pl.BlockSpec((chips, 16, LANE), lambda k, h: (k, HALF // 16, 0)),
        pl.BlockSpec((depth, 256), lambda k, h: (k, 0)),
        pl.BlockSpec((16, depth), lambda k, h: (0, k)),
        pl.BlockSpec((16, depth), lambda k, h: (0, k)),
    ]
    operands = [h, x, gains, wq, wk_t, wv_t]
    aliases = {}
    if held is not None:
        in_specs.append(pl.BlockSpec(memory_space=pl.ANY))
        operands.append(held)
        aliases = {6: 0}
    return pl.pallas_call(
        qkv_kernel,
        grid_spec=pltpu.PrefetchScalarGridSpec(
            num_scalar_prefetch=1,
            grid=(KSTEP,),
            in_specs=in_specs,
            out_specs=pl.BlockSpec((HALF // SEQ, 128, 256), lambda k, h: (h[0], 0, 0)),
            scratch_shapes=[
                pltpu.VMEM((HALF, 256), F32),
                pltpu.VMEM((32, HALF), F32),
                pltpu.VMEM((HALF, LANE), F32),
            ],
        ),
        out_shape=jax.ShapeDtypeStruct((ROWS, 128, 256), BF),
        input_output_aliases=aliases,
        compiler_params=params(),
        cost_estimate=pl.CostEstimate(
            flops=2 * HALF * 2048 * 384, bytes_accessed=4 * 1024 * 1024, transcendentals=0
        ),
        name="qkv_half",
    )(*operands)


def qkv_sum_kernel(p_ref, q_ref, kv_ref):
    total = p_ref[0].astype(F32)
    for j in range(1, ROWS):
        total = total + p_ref[j].astype(F32)
    squares = total[112:113, :LANE] + total[113:114, :LANE]
    inv = lax.rsqrt(squares / D + EPS)
    down = jnp.transpose(jnp.broadcast_to(inv, (LANE, LANE)))[:SEQ]
    q_ref[...] = total[:SEQ] * jnp.concatenate([down, down], axis=1)
    kv = jnp.concatenate([total[96:112, :SEQ], total[96:112, LANE : LANE + SEQ]], axis=0)
    kv = kv * inv[:, :SEQ]
    for j in range(8):
        kv_ref[j] = kv


def qkv_sum(parts):
    return pl.pallas_call(
        qkv_sum_kernel,
        out_shape=(
            jax.ShapeDtypeStruct((SEQ, 256), F32),
            jax.ShapeDtypeStruct((8, 32, SEQ), F32),
        ),
        compiler_params=params(),
        name="qkv_sum",
    )(parts)


def attend_kernel(len_ref, q_ref, kv_ref, seg_ref, table_ref, out_ref):
    cos, sin = table_ref[0], table_ref[1]
    cos_t, sin_t = jnp.transpose(cos)[:, :SEQ], jnp.transpose(sin)[:, :SEQ]
    cos, sin = cos[:SEQ], sin[:SEQ]
    keys = jnp.concatenate([kv_ref[j, :16] for j in range(8)], axis=0)
    turned = jnp.concatenate([keys[64:], keys[:64]], axis=0)
    keys = (keys * cos_t + turned * sin_t).astype(BF)
    values = jnp.concatenate([kv_ref[j, 16:] for j in range(8)], axis=0).astype(BF)
    seg = jnp.concatenate([seg_ref[...].astype(F32), jnp.zeros((1, LANE - SEQ), F32)], axis=1)
    seg = jnp.broadcast_to(seg, (LANE, LANE))
    same = (seg == jnp.transpose(seg))[:SEQ, :SEQ]
    q_at = lax.broadcasted_iota(jnp.int32, (SEQ, SEQ), 0)
    k_at = lax.broadcasted_iota(jnp.int32, (SEQ, SEQ), 1)
    allowed = same & (k_at <= q_at) & (k_at < len_ref[0])
    allowed = allowed | (k_at == q_at)
    for head in range(2):
        query = q_ref[:, head * HEAD_DIM : (head + 1) * HEAD_DIM]
        query = (query * cos + pltpu.roll(query, 64, 1) * sin).astype(BF)
        scores = nn(query, keys) * (1.0 / math.sqrt(HEAD_DIM))
        scores = jnp.where(allowed, scores, F32(-1e30))
        expo = jnp.exp(scores - jnp.max(scores, axis=1, keepdims=True))
        soft = (expo / jnp.sum(expo, axis=1, keepdims=True)).astype(BF)
        attended = nt(soft, values).astype(BF)
        for j in range(ROWS):
            out_ref[j, :, head * HEAD_DIM : (head + 1) * HEAD_DIM] = attended


def attend(lengths, q, kv, segments):
    vmem = pl.BlockSpec(memory_space=pltpu.VMEM)
    return pl.pallas_call(
        attend_kernel,
        in_specs=[pl.BlockSpec(memory_space=pltpu.SMEM)] + [vmem] * 4,
        out_specs=vmem,
        out_shape=jax.ShapeDtypeStruct((ROWS, SEQ, 256), BF),
        compiler_params=params(),
        name="attend",
    )(lengths, q, kv, segments.reshape(1, SEQ), rope_table())


def proj_kernel(h_ref, x_ref, w_ref, out_ref):
    result = nn(x_ref[...], w_ref[...]).astype(out_ref.dtype)
    for j in range(out_ref.shape[0]):
        out_ref[j] = result[:, j * LANE : (j + 1) * LANE]


def proj_half(h, x, w, dtype):
    depth = x.shape[1]
    steps = 2
    wide = 2048 // steps
    return pl.pallas_call(
        proj_kernel,
        grid_spec=pltpu.PrefetchScalarGridSpec(
            num_scalar_prefetch=1,
            grid=(steps,),
            in_specs=[
                pl.BlockSpec((HALF, depth), lambda i, h: (h[0], 0)),
                pl.BlockSpec((depth, wide), lambda i, h: (0, i)),
            ],
            out_specs=pl.BlockSpec((wide // LANE, HALF, LANE), lambda i, h: (i, 0, 0)),
        ),
        out_shape=jax.ShapeDtypeStruct((CHIPS, HALF, LANE), dtype),
        compiler_params=params(),
        cost_estimate=pl.CostEstimate(
            flops=2 * HALF * 2048 * depth, bytes_accessed=4 * 1024 * 1024, transcendentals=0
        ),
        name="proj_half",
    )(h, x, w)


def project_out(c, x, w):
    given = proj_half(1 - c, x, w, BF)
    got = swap(given)
    kept = proj_half(c, x, w, F32)
    return over_chips((kept + got.astype(F32)).astype(BF))


def residual_kernel(base_ref, p_ref, out_ref, copies_ref):
    total = p_ref[0].astype(F32)
    for j in range(1, CHIPS):
        total = total + p_ref[j].astype(F32)
    result = (base_ref[0, :HALF].astype(F32) + total).astype(BF)
    out_ref[...] = result
    for j in range(CHIPS):
        copies_ref[j] = result


def residual_copies(base, parts):
    return pl.pallas_call(
        residual_kernel,
        out_shape=(
            jax.ShapeDtypeStruct((HALF, LANE), BF),
            jax.ShapeDtypeStruct((CHIPS, HALF, LANE), BF),
        ),
        compiler_params=params(),
        name="residual_copies",
    )(base, parts)


def final_kernel(h_ref, base_ref, p_ref, keep_ref, give_ref):
    total = p_ref[0].astype(F32)
    for j in range(1, CHIPS):
        total = total + p_ref[j].astype(F32)
    done = (base_ref[...].astype(F32) + total).astype(BF)
    first, second = done[:, :64], done[:, 64:]
    keep_ref[...] = jnp.where(h_ref[0] == 0, first, second)
    give_ref[...] = jnp.where(h_ref[0] == 0, second, first)


def final_sum(h, base, parts):
    vmem = pl.BlockSpec(memory_space=pltpu.VMEM)
    return pl.pallas_call(
        final_kernel,
        in_specs=[pl.BlockSpec(memory_space=pltpu.SMEM), vmem, vmem],
        out_specs=(vmem, vmem),
        out_shape=(jax.ShapeDtypeStruct((HALF, 64), BF),) * 2,
        compiler_params=params(),
        name="final_sum",
    )(h, base, parts)


def place_kernel(h_ref, keep_ref, got_ref, out_ref):
    keep, got = keep_ref[...], got_ref[...]
    out_ref[:, :HALF] = jnp.transpose(jnp.where(h_ref[0] == 0, keep, got))
    out_ref[:, HALF:] = jnp.transpose(jnp.where(h_ref[0] == 0, got, keep))


def place_halves(h, keep, got):
    vmem = pl.BlockSpec(memory_space=pltpu.VMEM)
    return pl.pallas_call(
        place_kernel,
        in_specs=[pl.BlockSpec(memory_space=pltpu.SMEM), vmem, vmem],
        out_specs=vmem,
        out_shape=jax.ShapeDtypeStruct((64, TOK), BF),
        compiler_params=params(),
        name="place_halves",
    )(h, keep, got).T


def cut_kernel(h_ref, t_ref, ga_ref, gf_ref, keep_ref, give_ref):
    row = lax.broadcasted_iota(jnp.int32, (16, 64), 0)
    ga, gf = ga_ref[...].astype(F32), gf_ref[...].astype(F32)
    gains = jnp.where(row == 0, ga, jnp.where(row == 1, gf, 0.0)).astype(BF)
    keep_ref[HALF:] = gains
    give_ref[HALF:] = gains
    first = jnp.transpose(t_ref[:, :HALF])
    second = jnp.transpose(t_ref[:, HALF:])
    keep_ref[:HALF] = jnp.where(h_ref[0] == 0, first, second)
    give_ref[:HALF] = jnp.where(h_ref[0] == 0, second, first)


def cut_tokens(h, tokens_t, norm_attn, norm_ffn):
    whole = lambda *shape: pl.BlockSpec(shape, lambda i: (0, 0))
    return pl.pallas_call(
        cut_kernel,
        grid=(1,),
        in_specs=[
            pl.BlockSpec(memory_space=pltpu.SMEM),
            whole(64, TOK),
            whole(1, 64),
            whole(1, 64),
        ],
        out_specs=(whole(HALF + 16, 64), whole(HALF + 16, 64)),
        out_shape=(jax.ShapeDtypeStruct((HALF + 16, 64), BF),) * 2,
        compiler_params=params(),
        name="cut_tokens",
    )(h, tokens_t, norm_attn.reshape(1, 64), norm_ffn.reshape(1, 64))


def join_kernel(h_ref, keep_ref, got_ref, copies_ref):
    keep, got = keep_ref[...], got_ref[...]
    mine_first = jnp.concatenate([keep, got], axis=1)
    mine_last = jnp.concatenate([got, keep], axis=1)
    base = jnp.where(h_ref[0] == 0, mine_first, mine_last)
    for j in range(CHIPS):
        copies_ref[j] = base


def join_copies(h, keep, got):
    vmem = pl.BlockSpec(memory_space=pltpu.VMEM)
    return pl.pallas_call(
        join_kernel,
        in_specs=[pl.BlockSpec(memory_space=pltpu.SMEM), vmem, vmem],
        out_specs=vmem,
        out_shape=jax.ShapeDtypeStruct((CHIPS, HALF + 16, LANE), BF),
        compiler_params=params(),
        name="join_copies",
    )(h, keep, got)


def gained_rows(x_ref, g_ref, xs):
    for j in range(CHIPS):
        gain = g_ref[j, 1:2].astype(F32)
        xs[:, j * LANE : (j + 1) * LANE] = (x_ref[j].astype(F32) * gain).astype(BF)


def gate_up_main_kernel(h_ref, x_ref, g_ref, wg_ref, wu_ref, *rest):
    out_ref, xs = rest[-2:]
    step = pl.program_id(0)

    @pl.when(step == 0)
    def _():
        gained_rows(x_ref, g_ref, xs)

    wide = wg_ref.shape[0]
    at = pl.multiple_of(step * wide, wide)
    out_ref[:, pl.ds(at, wide)] = nt(xs[...], wg_ref[...]).astype(BF)
    out_ref[:, pl.ds(MAIN + at, wide)] = nt(xs[...], wu_ref[...]).astype(BF)


def gate_up_main(h, x, gains, wg_t, wu_t, held=None):
    steps = 1
    wide = MAIN // steps
    in_specs = [
        pl.BlockSpec((CHIPS, HALF, LANE), lambda i, h: (0, 0, 0)),
        pl.BlockSpec((CHIPS, 16, LANE), lambda i, h: (0, HALF // 16, 0)),
        pl.BlockSpec((wide, 2048), lambda i, h: (i, 0)),
        pl.BlockSpec((wide, 2048), lambda i, h: (i, 0)),
    ]
    operands = [h, x, gains, wg_t, wu_t]
    aliases = {}
    if held is not None:
        in_specs.append(pl.BlockSpec(memory_space=pl.ANY))
        operands.append(held)
        aliases = {5: 0}
    return pl.pallas_call(
        gate_up_main_kernel,
        grid_spec=pltpu.PrefetchScalarGridSpec(
            num_scalar_prefetch=1,
            grid=(steps,),
            in_specs=in_specs,
            out_specs=pl.BlockSpec((HALF, 2 * MAIN), lambda i, h: (h[0], 0)),
            scratch_shapes=[pltpu.VMEM((HALF, 2048), BF)],
        ),
        out_shape=jax.ShapeDtypeStruct((TOK, 2 * MAIN), BF),
        input_output_aliases=aliases,
        compiler_params=params(24),
        cost_estimate=pl.CostEstimate(
            flops=4 * HALF * 2048 * MAIN,
            bytes_accessed=8 * 1024 * 1024,
            transcendentals=0,
        ),
        name="gate_up_main",
    )(*operands)


def gate_up_side_kernel(h_ref, own_ref, other_ref, g_ref, wg_ref, wu_ref, _, out_ref, xs):
    lane = lax.broadcasted_iota(jnp.int32, (HALF, SIDE // 2 - REST), 1)
    for x_ref, half in ((own_ref, h_ref[0]), (other_ref, 1 - h_ref[0])):
        gained_rows(x_ref, g_ref, xs)
        squares = None
        for j in range(CHIPS):
            wide = x_ref[j].astype(F32)
            squares = wide * wide if squares is None else squares + wide * wide
        high, low = split_two(jnp.sum(squares, axis=1, keepdims=True))
        extra = jnp.where(lane == 0, high, jnp.where(lane == 1, low, 0.0))
        rows = pl.ds(pl.multiple_of(half * HALF, HALF), HALF)
        gate = jnp.concatenate([nt(xs[...], wg_ref[...]), extra], axis=1)
        out_ref[rows, : SIDE // 2] = gate.astype(BF)
        up = jnp.concatenate([nt(xs[...], wu_ref[...]), jnp.zeros_like(extra)], axis=1)
        out_ref[rows, SIDE // 2 :] = up.astype(BF)


def gate_up_side(h, own, other, gains, wg_t, wu_t, main):
    x_spec = pl.BlockSpec((CHIPS, HALF, LANE), lambda i, h: (0, 0, 0))
    w_spec = pl.BlockSpec((pl.Element(REST), pl.Element(2048)), lambda i, h: (MAIN, 0))
    return pl.pallas_call(
        gate_up_side_kernel,
        grid_spec=pltpu.PrefetchScalarGridSpec(
            num_scalar_prefetch=1,
            grid=(1,),
            in_specs=[
                x_spec,
                x_spec,
                pl.BlockSpec((CHIPS, 16, LANE), lambda i, h: (0, HALF // 16, 0)),
                w_spec,
                w_spec,
                pl.BlockSpec(memory_space=pl.ANY),
            ],
            out_specs=pl.BlockSpec((TOK, SIDE), lambda i, h: (0, 0)),
            scratch_shapes=[pltpu.VMEM((HALF, 2048), BF)],
        ),
        out_shape=jax.ShapeDtypeStruct((TOK, SIDE), BF),
        compiler_params=params(24),
        cost_estimate=pl.CostEstimate(
            flops=4 * TOK * 2048 * REST, bytes_accessed=6 * 1024 * 1024, transcendentals=0
        ),
        name="gate_up_side",
    )(h, own, other, gains, wg_t, wu_t, main)


def hidden_kernel(main_ref, side_ref, out_ref):
    side = side_ref[0].astype(F32)
    for j in range(1, ROWS):
        side = side + side_ref[j].astype(F32)
    squares = side[:, REST : REST + 1] + side[:, REST + 1 : REST + 2]
    inv = lax.rsqrt(squares / D + EPS)

    def gated(gate, up):
        gate, up = gate * inv, up * inv
        return (gate / (1.0 + jnp.exp(-gate)) * up).astype(BF)

    first = gated(main_ref[:, :MAIN].astype(F32), main_ref[:, MAIN:].astype(F32))
    second = gated(side[:, :REST], side[:, SIDE // 2 : SIDE // 2 + REST])
    out_ref[:, :MAIN] = first
    out_ref[:, MAIN:] = second


def hidden_row(main, side):
    return pl.pallas_call(
        hidden_kernel,
        out_shape=jax.ShapeDtypeStruct((SEQ, FFL), BF),
        compiler_params=params(),
        name="hidden_row",
    )(main, side)


def from_ahead(x, k):
    return lax.ppermute(x, "gx", [(i, (i - k) % ROWS) for i in range(ROWS)])


def order_kernel(at_ref, *refs):
    out_ref = refs[-1]
    for k, ref in enumerate(refs[:-1]):
        out_ref[lax.rem(at_ref[0] + k, ROWS)] = ref[...]


def all_rows(x):
    ahead = {0: x}
    for k in (1, 7, 3, 5):
        ahead[k] = from_ahead(x, k)
    ahead[2] = from_ahead(ahead[1], 1)
    ahead[6] = from_ahead(ahead[7], 7)
    ahead[4] = from_ahead(ahead[3], 1)
    vmem = pl.BlockSpec(memory_space=pltpu.VMEM)
    at = jnp.reshape(lax.axis_index("gx"), (1,)).astype(jnp.int32)
    return pl.pallas_call(
        order_kernel,
        in_specs=[pl.BlockSpec(memory_space=pltpu.SMEM)] + [vmem] * ROWS,
        out_specs=vmem,
        out_shape=jax.ShapeDtypeStruct((ROWS,) + x.shape, x.dtype),
        compiler_params=params(),
        name="order_rows",
    )(at, *[ahead[k] for k in range(ROWS)])


def rope_table():
    inv_freq = np.power(
        np.float32(ROPE_BASE), -(np.arange(64, dtype=np.float32) * np.float32(2.0 / HEAD_DIM))
    ).astype(np.float32)
    angles = (np.arange(SEQ, dtype=np.float32)[:, None] * inv_freq[None, :]).astype(np.float64)
    cos, sin = np.cos(angles), np.sin(angles)
    table = np.zeros((2, LANE, LANE), np.float32)
    table[0, :SEQ] = np.concatenate([cos, cos], axis=1)
    table[1, :SEQ] = np.concatenate([-sin, sin], axis=1)
    return table


def per_device(
    tokens,
    norm_attn,
    w_query,
    w_key,
    w_value,
    w_out,
    norm_ffn,
    w_gate,
    w_up,
    w_down,
    lengths,
    segments,
):
    core = lax.axis_index("gy") % 2
    c = jnp.reshape(core, (1,)).astype(jnp.int32)

    keep, give = cut_tokens(c, tokens.T, norm_attn, norm_ffn)
    base = join_copies(c, keep, swap(give))
    first = over_chips(base)
    other = swap(first)
    held = qkv_half(c, first, first, w_query, w_key.T, w_value.T)
    parts = qkv_half(1 - c, other, first, w_query, w_key.T, w_value.T, held)
    q, kv = qkv_sum(over_rows(parts))
    kv = lax.all_to_all(kv, "gy", 0, 0, axis_index_groups=KV_GROUPS, tiled=True)
    attended = over_rows(attend(lengths, q, kv, segments)).reshape(TOK, 256)
    residual, copies = residual_copies(base, project_out(c, attended, w_out))

    own = over_chips(copies)
    other = swap(own)
    weights = (w_gate.T, w_up.T)
    held = gate_up_main(c, own, first, *weights)
    main = gate_up_main(1 - c, other, first, *weights, held)
    side = gate_up_side(c, own, other, first, *weights, main)
    main = lax.psum_scatter(main, "gx", scatter_dimension=0, tiled=True)
    side = over_rows(side.reshape(ROWS, SEQ, SIDE))
    hidden = all_rows(hidden_row(main, side)).reshape(TOK, FFL)
    keep, give = final_sum(c, residual, project_out(c, hidden, w_down))
    return place_halves(c, keep, swap(give))


def solution(mesh):
    in_specs = (
        P(None, ("gx", "gy")),
        P(("gx", "gy")),
        P("gx", "gy"),
        P("gx", "gy"),
        P("gx", "gy"),
        P("gy", "gx"),
        P(("gx", "gy")),
        P("gx", "gy"),
        P("gx", "gy"),
        P("gy", "gx"),
        P("gx"),
        P("gx"),
    )
    out_specs = P(None, ("gx", "gy"))
    return jax.shard_map(
        per_device, mesh=mesh, in_specs=in_specs, out_specs=out_specs, check_vma=False
    )
```

```python
import functools
import math

import jax
import jax.numpy as jnp
import numpy as np
from jax import lax
from jax.experimental import pallas as pl
from jax.experimental.pallas import tpu as pltpu
from jax.sharding import PartitionSpec as P

D = 16384
HEADS = 64
KV_HEADS = 4
HEAD_DIM = 128
SEQ = 96
EPS = 1e-05
ROPE_BASE = 500000.0

BF = jnp.bfloat16
F32 = jnp.float32

TOK = 768
HALF = 384
CHIPS = 16
LANE = 128
ROWS = 8
KSTEP = 4
FFL = 832
MAIN = 640
REST = FFL - MAIN
SIDE = 512
CHIP_GROUPS = [[2 * i + c for i in range(CHIPS)] for c in range(2)]
KV_GROUPS = [list(range(8 * i, 8 * i + 8)) for i in range(4)]


def swap(x):
    return lax.ppermute(x, "gy", [(i, i ^ 1) for i in range(32)])


def over_chips(x):
    return lax.all_to_all(x, "gy", 0, 0, axis_index_groups=CHIP_GROUPS, tiled=True)


def over_rows(x):
    return lax.all_to_all(x, "gx", 0, 0, tiled=True)


def params(mib=16):
    return pltpu.CompilerParams(vmem_limit_bytes=mib * 1024 * 1024)


def nt(a, b):
    return lax.dot_general(a, b, (((1,), (1,)), ((), ())), preferred_element_type=F32)


def nn(a, b):
    return jnp.dot(a, b, preferred_element_type=F32)


def fold_squares(wide):
    total = None
    for j in range(wide.shape[1] // LANE):
        part = wide[:, j * LANE : (j + 1) * LANE]
        total = part * part if total is None else total + part * part
    return total


def split_two(total):
    high = total.astype(BF).astype(F32)
    return high, total - high


def gained_block(x_ref, g_ref, row):
    chips = range(x_ref.shape[0])
    wide = jnp.concatenate([x_ref[j, :HALF] for j in chips], axis=1).astype(F32)
    gain = jnp.concatenate([g_ref[j, row : row + 1] for j in chips], axis=1).astype(F32)
    return wide, (wide * gain).astype(BF)


def qkv_kernel(h_ref, x_ref, g_ref, wq_ref, wk_ref, wv_ref, *rest):
    out_ref, acc_q, acc_kv, acc_sq = rest[-4:]
    k = pl.program_id(0)

    @pl.when(k == 0)
    def _():
        acc_q[...] = jnp.zeros_like(acc_q)
        acc_kv[...] = jnp.zeros_like(acc_kv)
        acc_sq[...] = jnp.zeros_like(acc_sq)

    wide, gained = gained_block(x_ref, g_ref, 0)
    acc_sq[...] += fold_squares(wide)
    acc_q[...] += nn(gained, wq_ref[...])
    acc_kv[...] += nt(jnp.concatenate([wk_ref[...], wv_ref[...]], axis=0), gained)

    @pl.when(k == pl.num_programs(0) - 1)
    def _():
        high, low = split_two(jnp.sum(jnp.transpose(acc_sq[...]), axis=0, keepdims=True))
        at = lax.broadcasted_iota(jnp.int32, (16, SEQ), 0)
        gap = jnp.zeros((16, LANE - SEQ), F32)
        for r in range(HALF // SEQ):
            here = slice(r * SEQ, (r + 1) * SEQ)
            out_ref[r, :SEQ] = acc_q[here].astype(BF)
            kv = acc_kv[:, here]
            sums = jnp.where(at == 0, high[:, here], jnp.where(at == 1, low[:, here], 0.0))
            top = jnp.concatenate([kv[:16], gap, kv[16:], gap], axis=1)
            bottom = jnp.concatenate([sums, gap, sums, gap], axis=1)
            out_ref[r, SEQ:] = jnp.concatenate([top, bottom], axis=0).astype(BF)


def qkv_half(h, x, gains, wq, wk_t, wv_t, held=None):
    depth = 2048 // KSTEP
    chips = CHIPS // KSTEP
    in_specs = [
        pl.BlockSpec((chips, HALF, LANE), lambda k, h: (k, 0, 0)),
        pl.BlockSpec((chips, 16, LANE), lambda k, h: (k, HALF // 16, 0)),
        pl.BlockSpec((depth, 256), lambda k, h: (k, 0)),
        pl.BlockSpec((16, depth), lambda k, h: (0, k)),
        pl.BlockSpec((16, depth), lambda k, h: (0, k)),
    ]
    operands = [h, x, gains, wq, wk_t, wv_t]
    aliases = {}
    if held is not None:
        in_specs.append(pl.BlockSpec(memory_space=pl.ANY))
        operands.append(held)
        aliases = {6: 0}
    return pl.pallas_call(
        qkv_kernel,
        grid_spec=pltpu.PrefetchScalarGridSpec(
            num_scalar_prefetch=1,
            grid=(KSTEP,),
            in_specs=in_specs,
            out_specs=pl.BlockSpec((HALF // SEQ, 128, 256), lambda k, h: (h[0], 0, 0)),
            scratch_shapes=[
                pltpu.VMEM((HALF, 256), F32),
                pltpu.VMEM((32, HALF), F32),
                pltpu.VMEM((HALF, LANE), F32),
            ],
        ),
        out_shape=jax.ShapeDtypeStruct((ROWS, 128, 256), BF),
        input_output_aliases=aliases,
        compiler_params=params(),
        cost_estimate=pl.CostEstimate(
            flops=2 * HALF * 2048 * 384, bytes_accessed=4 * 1024 * 1024, transcendentals=0
        ),
        name="qkv_half",
    )(*operands)


def qkv_sum_kernel(p_ref, q_ref, kv_ref):
    total = p_ref[0].astype(F32)
    for j in range(1, ROWS):
        total = total + p_ref[j].astype(F32)
    squares = total[112:113, :LANE] + total[113:114, :LANE]
    inv = lax.rsqrt(squares / D + EPS)
    down = jnp.transpose(jnp.broadcast_to(inv, (LANE, LANE)))[:SEQ]
    q_ref[...] = total[:SEQ] * jnp.concatenate([down, down], axis=1)
    kv = jnp.concatenate([total[96:112, :SEQ], total[96:112, LANE : LANE + SEQ]], axis=0)
    kv = kv * inv[:, :SEQ]
    for j in range(8):
        kv_ref[j] = kv


def qkv_sum(parts):
    return pl.pallas_call(
        qkv_sum_kernel,
        out_shape=(
            jax.ShapeDtypeStruct((SEQ, 256), F32),
            jax.ShapeDtypeStruct((8, 32, SEQ), F32),
        ),
        compiler_params=params(),
        name="qkv_sum",
    )(parts)


def attend_kernel(len_ref, q_ref, kv_ref, seg_ref, table_ref, out_ref):
    cos, sin = table_ref[0], table_ref[1]
    cos_t, sin_t = jnp.transpose(cos)[:, :SEQ], jnp.transpose(sin)[:, :SEQ]
    cos, sin = cos[:SEQ], sin[:SEQ]
    keys = jnp.concatenate([kv_ref[j, :16] for j in range(8)], axis=0)
    turned = jnp.concatenate([keys[64:], keys[:64]], axis=0)
    keys = (keys * cos_t + turned * sin_t).astype(BF)
    values = jnp.concatenate([kv_ref[j, 16:] for j in range(8)], axis=0).astype(BF)
    seg = jnp.concatenate([seg_ref[...].astype(F32), jnp.zeros((1, LANE - SEQ), F32)], axis=1)
    seg = jnp.broadcast_to(seg, (LANE, LANE))
    same = (seg == jnp.transpose(seg))[:SEQ, :SEQ]
    q_at = lax.broadcasted_iota(jnp.int32, (SEQ, SEQ), 0)
    k_at = lax.broadcasted_iota(jnp.int32, (SEQ, SEQ), 1)
    allowed = same & (k_at <= q_at) & (k_at < len_ref[0])
    allowed = allowed | (k_at == q_at)
    for head in range(2):
        query = q_ref[:, head * HEAD_DIM : (head + 1) * HEAD_DIM]
        query = (query * cos + pltpu.roll(query, 64, 1) * sin).astype(BF)
        scores = nn(query, keys) * (1.0 / math.sqrt(HEAD_DIM))
        scores = jnp.where(allowed, scores, F32(-1e30))
        expo = jnp.exp(scores - jnp.max(scores, axis=1, keepdims=True))
        soft = (expo / jnp.sum(expo, axis=1, keepdims=True)).astype(BF)
        attended = nt(soft, values).astype(BF)
        for j in range(ROWS):
            out_ref[j, :, head * HEAD_DIM : (head + 1) * HEAD_DIM] = attended


def attend(lengths, q, kv, segments):
    vmem = pl.BlockSpec(memory_space=pltpu.VMEM)
    return pl.pallas_call(
        attend_kernel,
        in_specs=[pl.BlockSpec(memory_space=pltpu.SMEM)] + [vmem] * 4,
        out_specs=vmem,
        out_shape=jax.ShapeDtypeStruct((ROWS, SEQ, 256), BF),
        compiler_params=params(),
        name="attend",
    )(lengths, q, kv, segments.reshape(1, SEQ), rope_table())


def proj_kernel(h_ref, x_ref, w_ref, out_ref):
    result = nn(x_ref[...], w_ref[...]).astype(out_ref.dtype)
    for j in range(out_ref.shape[0]):
        out_ref[j] = result[:, j * LANE : (j + 1) * LANE]


def proj_half(h, x, w, dtype):
    depth = x.shape[1]
    steps = 2
    wide = 2048 // steps
    return pl.pallas_call(
        proj_kernel,
        grid_spec=pltpu.PrefetchScalarGridSpec(
            num_scalar_prefetch=1,
            grid=(steps,),
            in_specs=[
                pl.BlockSpec((HALF, depth), lambda i, h: (h[0], 0)),
                pl.BlockSpec((depth, wide), lambda i, h: (0, i)),
            ],
            out_specs=pl.BlockSpec((wide // LANE, HALF, LANE), lambda i, h: (i, 0, 0)),
        ),
        out_shape=jax.ShapeDtypeStruct((CHIPS, HALF, LANE), dtype),
        compiler_params=params(),
        cost_estimate=pl.CostEstimate(
            flops=2 * HALF * 2048 * depth, bytes_accessed=4 * 1024 * 1024, transcendentals=0
        ),
        name="proj_half",
    )(h, x, w)


def proj_rows_kernel(h_ref, *refs):
    w_ref, out_ref, xs = refs[-3:]

    @pl.when(pl.program_id(0) == 0)
    def _():
        for k, ref in enumerate(refs[:-3]):
            row = lax.rem(h_ref[1] + k, ROWS)

            @pl.when(row // 4 == h_ref[0])
            def _():
                xs[pl.ds(pl.multiple_of(lax.rem(row, 4) * SEQ, SEQ), SEQ)] = ref[...]

    result = nn(xs[...], w_ref[...]).astype(out_ref.dtype)
    for j in range(out_ref.shape[0]):
        out_ref[j] = result[:, j * LANE : (j + 1) * LANE]


def proj_rows_half(h, pieces, w, dtype):
    depth = pieces[0].shape[1]
    steps = 2
    wide = 2048 // steps
    return pl.pallas_call(
        proj_rows_kernel,
        grid_spec=pltpu.PrefetchScalarGridSpec(
            num_scalar_prefetch=1,
            grid=(steps,),
            in_specs=[pl.BlockSpec((SEQ, depth), lambda i, h: (0, 0))] * ROWS
            + [pl.BlockSpec((depth, wide), lambda i, h: (0, i))],
            out_specs=pl.BlockSpec((wide // LANE, HALF, LANE), lambda i, h: (i, 0, 0)),
            scratch_shapes=[pltpu.VMEM((HALF, depth), BF)],
        ),
        out_shape=jax.ShapeDtypeStruct((CHIPS, HALF, LANE), dtype),
        compiler_params=params(24),
        cost_estimate=pl.CostEstimate(
            flops=2 * HALF * 2048 * depth, bytes_accessed=4 * 1024 * 1024, transcendentals=0
        ),
        name="proj_rows_half",
    )(h, *pieces, w)


def project_out(product, mine, theirs, x, w):
    got = swap(product(theirs, x, w, BF))
    kept = product(mine, x, w, F32)
    return over_chips((kept + got.astype(F32)).astype(BF))


def residual_kernel(base_ref, p_ref, out_ref, copies_ref):
    total = p_ref[0].astype(F32)
    for j in range(1, CHIPS):
        total = total + p_ref[j].astype(F32)
    result = (base_ref[0, :HALF].astype(F32) + total).astype(BF)
    out_ref[...] = result
    for j in range(CHIPS):
        copies_ref[j] = result


def residual_copies(base, parts):
    return pl.pallas_call(
        residual_kernel,
        out_shape=(
            jax.ShapeDtypeStruct((HALF, LANE), BF),
            jax.ShapeDtypeStruct((CHIPS, HALF, LANE), BF),
        ),
        compiler_params=params(),
        name="residual_copies",
    )(base, parts)


def final_kernel(h_ref, base_ref, p_ref, keep_ref, give_ref):
    total = p_ref[0].astype(F32)
    for j in range(1, CHIPS):
        total = total + p_ref[j].astype(F32)
    done = (base_ref[...].astype(F32) + total).astype(BF)
    first, second = done[:, :64], done[:, 64:]
    keep_ref[...] = jnp.where(h_ref[0] == 0, first, second)
    give_ref[...] = jnp.where(h_ref[0] == 0, second, first)


def final_sum(h, base, parts):
    vmem = pl.BlockSpec(memory_space=pltpu.VMEM)
    return pl.pallas_call(
        final_kernel,
        in_specs=[pl.BlockSpec(memory_space=pltpu.SMEM), vmem, vmem],
        out_specs=(vmem, vmem),
        out_shape=(jax.ShapeDtypeStruct((HALF, 64), BF),) * 2,
        compiler_params=params(),
        name="final_sum",
    )(h, base, parts)


def place_kernel(h_ref, keep_ref, got_ref, out_ref):
    keep, got = keep_ref[...], got_ref[...]
    out_ref[:, :HALF] = jnp.transpose(jnp.where(h_ref[0] == 0, keep, got))
    out_ref[:, HALF:] = jnp.transpose(jnp.where(h_ref[0] == 0, got, keep))


def place_halves(h, keep, got):
    vmem = pl.BlockSpec(memory_space=pltpu.VMEM)
    return pl.pallas_call(
        place_kernel,
        in_specs=[pl.BlockSpec(memory_space=pltpu.SMEM), vmem, vmem],
        out_specs=vmem,
        out_shape=jax.ShapeDtypeStruct((64, TOK), BF),
        compiler_params=params(),
        name="place_halves",
    )(h, keep, got).T


def cut_kernel(h_ref, t_hbm, ga_hbm, gf_hbm, keep_ref, give_ref, t_ref, ga_ref, gf_ref, sems):
    pairs = ((t_hbm, t_ref), (ga_hbm, ga_ref), (gf_hbm, gf_ref))
    copies = [pltpu.make_async_copy(a, b, sems.at[n]) for n, (a, b) in enumerate(pairs)]
    for copy in copies:
        copy.start()
    for copy in copies:
        copy.wait()
    row = lax.broadcasted_iota(jnp.int32, (16, 64), 0)
    ga, gf = ga_ref[...].astype(F32), gf_ref[...].astype(F32)
    gains = jnp.where(row == 0, ga, jnp.where(row == 1, gf, 0.0)).astype(BF)
    keep_ref[HALF:] = gains
    give_ref[HALF:] = gains
    first = jnp.transpose(t_ref[:, :HALF])
    second = jnp.transpose(t_ref[:, HALF:])
    keep_ref[:HALF] = jnp.where(h_ref[0] == 0, first, second)
    give_ref[:HALF] = jnp.where(h_ref[0] == 0, second, first)


def cut_tokens(h, tokens_t, norm_attn, norm_ffn):
    hbm = pl.BlockSpec(memory_space=pltpu.HBM)
    vmem = pl.BlockSpec(memory_space=pltpu.VMEM)
    return pl.pallas_call(
        cut_kernel,
        in_specs=[pl.BlockSpec(memory_space=pltpu.SMEM), hbm, hbm, hbm],
        out_specs=(vmem, vmem),
        out_shape=(jax.ShapeDtypeStruct((HALF + 16, 64), BF),) * 2,
        scratch_shapes=[
            pltpu.VMEM((64, TOK), BF),
            pltpu.VMEM((1, 64), BF),
            pltpu.VMEM((1, 64), BF),
            pltpu.SemaphoreType.DMA((3,)),
        ],
        compiler_params=params(58),
        name="cut_tokens",
    )(h, tokens_t, norm_attn.reshape(1, 64), norm_ffn.reshape(1, 64))


def join_kernel(h_ref, keep_ref, got_ref, copies_ref):
    keep, got = keep_ref[...], got_ref[...]
    mine_first = jnp.concatenate([keep, got], axis=1)
    mine_last = jnp.concatenate([got, keep], axis=1)
    base = jnp.where(h_ref[0] == 0, mine_first, mine_last)
    for j in range(CHIPS):
        copies_ref[j] = base


def join_copies(h, keep, got):
    vmem = pl.BlockSpec(memory_space=pltpu.VMEM)
    return pl.pallas_call(
        join_kernel,
        in_specs=[pl.BlockSpec(memory_space=pltpu.SMEM), vmem, vmem],
        out_specs=vmem,
        out_shape=jax.ShapeDtypeStruct((CHIPS, HALF + 16, LANE), BF),
        compiler_params=params(),
        name="join_copies",
    )(h, keep, got)


def load_half(x_ref, xv, sems):
    copies = [
        pltpu.make_async_copy(x_ref.at[pl.ds(4 * i, 4)], xv.at[pl.ds(4 * i, 4)], sems.at[i])
        for i in range(CHIPS // 4)
    ]
    for copy in copies:
        copy.start()
    return copies


def gained_rows(copies, xv, g_ref, xs):
    for i, copy in enumerate(copies):
        copy.wait()
        for j in range(4 * i, 4 * i + 4):
            gain = g_ref[j, 1:2].astype(F32)
            xs[:, j * LANE : (j + 1) * LANE] = (xv[j].astype(F32) * gain).astype(BF)


HBM = pl.BlockSpec(memory_space=pltpu.HBM)


def gate_up_main_kernel(h_ref, x_ref, g_ref, wg_ref, wu_ref, *rest):
    out_ref, copy_ref, xv, xs, result, in_sems, out_sems = rest[-7:]
    gained_rows(load_half(x_ref, xv, in_sems), xv, g_ref, xs)
    rows = pl.ds(pl.multiple_of(h_ref[0] * HALF, HALF), HALF)
    copies = [pltpu.make_async_copy(xv, copy_ref, out_sems.at[2])]
    copies[0].start()
    for n, w_ref in enumerate((wg_ref, wu_ref)):
        result[n] = nt(xs[...], w_ref[...]).astype(BF)
        copies.append(
            pltpu.make_async_copy(
                result.at[n], out_ref.at[rows, pl.ds(n * MAIN, MAIN)], out_sems.at[n]
            )
        )
        copies[-1].start()
    for copy in copies:
        copy.wait()


def gate_up_main(h, x, gains, wg_t, wu_t, held=None):
    w_spec = pl.BlockSpec((MAIN, 2048), lambda i, h: (0, 0))
    in_specs = [
        HBM,
        pl.BlockSpec((CHIPS, 16, LANE), lambda i, h: (0, HALF // 16, 0)),
        w_spec,
        w_spec,
    ]
    operands = [h, x, gains, wg_t, wu_t]
    aliases = {}
    if held is not None:
        in_specs.append(HBM)
        operands.append(held)
        aliases = {5: 0}
    return pl.pallas_call(
        gate_up_main_kernel,
        grid_spec=pltpu.PrefetchScalarGridSpec(
            num_scalar_prefetch=1,
            grid=(1,),
            in_specs=in_specs,
            out_specs=(HBM, HBM),
            scratch_shapes=[
                pltpu.VMEM((CHIPS, HALF, LANE), BF),
                pltpu.VMEM((HALF, 2048), BF),
                pltpu.VMEM((2, HALF, MAIN), BF),
                pltpu.SemaphoreType.DMA((CHIPS // 4,)),
                pltpu.SemaphoreType.DMA((3,)),
            ],
        ),
        out_shape=(
            jax.ShapeDtypeStruct((TOK, 2 * MAIN), BF),
            jax.ShapeDtypeStruct((CHIPS, HALF, LANE), BF),
        ),
        input_output_aliases=aliases,
        compiler_params=params(24),
        cost_estimate=pl.CostEstimate(
            flops=4 * HALF * 2048 * MAIN,
            bytes_accessed=8 * 1024 * 1024,
            transcendentals=0,
        ),
        name="gate_up_main",
    )(*operands)


def gate_up_side_kernel(
    h_ref, own_ref, other_ref, g_ref, wg_ref, wu_ref, _, out_ref, xv, xs, wv, own_sems, other_sems, w_sems
):
    loads = [load_half(own_ref, xv.at[0], own_sems), load_half(other_ref, xv.at[1], other_sems)]
    w_loads = [
        pltpu.make_async_copy(w_ref.at[pl.ds(MAIN, REST)], wv.at[n], w_sems.at[n])
        for n, w_ref in enumerate((wg_ref, wu_ref))
    ]
    for copy in w_loads:
        copy.start()
    lane = lax.broadcasted_iota(jnp.int32, (HALF, SIDE // 2 - REST), 1)
    for at, half in ((0, h_ref[0]), (1, 1 - h_ref[0])):
        gained_rows(loads[at], xv.at[at], g_ref, xs)
        squares = None
        for j in range(CHIPS):
            wide = xv[at, j].astype(F32)
            squares = wide * wide if squares is None else squares + wide * wide
        high, low = split_two(jnp.sum(squares, axis=1, keepdims=True))
        extra = jnp.where(lane == 0, high, jnp.where(lane == 1, low, 0.0))
        rows = pl.ds(pl.multiple_of(half * HALF, HALF), HALF)
        if at == 0:
            for copy in w_loads:
                copy.wait()
        gate = jnp.concatenate([nt(xs[...], wv[0]), extra], axis=1)
        out_ref[rows, : SIDE // 2] = gate.astype(BF)
        up = jnp.concatenate([nt(xs[...], wv[1]), jnp.zeros_like(extra)], axis=1)
        out_ref[rows, SIDE // 2 :] = up.astype(BF)


def gate_up_side(h, own, other, gains, wg_t, wu_t, main):
    return pl.pallas_call(
        gate_up_side_kernel,
        grid_spec=pltpu.PrefetchScalarGridSpec(
            num_scalar_prefetch=1,
            grid=(1,),
            in_specs=[
                HBM,
                HBM,
                pl.BlockSpec((CHIPS, 16, LANE), lambda i, h: (0, HALF // 16, 0)),
                HBM,
                HBM,
                HBM,
            ],
            out_specs=pl.BlockSpec((TOK, SIDE), lambda i, h: (0, 0)),
            scratch_shapes=[
                pltpu.VMEM((2, CHIPS, HALF, LANE), BF),
                pltpu.VMEM((HALF, 2048), BF),
                pltpu.VMEM((2, REST, 2048), BF),
                pltpu.SemaphoreType.DMA((CHIPS // 4,)),
                pltpu.SemaphoreType.DMA((CHIPS // 4,)),
                pltpu.SemaphoreType.DMA((2,)),
            ],
        ),
        out_shape=jax.ShapeDtypeStruct((TOK, SIDE), BF),
        compiler_params=params(58),
        cost_estimate=pl.CostEstimate(
            flops=4 * TOK * 2048 * REST, bytes_accessed=6 * 1024 * 1024, transcendentals=0
        ),
        name="gate_up_side",
    )(h, own, other, gains, wg_t, wu_t, main)


def hidden_kernel(main_hbm, side_hbm, out_ref, main_ref, side_ref, sems):
    main_load = pltpu.make_async_copy(main_hbm, main_ref, sems.at[0])
    side_load = pltpu.make_async_copy(side_hbm, side_ref, sems.at[1])
    side_load.start()
    main_load.start()
    side_load.wait()
    side = side_ref[0].astype(F32)
    for j in range(1, ROWS):
        side = side + side_ref[j].astype(F32)
    squares = side[:, REST : REST + 1] + side[:, REST + 1 : REST + 2]
    inv = lax.rsqrt(squares / D + EPS)

    def gated(gate, up):
        gate, up = gate * inv, up * inv
        return (gate / (1.0 + jnp.exp(-gate)) * up).astype(BF)

    second = gated(side[:, :REST], side[:, SIDE // 2 : SIDE // 2 + REST])
    main_load.wait()
    first = gated(main_ref[:, :MAIN].astype(F32), main_ref[:, MAIN:].astype(F32))
    out_ref[:, :MAIN] = first
    out_ref[:, MAIN:] = second


def hidden_row(main, side):
    return pl.pallas_call(
        hidden_kernel,
        in_specs=[HBM, HBM],
        out_shape=jax.ShapeDtypeStruct((SEQ, FFL), BF),
        scratch_shapes=[
            pltpu.VMEM((SEQ, 2 * MAIN), BF),
            pltpu.VMEM((ROWS, SEQ, SIDE), BF),
            pltpu.SemaphoreType.DMA((2,)),
        ],
        compiler_params=params(58),
        name="hidden_row",
    )(main, side)


def from_ahead(x, k):
    return lax.ppermute(x, "gx", [(i, (i - k) % ROWS) for i in range(ROWS)])


def all_rows(x):
    ahead = {0: x}
    for k in (1, 7, 3, 5):
        ahead[k] = from_ahead(x, k)
    ahead[2] = from_ahead(ahead[1], 1)
    ahead[6] = from_ahead(ahead[7], 7)
    ahead[4] = from_ahead(ahead[3], 1)
    return [ahead[k] for k in range(ROWS)]


def rope_table():
    inv_freq = np.power(
        np.float32(ROPE_BASE), -(np.arange(64, dtype=np.float32) * np.float32(2.0 / HEAD_DIM))
    ).astype(np.float32)
    angles = (np.arange(SEQ, dtype=np.float32)[:, None] * inv_freq[None, :]).astype(np.float64)
    cos, sin = np.cos(angles), np.sin(angles)
    table = np.zeros((2, LANE, LANE), np.float32)
    table[0, :SEQ] = np.concatenate([cos, cos], axis=1)
    table[1, :SEQ] = np.concatenate([-sin, sin], axis=1)
    return table


def per_device(
    tokens,
    norm_attn,
    w_query,
    w_key,
    w_value,
    w_out,
    norm_ffn,
    w_gate,
    w_up,
    w_down,
    lengths,
    segments,
):
    core = lax.axis_index("gy") % 2
    c = jnp.reshape(core, (1,)).astype(jnp.int32)

    keep, give = cut_tokens(c, tokens.T, norm_attn, norm_ffn)
    base = join_copies(c, keep, swap(give))
    first = over_chips(base)
    other = swap(first)
    held = qkv_half(c, first, first, w_query, w_key.T, w_value.T)
    parts = qkv_half(1 - c, other, first, w_query, w_key.T, w_value.T, held)
    q, kv = qkv_sum(over_rows(parts))
    kv = lax.all_to_all(kv, "gy", 0, 0, axis_index_groups=KV_GROUPS, tiled=True)
    attended = over_rows(attend(lengths, q, kv, segments)).reshape(TOK, 256)
    residual, copies = residual_copies(
        base, project_out(proj_half, c, 1 - c, attended, w_out)
    )

    own = over_chips(copies)
    other = swap(own)
    weights = (w_gate.T, w_up.T)
    held, own = gate_up_main(c, own, first, *weights)
    main, other = gate_up_main(1 - c, other, first, *weights, held)
    side = gate_up_side(c, own, other, first, *weights, main)
    main = lax.psum_scatter(main, "gx", scatter_dimension=0, tiled=True)
    side = over_rows(side.reshape(ROWS, SEQ, SIDE))
    hidden = all_rows(hidden_row(main, side))
    at = jnp.reshape(lax.axis_index("gx"), (1,)).astype(jnp.int32)
    mine, theirs = jnp.concatenate([c, at]), jnp.concatenate([1 - c, at])
    keep, give = final_sum(c, residual, project_out(proj_rows_half, mine, theirs, hidden, w_down))
    return place_halves(c, keep, swap(give))


def solution(mesh):
    in_specs = (
        P(None, ("gx", "gy")),
        P(("gx", "gy")),
        P("gx", "gy"),
        P("gx", "gy"),
        P("gx", "gy"),
        P("gy", "gx"),
        P(("gx", "gy")),
        P("gx", "gy"),
        P("gx", "gy"),
        P("gy", "gx"),
        P("gx"),
        P("gx"),
    )
    out_specs = P(None, ("gx", "gy"))
    return jax.shard_map(
        per_device, mesh=mesh, in_specs=in_specs, out_specs=out_specs, check_vma=False
    )
```

```python
import functools
import math

import jax
import jax.numpy as jnp
import numpy as np
from jax import lax
from jax.experimental import pallas as pl
from jax.experimental.pallas import tpu as pltpu
from jax.sharding import PartitionSpec as P

D = 16384
HEADS = 64
KV_HEADS = 4
HEAD_DIM = 128
SEQ = 96
EPS = 1e-05
ROPE_BASE = 500000.0

BF = jnp.bfloat16
F32 = jnp.float32

TOK = 768
HALF = 384
CHIPS = 16
LANE = 128
ROWS = 8
KSTEP = 4
FFL = 832
MAIN = 640
REST = FFL - MAIN
SIDE = 512
CHIP_GROUPS = [[2 * i + c for i in range(CHIPS)] for c in range(2)]
KV_GROUPS = [list(range(8 * i, 8 * i + 8)) for i in range(4)]


def swap(x):
    return lax.ppermute(x, "gy", [(i, i ^ 1) for i in range(32)])


def over_chips(x):
    return lax.all_to_all(x, "gy", 0, 0, axis_index_groups=CHIP_GROUPS, tiled=True)


def over_rows(x):
    return lax.all_to_all(x, "gx", 0, 0, tiled=True)


def params(mib=16):
    return pltpu.CompilerParams(vmem_limit_bytes=mib * 1024 * 1024)


def nt(a, b):
    return lax.dot_general(a, b, (((1,), (1,)), ((), ())), preferred_element_type=F32)


def nn(a, b):
    return jnp.dot(a, b, preferred_element_type=F32)


def fold_squares(wide):
    total = None
    for j in range(wide.shape[1] // LANE):
        part = wide[:, j * LANE : (j + 1) * LANE]
        total = part * part if total is None else total + part * part
    return total


def split_two(total):
    high = total.astype(BF).astype(F32)
    return high, total - high


def gained_block(x_ref, g_ref, row):
    chips = range(x_ref.shape[0])
    wide = jnp.concatenate([x_ref[j, :HALF] for j in chips], axis=1).astype(F32)
    gain = jnp.concatenate([g_ref[j, row : row + 1] for j in chips], axis=1).astype(F32)
    return wide, (wide * gain).astype(BF)


def qkv_kernel(h_ref, x_ref, g_ref, wq_ref, wk_ref, wv_ref, *rest):
    out_ref, gains_ref, acc_q, acc_kv, acc_sq = rest[-5:]
    k = pl.program_id(0)
    gains_ref[...] = g_ref[...]

    @pl.when(k == 0)
    def _():
        acc_q[...] = jnp.zeros_like(acc_q)
        acc_kv[...] = jnp.zeros_like(acc_kv)
        acc_sq[...] = jnp.zeros_like(acc_sq)

    wide, gained = gained_block(x_ref, g_ref, 0)
    acc_sq[...] += fold_squares(wide)
    acc_q[...] += nn(gained, wq_ref[...])
    acc_kv[...] += nt(jnp.concatenate([wk_ref[...], wv_ref[...]], axis=0), gained)

    @pl.when(k == pl.num_programs(0) - 1)
    def _():
        high, low = split_two(jnp.sum(jnp.transpose(acc_sq[...]), axis=0, keepdims=True))
        at = lax.broadcasted_iota(jnp.int32, (16, SEQ), 0)
        gap = jnp.zeros((16, LANE - SEQ), F32)
        for r in range(HALF // SEQ):
            here = slice(r * SEQ, (r + 1) * SEQ)
            out_ref[r, :SEQ] = acc_q[here].astype(BF)
            kv = acc_kv[:, here]
            sums = jnp.where(at == 0, high[:, here], jnp.where(at == 1, low[:, here], 0.0))
            top = jnp.concatenate([kv[:16], gap, kv[16:], gap], axis=1)
            bottom = jnp.concatenate([sums, gap, sums, gap], axis=1)
            out_ref[r, SEQ:] = jnp.concatenate([top, bottom], axis=0).astype(BF)


def qkv_half(h, x, gains, wq, wk_t, wv_t, held=None):
    depth = 2048 // KSTEP
    chips = CHIPS // KSTEP
    in_specs = [
        pl.BlockSpec((chips, HALF, LANE), lambda k, h: (k, 0, 0)),
        pl.BlockSpec((chips, 16, LANE), lambda k, h: (k, HALF // 16, 0)),
        pl.BlockSpec((depth, 256), lambda k, h: (k, 0)),
        pl.BlockSpec((16, depth), lambda k, h: (0, k)),
        pl.BlockSpec((16, depth), lambda k, h: (0, k)),
    ]
    operands = [h, x, gains, wq, wk_t, wv_t]
    aliases = {}
    if held is not None:
        in_specs.append(pl.BlockSpec(memory_space=pl.ANY))
        operands.append(held)
        aliases = {6: 0}
    return pl.pallas_call(
        qkv_kernel,
        grid_spec=pltpu.PrefetchScalarGridSpec(
            num_scalar_prefetch=1,
            grid=(KSTEP,),
            in_specs=in_specs,
            out_specs=(
                pl.BlockSpec((HALF // SEQ, 128, 256), lambda k, h: (h[0], 0, 0)),
                pl.BlockSpec((chips, 16, LANE), lambda k, h: (k, 0, 0)),
            ),
            scratch_shapes=[
                pltpu.VMEM((HALF, 256), F32),
                pltpu.VMEM((32, HALF), F32),
                pltpu.VMEM((HALF, LANE), F32),
            ],
        ),
        out_shape=(
            jax.ShapeDtypeStruct((ROWS, 128, 256), BF),
            jax.ShapeDtypeStruct((CHIPS, 16, LANE), BF),
        ),
        input_output_aliases=aliases,
        compiler_params=params(),
        cost_estimate=pl.CostEstimate(
            flops=2 * HALF * 2048 * 384, bytes_accessed=4 * 1024 * 1024, transcendentals=0
        ),
        name="qkv_half",
    )(*operands)


def qkv_sum_kernel(p_ref, q_ref, kv_ref):
    total = p_ref[0].astype(F32)
    for j in range(1, ROWS):
        total = total + p_ref[j].astype(F32)
    squares = total[112:113, :LANE] + total[113:114, :LANE]
    inv = lax.rsqrt(squares / D + EPS)
    down = jnp.transpose(jnp.broadcast_to(inv, (LANE, LANE)))[:SEQ]
    q_ref[...] = total[:SEQ] * jnp.concatenate([down, down], axis=1)
    kv = jnp.concatenate([total[96:112, :SEQ], total[96:112, LANE : LANE + SEQ]], axis=0)
    kv = kv * inv[:, :SEQ]
    for j in range(8):
        kv_ref[j] = kv


def qkv_sum(parts):
    return pl.pallas_call(
        qkv_sum_kernel,
        out_shape=(
            jax.ShapeDtypeStruct((SEQ, 256), F32),
            jax.ShapeDtypeStruct((8, 32, SEQ), F32),
        ),
        compiler_params=params(),
        name="qkv_sum",
    )(parts)


def attend_kernel(len_ref, q_ref, kv_ref, seg_ref, table_ref, out_ref):
    cos, sin = table_ref[0], table_ref[1]
    cos_t, sin_t = jnp.transpose(cos)[:, :SEQ], jnp.transpose(sin)[:, :SEQ]
    cos, sin = cos[:SEQ], sin[:SEQ]
    keys = jnp.concatenate([kv_ref[j, :16] for j in range(8)], axis=0)
    turned = jnp.concatenate([keys[64:], keys[:64]], axis=0)
    keys = (keys * cos_t + turned * sin_t).astype(BF)
    values = jnp.concatenate([kv_ref[j, 16:] for j in range(8)], axis=0).astype(BF)
    seg = jnp.concatenate([seg_ref[...].astype(F32), jnp.zeros((1, LANE - SEQ), F32)], axis=1)
    seg = jnp.broadcast_to(seg, (LANE, LANE))
    same = (seg == jnp.transpose(seg))[:SEQ, :SEQ]
    q_at = lax.broadcasted_iota(jnp.int32, (SEQ, SEQ), 0)
    k_at = lax.broadcasted_iota(jnp.int32, (SEQ, SEQ), 1)
    allowed = same & (k_at <= q_at) & (k_at < len_ref[0])
    allowed = allowed | (k_at == q_at)
    for head in range(2):
        query = q_ref[:, head * HEAD_DIM : (head + 1) * HEAD_DIM]
        query = (query * cos + pltpu.roll(query, 64, 1) * sin).astype(BF)
        scores = nn(query, keys) * (1.0 / math.sqrt(HEAD_DIM))
        scores = jnp.where(allowed, scores, F32(-1e30))
        expo = jnp.exp(scores - jnp.max(scores, axis=1, keepdims=True))
        soft = (expo / jnp.sum(expo, axis=1, keepdims=True)).astype(BF)
        attended = nt(soft, values).astype(BF)
        for j in range(ROWS):
            out_ref[j, :, head * HEAD_DIM : (head + 1) * HEAD_DIM] = attended


def attend(lengths, q, kv, segments):
    vmem = pl.BlockSpec(memory_space=pltpu.VMEM)
    return pl.pallas_call(
        attend_kernel,
        in_specs=[pl.BlockSpec(memory_space=pltpu.SMEM)] + [vmem] * 4,
        out_specs=vmem,
        out_shape=jax.ShapeDtypeStruct((ROWS, SEQ, 256), BF),
        compiler_params=params(),
        name="attend",
    )(lengths, q, kv, segments.reshape(1, SEQ), rope_table())


def proj_kernel(h_ref, x_ref, w_ref, out_ref):
    result = nn(x_ref[...], w_ref[...]).astype(out_ref.dtype)
    for j in range(out_ref.shape[0]):
        out_ref[j] = result[:, j * LANE : (j + 1) * LANE]


def proj_half(h, x, w, dtype):
    depth = x.shape[1]
    steps = 2
    wide = 2048 // steps
    return pl.pallas_call(
        proj_kernel,
        grid_spec=pltpu.PrefetchScalarGridSpec(
            num_scalar_prefetch=1,
            grid=(steps,),
            in_specs=[
                pl.BlockSpec((HALF, depth), lambda i, h: (h[0], 0)),
                pl.BlockSpec((depth, wide), lambda i, h: (0, i)),
            ],
            out_specs=pl.BlockSpec((wide // LANE, HALF, LANE), lambda i, h: (i, 0, 0)),
        ),
        out_shape=jax.ShapeDtypeStruct((CHIPS, HALF, LANE), dtype),
        compiler_params=params(),
        cost_estimate=pl.CostEstimate(
            flops=2 * HALF * 2048 * depth, bytes_accessed=4 * 1024 * 1024, transcendentals=0
        ),
        name="proj_half",
    )(h, x, w)


def project_out(mine, theirs, x, w):
    given = proj_half(theirs, x, w, BF)
    got = swap(given)
    kept = proj_half(mine, x, w, F32)
    return over_chips((kept + got.astype(F32)).astype(BF))


def residual_kernel(base_ref, p_ref, out_ref, copies_ref):
    total = p_ref[0].astype(F32)
    for j in range(1, CHIPS):
        total = total + p_ref[j].astype(F32)
    result = (base_ref[0, :HALF].astype(F32) + total).astype(BF)
    out_ref[...] = result
    for j in range(CHIPS):
        copies_ref[j] = result


def residual_copies(base, parts):
    return pl.pallas_call(
        residual_kernel,
        out_shape=(
            jax.ShapeDtypeStruct((HALF, LANE), BF),
            jax.ShapeDtypeStruct((CHIPS, HALF, LANE), BF),
        ),
        compiler_params=params(),
        name="residual_copies",
    )(base, parts)


def final_kernel(h_ref, base_ref, p_ref, keep_ref, give_ref):
    total = p_ref[0].astype(F32)
    for j in range(1, CHIPS):
        total = total + p_ref[j].astype(F32)
    done = (base_ref[...].astype(F32) + total).astype(BF)
    first, second = done[:, :64], done[:, 64:]
    keep_ref[...] = jnp.where(h_ref[0] == 0, first, second)
    give_ref[...] = jnp.where(h_ref[0] == 0, second, first)


def final_sum(h, base, parts):
    vmem = pl.BlockSpec(memory_space=pltpu.VMEM)
    return pl.pallas_call(
        final_kernel,
        in_specs=[pl.BlockSpec(memory_space=pltpu.SMEM), vmem, vmem],
        out_specs=(vmem, vmem),
        out_shape=(jax.ShapeDtypeStruct((HALF, 64), BF),) * 2,
        compiler_params=params(),
        name="final_sum",
    )(h, base, parts)


def place_kernel(h_ref, keep_ref, got_ref, out_ref):
    keep, got = keep_ref[...], got_ref[...]
    out_ref[:, :HALF] = jnp.transpose(jnp.where(h_ref[0] == 0, keep, got))
    out_ref[:, HALF:] = jnp.transpose(jnp.where(h_ref[0] == 0, got, keep))


def place_halves(h, keep, got):
    vmem = pl.BlockSpec(memory_space=pltpu.VMEM)
    return pl.pallas_call(
        place_kernel,
        in_specs=[pl.BlockSpec(memory_space=pltpu.SMEM), vmem, vmem],
        out_specs=vmem,
        out_shape=jax.ShapeDtypeStruct((64, TOK), BF),
        compiler_params=params(),
        name="place_halves",
    )(h, keep, got).T


def cut_kernel(h_ref, other_ref, at_ref, t_ref, ga_ref, gf_ref, keep_ref, give_ref):
    row = lax.broadcasted_iota(jnp.int32, (16, 64), 0)
    ga, gf = ga_ref[...].astype(F32), gf_ref[...].astype(F32)
    gains = jnp.where(row == 0, ga, jnp.where(row == 1, gf, 0.0)).astype(BF)
    keep_ref[HALF:] = gains
    give_ref[HALF:] = gains
    first = jnp.transpose(t_ref[:, :HALF])
    second = jnp.transpose(t_ref[:, HALF:])
    keep_ref[:HALF] = jnp.where(h_ref[0] == 0, first, second)
    give_ref[:HALF] = jnp.where(h_ref[0] == 0, second, first)


def cut_tokens(h, other, at, tokens_t, norm_attn, norm_ffn):
    whole = lambda *shape: pl.BlockSpec(shape, lambda i: (0, 0))
    return pl.pallas_call(
        cut_kernel,
        grid=(1,),
        in_specs=[
            pl.BlockSpec(memory_space=pltpu.SMEM),
            pl.BlockSpec(memory_space=pltpu.SMEM),
            pl.BlockSpec(memory_space=pltpu.SMEM),
            whole(64, TOK),
            whole(1, 64),
            whole(1, 64),
        ],
        out_specs=(whole(HALF + 16, 64), whole(HALF + 16, 64)),
        out_shape=(jax.ShapeDtypeStruct((HALF + 16, 64), BF),) * 2,
        compiler_params=params(),
        name="cut_tokens",
    )(h, other, at, tokens_t, norm_attn.reshape(1, 64), norm_ffn.reshape(1, 64))


def join_kernel(h_ref, keep_ref, got_ref, copies_ref):
    keep, got = keep_ref[...], got_ref[...]
    mine_first = jnp.concatenate([keep, got], axis=1)
    mine_last = jnp.concatenate([got, keep], axis=1)
    base = jnp.where(h_ref[0] == 0, mine_first, mine_last)
    for j in range(CHIPS):
        copies_ref[j] = base


def join_copies(h, keep, got):
    vmem = pl.BlockSpec(memory_space=pltpu.VMEM)
    return pl.pallas_call(
        join_kernel,
        in_specs=[pl.BlockSpec(memory_space=pltpu.SMEM), vmem, vmem],
        out_specs=vmem,
        out_shape=jax.ShapeDtypeStruct((CHIPS, HALF + 16, LANE), BF),
        compiler_params=params(),
        name="join_copies",
    )(h, keep, got)


def gained_rows(x_ref, g_ref, xs):
    for j in range(CHIPS):
        gain = g_ref[j, 1:2].astype(F32)
        xs[:, j * LANE : (j + 1) * LANE] = (x_ref[j].astype(F32) * gain).astype(BF)


def gate_up_main_kernel(h_ref, x_ref, g_ref, wg_ref, wu_ref, *rest):
    out_ref, made_ref, xs = rest[-3:]
    step = pl.program_id(0)
    made_ref[0] = step

    @pl.when(step == 0)
    def _():
        gained_rows(x_ref, g_ref, xs)

    wide = wg_ref.shape[0]
    at = pl.multiple_of(step * wide, wide)
    out_ref[:, pl.ds(at, wide)] = nt(xs[...], wg_ref[...]).astype(BF)
    out_ref[:, pl.ds(MAIN + at, wide)] = nt(xs[...], wu_ref[...]).astype(BF)


def gate_up_main(h, x, gains, wg_t, wu_t, held=None):
    steps = 1
    wide = MAIN // steps
    in_specs = [
        pl.BlockSpec((CHIPS, HALF, LANE), lambda i, h: (0, 0, 0)),
        pl.BlockSpec((CHIPS, 16, LANE), lambda i, h: (0, 0, 0)),
        pl.BlockSpec((wide, 2048), lambda i, h: (i, 0)),
        pl.BlockSpec((wide, 2048), lambda i, h: (i, 0)),
    ]
    operands = [h, x, gains, wg_t, wu_t]
    aliases = {}
    if held is not None:
        in_specs.append(pl.BlockSpec(memory_space=pl.ANY))
        operands.append(held)
        aliases = {5: 0}
    return pl.pallas_call(
        gate_up_main_kernel,
        grid_spec=pltpu.PrefetchScalarGridSpec(
            num_scalar_prefetch=1,
            grid=(steps,),
            in_specs=in_specs,
            out_specs=(
                pl.BlockSpec((HALF, 2 * MAIN), lambda i, h: (h[0], 0)),
                pl.BlockSpec(memory_space=pltpu.SMEM),
            ),
            scratch_shapes=[pltpu.VMEM((HALF, 2048), BF)],
        ),
        out_shape=(
            jax.ShapeDtypeStruct((TOK, 2 * MAIN), BF),
            jax.ShapeDtypeStruct((1,), jnp.int32),
        ),
        input_output_aliases=aliases,
        compiler_params=params(24),
        cost_estimate=pl.CostEstimate(
            flops=4 * HALF * 2048 * MAIN,
            bytes_accessed=8 * 1024 * 1024,
            transcendentals=0,
        ),
        name="gate_up_main",
    )(*operands)


def gate_up_side_kernel(h_ref, own_ref, other_ref, g_ref, wg_ref, wu_ref, _, out_ref, xs):
    lane = lax.broadcasted_iota(jnp.int32, (HALF, SIDE // 2 - REST), 1)
    for x_ref, half in ((own_ref, h_ref[0]), (other_ref, 1 - h_ref[0])):
        gained_rows(x_ref, g_ref, xs)
        squares = None
        for j in range(CHIPS):
            wide = x_ref[j].astype(F32)
            squares = wide * wide if squares is None else squares + wide * wide
        high, low = split_two(jnp.sum(squares, axis=1, keepdims=True))
        extra = jnp.where(lane == 0, high, jnp.where(lane == 1, low, 0.0))
        rows = pl.ds(pl.multiple_of(half * HALF, HALF), HALF)
        gate = jnp.concatenate([nt(xs[...], wg_ref[...]), extra], axis=1)
        out_ref[rows, : SIDE // 2] = gate.astype(BF)
        up = jnp.concatenate([nt(xs[...], wu_ref[...]), jnp.zeros_like(extra)], axis=1)
        out_ref[rows, SIDE // 2 :] = up.astype(BF)


def gate_up_side(h, own, other, gains, wg_t, wu_t, made):
    x_spec = pl.BlockSpec((CHIPS, HALF, LANE), lambda i, h: (0, 0, 0))
    w_spec = pl.BlockSpec((pl.Element(REST), pl.Element(2048)), lambda i, h: (MAIN, 0))
    return pl.pallas_call(
        gate_up_side_kernel,
        grid_spec=pltpu.PrefetchScalarGridSpec(
            num_scalar_prefetch=1,
            grid=(1,),
            in_specs=[
                x_spec,
                x_spec,
                pl.BlockSpec((CHIPS, 16, LANE), lambda i, h: (0, 0, 0)),
                w_spec,
                w_spec,
                pl.BlockSpec(memory_space=pltpu.SMEM),
            ],
            out_specs=pl.BlockSpec((TOK, SIDE), lambda i, h: (0, 0)),
            scratch_shapes=[pltpu.VMEM((HALF, 2048), BF)],
        ),
        out_shape=jax.ShapeDtypeStruct((TOK, SIDE), BF),
        compiler_params=params(58),
        cost_estimate=pl.CostEstimate(
            flops=4 * TOK * 2048 * REST, bytes_accessed=6 * 1024 * 1024, transcendentals=0
        ),
        name="gate_up_side",
    )(h, own, other, gains, wg_t, wu_t, made)


def hidden_kernel(main_ref, side_ref, out_ref):
    side = side_ref[0].astype(F32)
    for j in range(1, ROWS):
        side = side + side_ref[j].astype(F32)
    squares = side[:, REST : REST + 1] + side[:, REST + 1 : REST + 2]
    inv = lax.rsqrt(squares / D + EPS)

    def gated(gate, up):
        gate, up = gate * inv, up * inv
        return (gate / (1.0 + jnp.exp(-gate)) * up).astype(BF)

    first = gated(main_ref[:, :MAIN].astype(F32), main_ref[:, MAIN:].astype(F32))
    second = gated(side[:, :REST], side[:, SIDE // 2 : SIDE // 2 + REST])
    out_ref[:, :MAIN] = first
    out_ref[:, MAIN:] = second


def hidden_row(main, side):
    return pl.pallas_call(
        hidden_kernel,
        out_shape=jax.ShapeDtypeStruct((SEQ, FFL), BF),
        compiler_params=params(),
        name="hidden_row",
    )(main, side)


def from_ahead(x, k):
    return lax.ppermute(x, "gx", [(i, (i - k) % ROWS) for i in range(ROWS)])


def order_kernel(at_ref, *refs):
    out_ref = refs[-1]
    for k, ref in enumerate(refs[:-1]):
        out_ref[lax.rem(at_ref[0] + k, ROWS)] = ref[...]


def all_rows(at, x):
    ahead = {0: x}
    for k in (1, 7, 3, 5):
        ahead[k] = from_ahead(x, k)
    ahead[2] = from_ahead(ahead[1], 1)
    ahead[6] = from_ahead(ahead[7], 7)
    ahead[4] = from_ahead(ahead[3], 1)
    vmem = pl.BlockSpec(memory_space=pltpu.VMEM)
    return pl.pallas_call(
        order_kernel,
        in_specs=[pl.BlockSpec(memory_space=pltpu.SMEM)] + [vmem] * ROWS,
        out_specs=vmem,
        out_shape=jax.ShapeDtypeStruct((ROWS,) + x.shape, x.dtype),
        compiler_params=params(),
        name="order_rows",
    )(at, *[ahead[k] for k in range(ROWS)])


def rope_table():
    inv_freq = np.power(
        np.float32(ROPE_BASE), -(np.arange(64, dtype=np.float32) * np.float32(2.0 / HEAD_DIM))
    ).astype(np.float32)
    angles = (np.arange(SEQ, dtype=np.float32)[:, None] * inv_freq[None, :]).astype(np.float64)
    cos, sin = np.cos(angles), np.sin(angles)
    table = np.zeros((2, LANE, LANE), np.float32)
    table[0, :SEQ] = np.concatenate([cos, cos], axis=1)
    table[1, :SEQ] = np.concatenate([-sin, sin], axis=1)
    return table


def per_device(
    tokens,
    norm_attn,
    w_query,
    w_key,
    w_value,
    w_out,
    norm_ffn,
    w_gate,
    w_up,
    w_down,
    lengths,
    segments,
):
    core, at = lax.axis_index("gy") % 2, jnp.reshape(lax.axis_index("gx"), (1,))
    mine, theirs = jnp.reshape(core, (1,)), jnp.reshape(1 - core, (1,))

    keep, give = cut_tokens(mine, theirs, at, tokens.T, norm_attn, norm_ffn)
    base = join_copies(mine, keep, swap(give))
    first = over_chips(base)
    other = swap(first)
    held, gains = qkv_half(mine, first, first, w_query, w_key.T, w_value.T)
    parts, _ = qkv_half(theirs, other, first, w_query, w_key.T, w_value.T, held)
    q, kv = qkv_sum(over_rows(parts))
    kv = lax.all_to_all(kv, "gy", 0, 0, axis_index_groups=KV_GROUPS, tiled=True)
    attended = over_rows(attend(lengths, q, kv, segments)).reshape(TOK, 256)
    residual, copies = residual_copies(base, project_out(mine, theirs, attended, w_out))

    own = over_chips(copies)
    other = swap(own)
    weights = (w_gate.T, w_up.T)
    held, _ = gate_up_main(mine, own, gains, *weights)
    main, made = gate_up_main(theirs, other, gains, *weights, held)
    side = gate_up_side(mine, own, other, gains, *weights, made)
    main = lax.psum_scatter(main, "gx", scatter_dimension=0, tiled=True)
    side = over_rows(side.reshape(ROWS, SEQ, SIDE))
    hidden = all_rows(at, hidden_row(main, side)).reshape(TOK, FFL)
    keep, give = final_sum(mine, residual, project_out(mine, theirs, hidden, w_down))
    return place_halves(mine, keep, swap(give))


def solution(mesh):
    in_specs = (
        P(None, ("gx", "gy")),
        P(("gx", "gy")),
        P("gx", "gy"),
        P("gx", "gy"),
        P("gx", "gy"),
        P("gy", "gx"),
        P(("gx", "gy")),
        P("gx", "gy"),
        P("gx", "gy"),
        P("gy", "gx"),
        P("gx"),
        P("gx"),
    )
    out_specs = P(None, ("gx", "gy"))
    return jax.shard_map(
        per_device, mesh=mesh, in_specs=in_specs, out_specs=out_specs, check_vma=False
    )
```

```python
import functools
import math

import jax
import jax.numpy as jnp
import numpy as np
from jax import lax
from jax.experimental import pallas as pl
from jax.experimental.pallas import tpu as pltpu
from jax.sharding import PartitionSpec as P

D = 16384
HEADS = 64
KV_HEADS = 4
HEAD_DIM = 128
SEQ = 96
EPS = 1e-05
ROPE_BASE = 500000.0

BF = jnp.bfloat16
F32 = jnp.float32

TOK = 768
HALF = 384
CHIPS = 16
LANE = 128
ROWS = 8
KSTEP = 4
FFL = 832
MAIN = 768
REST = FFL - MAIN
SIDE = 256
CHIP_GROUPS = [[2 * i + c for i in range(CHIPS)] for c in range(2)]
KV_GROUPS = [list(range(8 * i, 8 * i + 8)) for i in range(4)]


def swap(x):
    return lax.ppermute(x, "gy", [(i, i ^ 1) for i in range(32)])


def over_chips(x):
    return lax.all_to_all(x, "gy", 0, 0, axis_index_groups=CHIP_GROUPS, tiled=True)


def over_rows(x):
    return lax.all_to_all(x, "gx", 0, 0, tiled=True)


def params(mib=16):
    return pltpu.CompilerParams(vmem_limit_bytes=mib * 1024 * 1024)


def nt(a, b):
    return lax.dot_general(a, b, (((1,), (1,)), ((), ())), preferred_element_type=F32)


def nn(a, b):
    return jnp.dot(a, b, preferred_element_type=F32)


def fold_squares(wide):
    total = None
    for j in range(wide.shape[1] // LANE):
        part = wide[:, j * LANE : (j + 1) * LANE]
        total = part * part if total is None else total + part * part
    return total


def split_two(total):
    high = total.astype(BF).astype(F32)
    return high, total - high


def gained_block(x_ref, g_ref, row):
    chips = range(x_ref.shape[0])
    wide = jnp.concatenate([x_ref[j, :HALF] for j in chips], axis=1).astype(F32)
    gain = jnp.concatenate([g_ref[j, row : row + 1] for j in chips], axis=1).astype(F32)
    return wide, (wide * gain).astype(BF)


def qkv_kernel(h_ref, x_ref, g_ref, wq_ref, wk_ref, wv_ref, *rest):
    out_ref, gains_ref, acc_q, acc_kv, acc_sq = rest[-5:]
    k = pl.program_id(0)
    gains_ref[...] = g_ref[...]

    @pl.when(k == 0)
    def _():
        acc_q[...] = jnp.zeros_like(acc_q)
        acc_kv[...] = jnp.zeros_like(acc_kv)
        acc_sq[...] = jnp.zeros_like(acc_sq)

    wide, gained = gained_block(x_ref, g_ref, 0)
    acc_sq[...] += fold_squares(wide)
    acc_q[...] += nn(gained, wq_ref[...])
    acc_kv[...] += nt(jnp.concatenate([wk_ref[...], wv_ref[...]], axis=0), gained)

    @pl.when(k == pl.num_programs(0) - 1)
    def _():
        high, low = split_two(jnp.sum(jnp.transpose(acc_sq[...]), axis=0, keepdims=True))
        def squeezed(row):
            cuts = [row[:, j * 32 : (j + 1) * 32] for j in range(SEQ // 32)]
            return jnp.concatenate(cuts + [jnp.zeros((16 - SEQ // 32, 32), F32)], axis=0)

        for r in range(HALF // SEQ):
            here = slice(r * SEQ, (r + 1) * SEQ)
            kv = acc_kv[:, here]
            out_ref[r, :SEQ] = acc_q[here].astype(BF)
            below = [kv[:16], squeezed(high[:, here]), kv[16:], squeezed(low[:, here])]
            out_ref[r, SEQ:] = jnp.concatenate(below, axis=1).astype(BF)


def qkv_half(h, x, gains, wq, wk_t, wv_t, held=None):
    depth = 2048 // KSTEP
    chips = CHIPS // KSTEP
    in_specs = [
        pl.BlockSpec((chips, HALF, LANE), lambda k, h: (k, 0, 0)),
        pl.BlockSpec((chips, 16, LANE), lambda k, h: (k, HALF // 16, 0)),
        pl.BlockSpec((depth, 256), lambda k, h: (k, 0)),
        pl.BlockSpec((16, depth), lambda k, h: (0, k)),
        pl.BlockSpec((16, depth), lambda k, h: (0, k)),
    ]
    operands = [h, x, gains, wq, wk_t, wv_t]
    aliases = {}
    if held is not None:
        in_specs.append(pl.BlockSpec(memory_space=pl.ANY))
        operands.append(held)
        aliases = {6: 0}
    return pl.pallas_call(
        qkv_kernel,
        grid_spec=pltpu.PrefetchScalarGridSpec(
            num_scalar_prefetch=1,
            grid=(KSTEP,),
            in_specs=in_specs,
            out_specs=(
                pl.BlockSpec((HALF // SEQ, SEQ + 16, 256), lambda k, h: (h[0], 0, 0)),
                pl.BlockSpec((chips, 16, LANE), lambda k, h: (k, 0, 0)),
            ),
            scratch_shapes=[
                pltpu.VMEM((HALF, 256), F32),
                pltpu.VMEM((32, HALF), F32),
                pltpu.VMEM((HALF, LANE), F32),
            ],
        ),
        out_shape=(
            jax.ShapeDtypeStruct((ROWS, SEQ + 16, 256), BF),
            jax.ShapeDtypeStruct((CHIPS, 16, LANE), BF),
        ),
        input_output_aliases=aliases,
        compiler_params=params(),
        cost_estimate=pl.CostEstimate(
            flops=2 * HALF * 2048 * 384, bytes_accessed=4 * 1024 * 1024, transcendentals=0
        ),
        name="qkv_half",
    )(*operands)


def qkv_sum_kernel(p_ref, q_ref, kv_ref):
    total = p_ref[0].astype(F32)
    for j in range(1, ROWS):
        total = total + p_ref[j].astype(F32)
    extra = total[SEQ:, SEQ:LANE] + total[SEQ:, LANE + SEQ :]
    squares = jnp.concatenate([extra[j : j + 1] for j in range(3)] + [extra[3:4]], axis=1)
    inv = lax.rsqrt(squares / D + EPS)
    down = jnp.transpose(jnp.broadcast_to(inv, (LANE, LANE)))[:SEQ]
    q_ref[...] = total[:SEQ] * jnp.concatenate([down, down], axis=1)
    kv = jnp.concatenate([total[96:112, :SEQ], total[96:112, LANE : LANE + SEQ]], axis=0)
    kv = kv * inv[:, :SEQ]
    for j in range(8):
        kv_ref[j] = kv


def qkv_sum(parts):
    return pl.pallas_call(
        qkv_sum_kernel,
        out_shape=(
            jax.ShapeDtypeStruct((SEQ, 256), F32),
            jax.ShapeDtypeStruct((8, 32, SEQ), F32),
        ),
        compiler_params=params(),
        name="qkv_sum",
    )(parts)


def attend_kernel(len_ref, q_ref, kv_ref, seg_ref, table_ref, out_ref):
    cos, sin = table_ref[0], table_ref[1]
    cos_t, sin_t = jnp.transpose(cos)[:, :SEQ], jnp.transpose(sin)[:, :SEQ]
    cos, sin = cos[:SEQ], sin[:SEQ]
    keys = jnp.concatenate([kv_ref[j, :16] for j in range(8)], axis=0)
    turned = jnp.concatenate([keys[64:], keys[:64]], axis=0)
    keys = (keys * cos_t + turned * sin_t).astype(BF)
    values = jnp.concatenate([kv_ref[j, 16:] for j in range(8)], axis=0).astype(BF)
    seg = jnp.concatenate([seg_ref[...].astype(F32), jnp.zeros((1, LANE - SEQ), F32)], axis=1)
    seg = jnp.broadcast_to(seg, (LANE, LANE))
    same = (seg == jnp.transpose(seg))[:SEQ, :SEQ]
    q_at = lax.broadcasted_iota(jnp.int32, (SEQ, SEQ), 0)
    k_at = lax.broadcasted_iota(jnp.int32, (SEQ, SEQ), 1)
    allowed = same & (k_at <= q_at) & (k_at < len_ref[0])
    allowed = allowed | (k_at == q_at)
    for head in range(2):
        query = q_ref[:, head * HEAD_DIM : (head + 1) * HEAD_DIM]
        query = (query * cos + pltpu.roll(query, 64, 1) * sin).astype(BF)
        scores = nn(query, keys) * (1.0 / math.sqrt(HEAD_DIM))
        scores = jnp.where(allowed, scores, F32(-1e30))
        expo = jnp.exp(scores - jnp.max(scores, axis=1, keepdims=True))
        soft = (expo / jnp.sum(expo, axis=1, keepdims=True)).astype(BF)
        attended = nt(soft, values).astype(BF)
        for j in range(ROWS):
            out_ref[j, :, head * HEAD_DIM : (head + 1) * HEAD_DIM] = attended


def attend(lengths, q, kv, segments):
    vmem = pl.BlockSpec(memory_space=pltpu.VMEM)
    return pl.pallas_call(
        attend_kernel,
        in_specs=[pl.BlockSpec(memory_space=pltpu.SMEM)] + [vmem] * 4,
        out_specs=vmem,
        out_shape=jax.ShapeDtypeStruct((ROWS, SEQ, 256), BF),
        compiler_params=params(),
        name="attend",
    )(lengths, q, kv, segments.reshape(1, SEQ), rope_table())


def proj_kernel(h_ref, x_ref, w_ref, out_ref):
    result = nn(x_ref[...], w_ref[...]).astype(out_ref.dtype)
    for j in range(out_ref.shape[0]):
        out_ref[j] = result[:, j * LANE : (j + 1) * LANE]


def proj_half(h, x, w, dtype):
    depth = x.shape[1]
    steps = 2
    wide = 2048 // steps
    return pl.pallas_call(
        proj_kernel,
        grid_spec=pltpu.PrefetchScalarGridSpec(
            num_scalar_prefetch=1,
            grid=(steps,),
            in_specs=[
                pl.BlockSpec((HALF, depth), lambda i, h: (h[0], 0)),
                pl.BlockSpec((depth, wide), lambda i, h: (0, i)),
            ],
            out_specs=pl.BlockSpec((wide // LANE, HALF, LANE), lambda i, h: (i, 0, 0)),
        ),
        out_shape=jax.ShapeDtypeStruct((CHIPS, HALF, LANE), dtype),
        compiler_params=params(),
        cost_estimate=pl.CostEstimate(
            flops=2 * HALF * 2048 * depth, bytes_accessed=4 * 1024 * 1024, transcendentals=0
        ),
        name="proj_half",
    )(h, x, w)


def project_out(mine, theirs, x, w):
    given = proj_half(theirs, x, w, BF)
    got = swap(given)
    kept = proj_half(mine, x, w, F32)
    return over_chips((kept + got.astype(F32)).astype(BF))


def residual_kernel(base_ref, p_ref, out_ref, copies_ref):
    total = p_ref[0].astype(F32)
    for j in range(1, CHIPS):
        total = total + p_ref[j].astype(F32)
    result = (base_ref[0, :HALF].astype(F32) + total).astype(BF)
    out_ref[...] = result
    for j in range(CHIPS):
        copies_ref[j] = result


def residual_copies(base, parts):
    return pl.pallas_call(
        residual_kernel,
        out_shape=(
            jax.ShapeDtypeStruct((HALF, LANE), BF),
            jax.ShapeDtypeStruct((CHIPS, HALF, LANE), BF),
        ),
        compiler_params=params(),
        name="residual_copies",
    )(base, parts)


def final_kernel(h_ref, base_ref, p_ref, keep_ref, give_ref):
    total = p_ref[0].astype(F32)
    for j in range(1, CHIPS):
        total = total + p_ref[j].astype(F32)
    done = (base_ref[...].astype(F32) + total).astype(BF)
    first, second = done[:, :64], done[:, 64:]
    keep_ref[...] = jnp.where(h_ref[0] == 0, first, second)
    give_ref[...] = jnp.where(h_ref[0] == 0, second, first)


def final_sum(h, base, parts):
    vmem = pl.BlockSpec(memory_space=pltpu.VMEM)
    return pl.pallas_call(
        final_kernel,
        in_specs=[pl.BlockSpec(memory_space=pltpu.SMEM), vmem, vmem],
        out_specs=(vmem, vmem),
        out_shape=(jax.ShapeDtypeStruct((HALF, 64), BF),) * 2,
        compiler_params=params(),
        name="final_sum",
    )(h, base, parts)


def place_kernel(h_ref, keep_ref, got_ref, out_ref):
    keep, got = keep_ref[...], got_ref[...]
    out_ref[:, :HALF] = jnp.transpose(jnp.where(h_ref[0] == 0, keep, got))
    out_ref[:, HALF:] = jnp.transpose(jnp.where(h_ref[0] == 0, got, keep))


def place_halves(h, keep, got):
    vmem = pl.BlockSpec(memory_space=pltpu.VMEM)
    return pl.pallas_call(
        place_kernel,
        in_specs=[pl.BlockSpec(memory_space=pltpu.SMEM), vmem, vmem],
        out_specs=vmem,
        out_shape=jax.ShapeDtypeStruct((64, TOK), BF),
        compiler_params=params(),
        name="place_halves",
    )(h, keep, got).T


def cut_kernel(h_ref, other_ref, at_ref, t_ref, ga_ref, gf_ref, keep_ref, give_ref):
    row = lax.broadcasted_iota(jnp.int32, (16, 64), 0)
    ga, gf = ga_ref[...].astype(F32), gf_ref[...].astype(F32)
    gains = jnp.where(row == 0, ga, jnp.where(row == 1, gf, 0.0)).astype(BF)
    keep_ref[HALF:] = gains
    give_ref[HALF:] = gains
    first = jnp.transpose(t_ref[:, :HALF])
    second = jnp.transpose(t_ref[:, HALF:])
    keep_ref[:HALF] = jnp.where(h_ref[0] == 0, first, second)
    give_ref[:HALF] = jnp.where(h_ref[0] == 0, second, first)


def cut_tokens(h, other, at, tokens_t, norm_attn, norm_ffn):
    whole = lambda *shape: pl.BlockSpec(shape, lambda i: (0, 0))
    return pl.pallas_call(
        cut_kernel,
        grid=(1,),
        in_specs=[
            pl.BlockSpec(memory_space=pltpu.SMEM),
            pl.BlockSpec(memory_space=pltpu.SMEM),
            pl.BlockSpec(memory_space=pltpu.SMEM),
            whole(64, TOK),
            whole(1, 64),
            whole(1, 64),
        ],
        out_specs=(whole(HALF + 16, 64), whole(HALF + 16, 64)),
        out_shape=(jax.ShapeDtypeStruct((HALF + 16, 64), BF),) * 2,
        compiler_params=params(),
        name="cut_tokens",
    )(h, other, at, tokens_t, norm_attn.reshape(1, 64), norm_ffn.reshape(1, 64))


def join_kernel(h_ref, keep_ref, got_ref, copies_ref):
    keep, got = keep_ref[...], got_ref[...]
    mine_first = jnp.concatenate([keep, got], axis=1)
    mine_last = jnp.concatenate([got, keep], axis=1)
    base = jnp.where(h_ref[0] == 0, mine_first, mine_last)
    for j in range(CHIPS):
        copies_ref[j] = base


def join_copies(h, keep, got):
    vmem = pl.BlockSpec(memory_space=pltpu.VMEM)
    return pl.pallas_call(
        join_kernel,
        in_specs=[pl.BlockSpec(memory_space=pltpu.SMEM), vmem, vmem],
        out_specs=vmem,
        out_shape=jax.ShapeDtypeStruct((CHIPS, HALF + 16, LANE), BF),
        compiler_params=params(),
        name="join_copies",
    )(h, keep, got)


def gained_rows(x_ref, g_ref, xs):
    for j in range(CHIPS):
        gain = g_ref[j, 1:2].astype(F32)
        xs[:, j * LANE : (j + 1) * LANE] = (x_ref[j].astype(F32) * gain).astype(BF)


def gate_up_main_kernel(h_ref, x_ref, g_ref, wg_ref, wu_ref, *rest):
    out_ref, made_ref, xs = rest[-3:]
    step = pl.program_id(0)
    made_ref[0] = step

    @pl.when(step == 0)
    def _():
        gained_rows(x_ref, g_ref, xs)

    wide = wg_ref.shape[0]
    at = pl.multiple_of(step * wide, wide)
    out_ref[:, pl.ds(at, wide)] = nt(xs[...], wg_ref[...]).astype(BF)
    out_ref[:, pl.ds(MAIN + at, wide)] = nt(xs[...], wu_ref[...]).astype(BF)


def gate_up_main(h, x, gains, wg_t, wu_t, held=None):
    steps = 1
    wide = MAIN // steps
    in_specs = [
        pl.BlockSpec((CHIPS, HALF, LANE), lambda i, h: (0, 0, 0)),
        pl.BlockSpec((CHIPS, 16, LANE), lambda i, h: (0, 0, 0)),
        pl.BlockSpec((wide, 2048), lambda i, h: (i, 0)),
        pl.BlockSpec((wide, 2048), lambda i, h: (i, 0)),
    ]
    operands = [h, x, gains, wg_t, wu_t]
    aliases = {}
    if held is not None:
        in_specs.append(pl.BlockSpec(memory_space=pl.ANY))
        operands.append(held)
        aliases = {5: 0}
    return pl.pallas_call(
        gate_up_main_kernel,
        grid_spec=pltpu.PrefetchScalarGridSpec(
            num_scalar_prefetch=1,
            grid=(steps,),
            in_specs=in_specs,
            out_specs=(
                pl.BlockSpec((HALF, 2 * MAIN), lambda i, h: (h[0], 0)),
                pl.BlockSpec(memory_space=pltpu.SMEM),
            ),
            scratch_shapes=[pltpu.VMEM((HALF, 2048), BF)],
        ),
        out_shape=(
            jax.ShapeDtypeStruct((TOK, 2 * MAIN), BF),
            jax.ShapeDtypeStruct((1,), jnp.int32),
        ),
        input_output_aliases=aliases,
        compiler_params=params(24),
        cost_estimate=pl.CostEstimate(
            flops=4 * HALF * 2048 * MAIN,
            bytes_accessed=8 * 1024 * 1024,
            transcendentals=0,
        ),
        name="gate_up_main",
    )(*operands)


def gate_up_side_kernel(h_ref, own_ref, other_ref, g_ref, wg_ref, wu_ref, _, out_ref, xs):
    lane = lax.broadcasted_iota(jnp.int32, (HALF, SIDE // 2 - REST), 1)
    for x_ref, half in ((own_ref, h_ref[0]), (other_ref, 1 - h_ref[0])):
        gained_rows(x_ref, g_ref, xs)
        squares = None
        for j in range(CHIPS):
            wide = x_ref[j].astype(F32)
            squares = wide * wide if squares is None else squares + wide * wide
        high, low = split_two(jnp.sum(squares, axis=1, keepdims=True))
        extra = jnp.where(lane == 0, high, jnp.where(lane == 1, low, 0.0))
        rows = pl.ds(pl.multiple_of(half * HALF, HALF), HALF)
        gate = jnp.concatenate([nt(xs[...], wg_ref[...]), extra], axis=1)
        out_ref[rows, : SIDE // 2] = gate.astype(BF)
        up = jnp.concatenate([nt(xs[...], wu_ref[...]), jnp.zeros_like(extra)], axis=1)
        out_ref[rows, SIDE // 2 :] = up.astype(BF)


def gate_up_side(h, own, other, gains, wg_t, wu_t, made):
    x_spec = pl.BlockSpec((CHIPS, HALF, LANE), lambda i, h: (0, 0, 0))
    w_spec = pl.BlockSpec((pl.Element(REST), pl.Element(2048)), lambda i, h: (MAIN, 0))
    return pl.pallas_call(
        gate_up_side_kernel,
        grid_spec=pltpu.PrefetchScalarGridSpec(
            num_scalar_prefetch=1,
            grid=(1,),
            in_specs=[
                x_spec,
                x_spec,
                pl.BlockSpec((CHIPS, 16, LANE), lambda i, h: (0, 0, 0)),
                w_spec,
                w_spec,
                pl.BlockSpec(memory_space=pltpu.SMEM),
            ],
            out_specs=pl.BlockSpec((TOK, SIDE), lambda i, h: (0, 0)),
            scratch_shapes=[pltpu.VMEM((HALF, 2048), BF)],
        ),
        out_shape=jax.ShapeDtypeStruct((TOK, SIDE), BF),
        compiler_params=params(58),
        cost_estimate=pl.CostEstimate(
            flops=4 * TOK * 2048 * REST, bytes_accessed=6 * 1024 * 1024, transcendentals=0
        ),
        name="gate_up_side",
    )(h, own, other, gains, wg_t, wu_t, made)


def hidden_kernel(main_ref, side_ref, out_ref):
    side = side_ref[0].astype(F32)
    for j in range(1, ROWS):
        side = side + side_ref[j].astype(F32)
    squares = side[:, REST : REST + 1] + side[:, REST + 1 : REST + 2]
    inv = lax.rsqrt(squares / D + EPS)

    def gated(gate, up):
        gate, up = gate * inv, up * inv
        return (gate / (1.0 + jnp.exp(-gate)) * up).astype(BF)

    first = gated(main_ref[:, :MAIN].astype(F32), main_ref[:, MAIN:].astype(F32))
    second = gated(side[:, :REST], side[:, SIDE // 2 : SIDE // 2 + REST])
    out_ref[:, :MAIN] = first
    out_ref[:, MAIN:] = second


def hidden_row(main, side):
    return pl.pallas_call(
        hidden_kernel,
        out_shape=jax.ShapeDtypeStruct((SEQ, FFL), BF),
        compiler_params=params(),
        name="hidden_row",
    )(main, side)


def from_ahead(x, k):
    return lax.ppermute(x, "gx", [(i, (i - k) % ROWS) for i in range(ROWS)])


def order_kernel(at_ref, *refs):
    out_ref = refs[-1]
    for k, ref in enumerate(refs[:-1]):
        out_ref[lax.rem(at_ref[0] + k, ROWS)] = ref[...]


def all_rows(at, x):
    ahead = {0: x}
    for k in (1, 7, 3, 5):
        ahead[k] = from_ahead(x, k)
    ahead[2] = from_ahead(ahead[1], 1)
    ahead[6] = from_ahead(ahead[7], 7)
    ahead[4] = from_ahead(ahead[3], 1)
    vmem = pl.BlockSpec(memory_space=pltpu.VMEM)
    return pl.pallas_call(
        order_kernel,
        in_specs=[pl.BlockSpec(memory_space=pltpu.SMEM)] + [vmem] * ROWS,
        out_specs=vmem,
        out_shape=jax.ShapeDtypeStruct((ROWS,) + x.shape, x.dtype),
        compiler_params=params(),
        name="order_rows",
    )(at, *[ahead[k] for k in range(ROWS)])


def rope_table():
    inv_freq = np.power(
        np.float32(ROPE_BASE), -(np.arange(64, dtype=np.float32) * np.float32(2.0 / HEAD_DIM))
    ).astype(np.float32)
    angles = (np.arange(SEQ, dtype=np.float32)[:, None] * inv_freq[None, :]).astype(np.float64)
    cos, sin = np.cos(angles), np.sin(angles)
    table = np.zeros((2, LANE, LANE), np.float32)
    table[0, :SEQ] = np.concatenate([cos, cos], axis=1)
    table[1, :SEQ] = np.concatenate([-sin, sin], axis=1)
    return table


def per_device(
    tokens,
    norm_attn,
    w_query,
    w_key,
    w_value,
    w_out,
    norm_ffn,
    w_gate,
    w_up,
    w_down,
    lengths,
    segments,
):
    core, at = lax.axis_index("gy") % 2, jnp.reshape(lax.axis_index("gx"), (1,))
    mine, theirs = jnp.reshape(core, (1,)), jnp.reshape(1 - core, (1,))

    keep, give = cut_tokens(mine, theirs, at, tokens.T, norm_attn, norm_ffn)
    base = join_copies(mine, keep, swap(give))
    first = over_chips(base)
    other = swap(first)
    held, gains = qkv_half(mine, first, first, w_query, w_key.T, w_value.T)
    parts, _ = qkv_half(theirs, other, first, w_query, w_key.T, w_value.T, held)
    q, kv = qkv_sum(over_rows(parts))
    kv = lax.all_to_all(kv, "gy", 0, 0, axis_index_groups=KV_GROUPS, tiled=True)
    attended = over_rows(attend(lengths, q, kv, segments)).reshape(TOK, 256)
    residual, copies = residual_copies(base, project_out(mine, theirs, attended, w_out))

    own = over_chips(copies)
    other = swap(own)
    weights = (w_gate.T, w_up.T)
    held, _ = gate_up_main(mine, own, gains, *weights)
    main, made = gate_up_main(theirs, other, gains, *weights, held)
    side = gate_up_side(mine, own, other, gains, *weights, made)
    main = lax.psum_scatter(main, "gx", scatter_dimension=0, tiled=True)
    side = over_rows(side.reshape(ROWS, SEQ, SIDE))
    hidden = all_rows(at, hidden_row(main, side)).reshape(TOK, FFL)
    keep, give = final_sum(mine, residual, project_out(mine, theirs, hidden, w_down))
    return place_halves(mine, keep, swap(give))


def solution(mesh):
    in_specs = (
        P(None, ("gx", "gy")),
        P(("gx", "gy")),
        P("gx", "gy"),
        P("gx", "gy"),
        P("gx", "gy"),
        P("gy", "gx"),
        P(("gx", "gy")),
        P("gx", "gy"),
        P("gx", "gy"),
        P("gy", "gx"),
        P("gx"),
        P("gx"),
    )
    out_specs = P(None, ("gx", "gy"))
    return jax.shard_map(
        per_device, mesh=mesh, in_specs=in_specs, out_specs=out_specs, check_vma=False
    )
```

```python
import functools
import math

import jax
import jax.numpy as jnp
import numpy as np
from jax import lax
from jax.experimental import pallas as pl
from jax.experimental.pallas import tpu as pltpu
from jax.sharding import PartitionSpec as P

D = 16384
HEADS = 64
KV_HEADS = 4
HEAD_DIM = 128
SEQ = 96
EPS = 1e-05
ROPE_BASE = 500000.0

BF = jnp.bfloat16
F32 = jnp.float32

TOK = 768
HALF = 384
CHIPS = 16
LANE = 128
ROWS = 8
KSTEP = 4
FFL = 832
MAIN = 768
REST = FFL - MAIN
SIDE = 256
CHIP_GROUPS = [[2 * i + c for i in range(CHIPS)] for c in range(2)]
KV_GROUPS = [list(range(8 * i, 8 * i + 8)) for i in range(4)]


def swap(x):
    return lax.ppermute(x, "gy", [(i, i ^ 1) for i in range(32)])


def over_chips(x):
    return lax.all_to_all(x, "gy", 0, 0, axis_index_groups=CHIP_GROUPS, tiled=True)


def over_ring(x, k, stage):
    pairs = []
    for i in range(32):
        y, across, core = i // 8, i // 2 % 4, i % 2
        if (core == 0) == (stage == 0):
            across = (across + k) % 4
        else:
            y = (y + k) % 4
        pairs.append((y * 8 + across * 2 + core, i))
    return lax.ppermute(x, "gy", pairs)


def stack_kernel(*refs):
    for j, ref in enumerate(refs[:-1]):
        refs[-1][j] = ref[...]


def order_chips_kernel(g_ref, *refs):
    out_ref = refs[-1]
    core = lax.rem(g_ref[0], 2)
    across, y = lax.rem(lax.div(g_ref[0], 2), 4), lax.div(g_ref[0], 8)
    for a in range(4):
        for b in range(4):
            here_y = lax.rem(y + jnp.where(core == 0, a, b), 4)
            here_x = lax.rem(across + jnp.where(core == 0, b, a), 4)
            out_ref[here_y * 4 + here_x] = refs[a][b]


def from_chips(g, x):
    vmem = pl.BlockSpec(memory_space=pltpu.VMEM)
    line = pl.pallas_call(
        stack_kernel,
        in_specs=[vmem] * 4,
        out_specs=vmem,
        out_shape=jax.ShapeDtypeStruct((4,) + x.shape, x.dtype),
        compiler_params=params(),
        name="stack_line",
    )(x, *[over_ring(x, k, 0) for k in (1, 2, 3)])
    return pl.pallas_call(
        order_chips_kernel,
        in_specs=[pl.BlockSpec(memory_space=pltpu.SMEM)] + [vmem] * 4,
        out_specs=vmem,
        out_shape=jax.ShapeDtypeStruct((CHIPS,) + x.shape, x.dtype),
        compiler_params=params(),
        name="order_chips",
    )(g, line, *[over_ring(line, k, 1) for k in (1, 2, 3)])


def over_rows(x):
    return lax.all_to_all(x, "gx", 0, 0, tiled=True)


def params(mib=16):
    return pltpu.CompilerParams(vmem_limit_bytes=mib * 1024 * 1024)


def nt(a, b):
    return lax.dot_general(a, b, (((1,), (1,)), ((), ())), preferred_element_type=F32)


def nn(a, b):
    return jnp.dot(a, b, preferred_element_type=F32)


def fold_squares(wide):
    total = None
    for j in range(wide.shape[1] // LANE):
        part = wide[:, j * LANE : (j + 1) * LANE]
        total = part * part if total is None else total + part * part
    return total


def split_two(total):
    high = total.astype(BF).astype(F32)
    return high, total - high


def gained_block(x_ref, g_ref, row):
    chips = range(x_ref.shape[0])
    wide = jnp.concatenate([x_ref[j, :HALF] for j in chips], axis=1).astype(F32)
    gain = jnp.concatenate([g_ref[j, row : row + 1] for j in chips], axis=1).astype(F32)
    return wide, (wide * gain).astype(BF)


def qkv_kernel(h_ref, x_ref, g_ref, wq_ref, wk_ref, wv_ref, *rest):
    out_ref, gains_ref, acc_q, acc_kv, acc_sq = rest[-5:]
    k = pl.program_id(0)
    gains_ref[...] = g_ref[...]

    @pl.when(k == 0)
    def _():
        acc_q[...] = jnp.zeros_like(acc_q)
        acc_kv[...] = jnp.zeros_like(acc_kv)
        acc_sq[...] = jnp.zeros_like(acc_sq)

    wide, gained = gained_block(x_ref, g_ref, 0)
    acc_sq[...] += fold_squares(wide)
    acc_q[...] += nn(gained, wq_ref[...])
    acc_kv[...] += nt(jnp.concatenate([wk_ref[...], wv_ref[...]], axis=0), gained)

    @pl.when(k == pl.num_programs(0) - 1)
    def _():
        high, low = split_two(jnp.sum(jnp.transpose(acc_sq[...]), axis=0, keepdims=True))
        def squeezed(row):
            cuts = [row[:, j * 32 : (j + 1) * 32] for j in range(SEQ // 32)]
            return jnp.concatenate(cuts + [jnp.zeros((16 - SEQ // 32, 32), F32)], axis=0)

        for r in range(HALF // SEQ):
            here = slice(r * SEQ, (r + 1) * SEQ)
            kv = acc_kv[:, here]
            out_ref[r, :SEQ] = acc_q[here].astype(BF)
            below = [kv[:16], squeezed(high[:, here]), kv[16:], squeezed(low[:, here])]
            out_ref[r, SEQ:] = jnp.concatenate(below, axis=1).astype(BF)


def qkv_half(h, x, gains, wq, wk_t, wv_t, held=None):
    depth = 2048 // KSTEP
    chips = CHIPS // KSTEP
    in_specs = [
        pl.BlockSpec((chips, HALF, LANE), lambda k, h: (k, 0, 0)),
        pl.BlockSpec((chips, 16, LANE), lambda k, h: (k, HALF // 16, 0)),
        pl.BlockSpec((depth, 256), lambda k, h: (k, 0)),
        pl.BlockSpec((16, depth), lambda k, h: (0, k)),
        pl.BlockSpec((16, depth), lambda k, h: (0, k)),
    ]
    operands = [h, x, gains, wq, wk_t, wv_t]
    aliases = {}
    if held is not None:
        in_specs.append(pl.BlockSpec(memory_space=pl.ANY))
        operands.append(held)
        aliases = {6: 0}
    return pl.pallas_call(
        qkv_kernel,
        grid_spec=pltpu.PrefetchScalarGridSpec(
            num_scalar_prefetch=1,
            grid=(KSTEP,),
            in_specs=in_specs,
            out_specs=(
                pl.BlockSpec((HALF // SEQ, SEQ + 16, 256), lambda k, h: (h[0], 0, 0)),
                pl.BlockSpec((chips, 16, LANE), lambda k, h: (k, 0, 0)),
            ),
            scratch_shapes=[
                pltpu.VMEM((HALF, 256), F32),
                pltpu.VMEM((32, HALF), F32),
                pltpu.VMEM((HALF, LANE), F32),
            ],
        ),
        out_shape=(
            jax.ShapeDtypeStruct((ROWS, SEQ + 16, 256), BF),
            jax.ShapeDtypeStruct((CHIPS, 16, LANE), BF),
        ),
        input_output_aliases=aliases,
        compiler_params=params(),
        cost_estimate=pl.CostEstimate(
            flops=2 * HALF * 2048 * 384, bytes_accessed=4 * 1024 * 1024, transcendentals=0
        ),
        name="qkv_half",
    )(*operands)


def qkv_sum_kernel(p_ref, q_ref, kv_ref):
    total = p_ref[0].astype(F32)
    for j in range(1, ROWS):
        total = total + p_ref[j].astype(F32)
    extra = total[SEQ:, SEQ:LANE] + total[SEQ:, LANE + SEQ :]
    squares = jnp.concatenate([extra[j : j + 1] for j in range(3)] + [extra[3:4]], axis=1)
    inv = lax.rsqrt(squares / D + EPS)
    down = jnp.transpose(jnp.broadcast_to(inv, (LANE, LANE)))[:SEQ]
    q_ref[...] = total[:SEQ] * jnp.concatenate([down, down], axis=1)
    kv = jnp.concatenate([total[96:112, :SEQ], total[96:112, LANE : LANE + SEQ]], axis=0)
    kv = kv * inv[:, :SEQ]
    for j in range(8):
        kv_ref[j] = kv


def qkv_sum(parts):
    return pl.pallas_call(
        qkv_sum_kernel,
        out_shape=(
            jax.ShapeDtypeStruct((SEQ, 256), F32),
            jax.ShapeDtypeStruct((8, 32, SEQ), F32),
        ),
        compiler_params=params(),
        name="qkv_sum",
    )(parts)


def attend_kernel(len_ref, q_ref, kv_ref, seg_ref, table_ref, out_ref):
    cos, sin = table_ref[0], table_ref[1]
    cos_t, sin_t = jnp.transpose(cos)[:, :SEQ], jnp.transpose(sin)[:, :SEQ]
    cos, sin = cos[:SEQ], sin[:SEQ]
    keys = jnp.concatenate([kv_ref[j, :16] for j in range(8)], axis=0)
    turned = jnp.concatenate([keys[64:], keys[:64]], axis=0)
    keys = (keys * cos_t + turned * sin_t).astype(BF)
    values = jnp.concatenate([kv_ref[j, 16:] for j in range(8)], axis=0).astype(BF)
    seg = jnp.concatenate([seg_ref[...].astype(F32), jnp.zeros((1, LANE - SEQ), F32)], axis=1)
    seg = jnp.broadcast_to(seg, (LANE, LANE))
    same = (seg == jnp.transpose(seg))[:SEQ, :SEQ]
    q_at = lax.broadcasted_iota(jnp.int32, (SEQ, SEQ), 0)
    k_at = lax.broadcasted_iota(jnp.int32, (SEQ, SEQ), 1)
    allowed = same & (k_at <= q_at) & (k_at < len_ref[0])
    allowed = allowed | (k_at == q_at)
    for head in range(2):
        query = q_ref[:, head * HEAD_DIM : (head + 1) * HEAD_DIM]
        query = (query * cos + pltpu.roll(query, 64, 1) * sin).astype(BF)
        scores = nn(query, keys) * (1.0 / math.sqrt(HEAD_DIM))
        scores = jnp.where(allowed, scores, F32(-1e30))
        expo = jnp.exp(scores - jnp.max(scores, axis=1, keepdims=True))
        soft = (expo / jnp.sum(expo, axis=1, keepdims=True)).astype(BF)
        attended = nt(soft, values).astype(BF)
        for j in range(ROWS):
            out_ref[j, :, head * HEAD_DIM : (head + 1) * HEAD_DIM] = attended


def attend(lengths, q, kv, segments):
    vmem = pl.BlockSpec(memory_space=pltpu.VMEM)
    return pl.pallas_call(
        attend_kernel,
        in_specs=[pl.BlockSpec(memory_space=pltpu.SMEM)] + [vmem] * 4,
        out_specs=vmem,
        out_shape=jax.ShapeDtypeStruct((ROWS, SEQ, 256), BF),
        compiler_params=params(),
        name="attend",
    )(lengths, q, kv, segments.reshape(1, SEQ), rope_table())


def proj_kernel(h_ref, x_ref, w_ref, out_ref):
    result = nn(x_ref[...], w_ref[...]).astype(out_ref.dtype)
    for j in range(out_ref.shape[0]):
        out_ref[j] = result[:, j * LANE : (j + 1) * LANE]


def proj_half(h, x, w, dtype):
    depth = x.shape[1]
    steps = 2
    wide = 2048 // steps
    return pl.pallas_call(
        proj_kernel,
        grid_spec=pltpu.PrefetchScalarGridSpec(
            num_scalar_prefetch=1,
            grid=(steps,),
            in_specs=[
                pl.BlockSpec((HALF, depth), lambda i, h: (h[0], 0)),
                pl.BlockSpec((depth, wide), lambda i, h: (0, i)),
            ],
            out_specs=pl.BlockSpec((wide // LANE, HALF, LANE), lambda i, h: (i, 0, 0)),
        ),
        out_shape=jax.ShapeDtypeStruct((CHIPS, HALF, LANE), dtype),
        compiler_params=params(),
        cost_estimate=pl.CostEstimate(
            flops=2 * HALF * 2048 * depth, bytes_accessed=4 * 1024 * 1024, transcendentals=0
        ),
        name="proj_half",
    )(h, x, w)


def project_out(mine, theirs, x, w):
    given = proj_half(theirs, x, w, BF)
    got = swap(given)
    kept = proj_half(mine, x, w, F32)
    return over_chips((kept + got.astype(F32)).astype(BF))


def residual_kernel(base_ref, p_ref, out_ref):
    total = p_ref[0].astype(F32)
    for j in range(1, CHIPS):
        total = total + p_ref[j].astype(F32)
    out_ref[...] = (base_ref[:HALF].astype(F32) + total).astype(BF)


def residual_sum(base, parts):
    return pl.pallas_call(
        residual_kernel,
        out_shape=jax.ShapeDtypeStruct((HALF, LANE), BF),
        compiler_params=params(),
        name="residual_sum",
    )(base, parts)


def final_kernel(h_ref, base_ref, p_ref, keep_ref, give_ref):
    total = p_ref[0].astype(F32)
    for j in range(1, CHIPS):
        total = total + p_ref[j].astype(F32)
    done = (base_ref[...].astype(F32) + total).astype(BF)
    first, second = done[:, :64], done[:, 64:]
    keep_ref[...] = jnp.where(h_ref[0] == 0, first, second)
    give_ref[...] = jnp.where(h_ref[0] == 0, second, first)


def final_sum(h, base, parts):
    vmem = pl.BlockSpec(memory_space=pltpu.VMEM)
    return pl.pallas_call(
        final_kernel,
        in_specs=[pl.BlockSpec(memory_space=pltpu.SMEM), vmem, vmem],
        out_specs=(vmem, vmem),
        out_shape=(jax.ShapeDtypeStruct((HALF, 64), BF),) * 2,
        compiler_params=params(),
        name="final_sum",
    )(h, base, parts)


def place_kernel(h_ref, keep_ref, got_ref, out_ref):
    keep, got = keep_ref[...], got_ref[...]
    out_ref[:, :HALF] = jnp.transpose(jnp.where(h_ref[0] == 0, keep, got))
    out_ref[:, HALF:] = jnp.transpose(jnp.where(h_ref[0] == 0, got, keep))


def place_halves(h, keep, got):
    vmem = pl.BlockSpec(memory_space=pltpu.VMEM)
    return pl.pallas_call(
        place_kernel,
        in_specs=[pl.BlockSpec(memory_space=pltpu.SMEM), vmem, vmem],
        out_specs=vmem,
        out_shape=jax.ShapeDtypeStruct((64, TOK), BF),
        compiler_params=params(),
        name="place_halves",
    )(h, keep, got).T


def cut_kernel(h_ref, other_ref, at_ref, place_ref, t_ref, ga_ref, gf_ref, keep_ref, give_ref):
    row = lax.broadcasted_iota(jnp.int32, (16, 64), 0)
    ga, gf = ga_ref[...].astype(F32), gf_ref[...].astype(F32)
    gains = jnp.where(row == 0, ga, jnp.where(row == 1, gf, 0.0)).astype(BF)
    keep_ref[HALF:] = gains
    give_ref[HALF:] = gains
    first = jnp.transpose(t_ref[:, :HALF])
    second = jnp.transpose(t_ref[:, HALF:])
    keep_ref[:HALF] = jnp.where(h_ref[0] == 0, first, second)
    give_ref[:HALF] = jnp.where(h_ref[0] == 0, second, first)


def cut_tokens(h, other, at, place, tokens_t, norm_attn, norm_ffn):
    whole = lambda *shape: pl.BlockSpec(shape, lambda i: (0, 0))
    return pl.pallas_call(
        cut_kernel,
        grid=(1,),
        in_specs=[
            pl.BlockSpec(memory_space=pltpu.SMEM),
            pl.BlockSpec(memory_space=pltpu.SMEM),
            pl.BlockSpec(memory_space=pltpu.SMEM),
            pl.BlockSpec(memory_space=pltpu.SMEM),
            whole(64, TOK),
            whole(1, 64),
            whole(1, 64),
        ],
        out_specs=(whole(HALF + 16, 64), whole(HALF + 16, 64)),
        out_shape=(jax.ShapeDtypeStruct((HALF + 16, 64), BF),) * 2,
        compiler_params=params(),
        name="cut_tokens",
    )(h, other, at, place, tokens_t, norm_attn.reshape(1, 64), norm_ffn.reshape(1, 64))


def join_kernel(h_ref, keep_ref, got_ref, out_ref):
    keep, got = keep_ref[...], got_ref[...]
    mine_first = jnp.concatenate([keep, got], axis=1)
    mine_last = jnp.concatenate([got, keep], axis=1)
    out_ref[...] = jnp.where(h_ref[0] == 0, mine_first, mine_last)


def join_cores(h, keep, got):
    vmem = pl.BlockSpec(memory_space=pltpu.VMEM)
    return pl.pallas_call(
        join_kernel,
        in_specs=[pl.BlockSpec(memory_space=pltpu.SMEM), vmem, vmem],
        out_specs=vmem,
        out_shape=jax.ShapeDtypeStruct((HALF + 16, LANE), BF),
        compiler_params=params(),
        name="join_cores",
    )(h, keep, got)


def gained_rows(x_ref, g_ref, xs):
    for j in range(CHIPS):
        gain = g_ref[j, 1:2].astype(F32)
        xs[:, j * LANE : (j + 1) * LANE] = (x_ref[j].astype(F32) * gain).astype(BF)


def gate_up_main_kernel(h_ref, x_ref, g_ref, wg_ref, wu_ref, *rest):
    out_ref, made_ref, xs = rest[-3:]
    step = pl.program_id(0)
    made_ref[0] = step

    @pl.when(step == 0)
    def _():
        gained_rows(x_ref, g_ref, xs)

    wide = wg_ref.shape[0]
    at = pl.multiple_of(step * wide, wide)
    out_ref[:, pl.ds(at, wide)] = nt(xs[...], wg_ref[...]).astype(BF)
    out_ref[:, pl.ds(MAIN + at, wide)] = nt(xs[...], wu_ref[...]).astype(BF)


def gate_up_main(h, x, gains, wg_t, wu_t, held=None):
    steps = 1
    wide = MAIN // steps
    in_specs = [
        pl.BlockSpec((CHIPS, HALF, LANE), lambda i, h: (0, 0, 0)),
        pl.BlockSpec((CHIPS, 16, LANE), lambda i, h: (0, 0, 0)),
        pl.BlockSpec((wide, 2048), lambda i, h: (i, 0)),
        pl.BlockSpec((wide, 2048), lambda i, h: (i, 0)),
    ]
    operands = [h, x, gains, wg_t, wu_t]
    aliases = {}
    if held is not None:
        in_specs.append(pl.BlockSpec(memory_space=pl.ANY))
        operands.append(held)
        aliases = {5: 0}
    return pl.pallas_call(
        gate_up_main_kernel,
        grid_spec=pltpu.PrefetchScalarGridSpec(
            num_scalar_prefetch=1,
            grid=(steps,),
            in_specs=in_specs,
            out_specs=(
                pl.BlockSpec((HALF, 2 * MAIN), lambda i, h: (h[0], 0)),
                pl.BlockSpec(memory_space=pltpu.SMEM),
            ),
            scratch_shapes=[pltpu.VMEM((HALF, 2048), BF)],
        ),
        out_shape=(
            jax.ShapeDtypeStruct((TOK, 2 * MAIN), BF),
            jax.ShapeDtypeStruct((1,), jnp.int32),
        ),
        input_output_aliases=aliases,
        compiler_params=params(24),
        cost_estimate=pl.CostEstimate(
            flops=4 * HALF * 2048 * MAIN,
            bytes_accessed=8 * 1024 * 1024,
            transcendentals=0,
        ),
        name="gate_up_main",
    )(*operands)


def gate_up_side_kernel(h_ref, own_ref, other_ref, g_ref, wg_ref, wu_ref, _, out_ref, xs):
    lane = lax.broadcasted_iota(jnp.int32, (HALF, SIDE // 2 - REST), 1)
    for x_ref, half in ((own_ref, h_ref[0]), (other_ref, 1 - h_ref[0])):
        gained_rows(x_ref, g_ref, xs)
        squares = None
        for j in range(CHIPS):
            wide = x_ref[j].astype(F32)
            squares = wide * wide if squares is None else squares + wide * wide
        high, low = split_two(jnp.sum(squares, axis=1, keepdims=True))
        extra = jnp.where(lane == 0, high, jnp.where(lane == 1, low, 0.0))
        rows = pl.ds(pl.multiple_of(half * HALF, HALF), HALF)
        gate = jnp.concatenate([nt(xs[...], wg_ref[...]), extra], axis=1)
        out_ref[rows, : SIDE // 2] = gate.astype(BF)
        up = jnp.concatenate([nt(xs[...], wu_ref[...]), jnp.zeros_like(extra)], axis=1)
        out_ref[rows, SIDE // 2 :] = up.astype(BF)


def gate_up_side(h, own, other, gains, wg_t, wu_t, made):
    x_spec = pl.BlockSpec((CHIPS, HALF, LANE), lambda i, h: (0, 0, 0))
    w_spec = pl.BlockSpec((pl.Element(REST), pl.Element(2048)), lambda i, h: (MAIN, 0))
    return pl.pallas_call(
        gate_up_side_kernel,
        grid_spec=pltpu.PrefetchScalarGridSpec(
            num_scalar_prefetch=1,
            grid=(1,),
            in_specs=[
                x_spec,
                x_spec,
                pl.BlockSpec((CHIPS, 16, LANE), lambda i, h: (0, 0, 0)),
                w_spec,
                w_spec,
                pl.BlockSpec(memory_space=pltpu.SMEM),
            ],
            out_specs=pl.BlockSpec((TOK, SIDE), lambda i, h: (0, 0)),
            scratch_shapes=[pltpu.VMEM((HALF, 2048), BF)],
        ),
        out_shape=jax.ShapeDtypeStruct((TOK, SIDE), BF),
        compiler_params=params(58),
        cost_estimate=pl.CostEstimate(
            flops=4 * TOK * 2048 * REST, bytes_accessed=6 * 1024 * 1024, transcendentals=0
        ),
        name="gate_up_side",
    )(h, own, other, gains, wg_t, wu_t, made)


def hidden_kernel(main_ref, side_ref, out_ref):
    side = side_ref[0].astype(F32)
    for j in range(1, ROWS):
        side = side + side_ref[j].astype(F32)
    squares = side[:, REST : REST + 1] + side[:, REST + 1 : REST + 2]
    inv = lax.rsqrt(squares / D + EPS)

    def gated(gate, up):
        gate, up = gate * inv, up * inv
        return (gate / (1.0 + jnp.exp(-gate)) * up).astype(BF)

    first = gated(main_ref[:, :MAIN].astype(F32), main_ref[:, MAIN:].astype(F32))
    second = gated(side[:, :REST], side[:, SIDE // 2 : SIDE // 2 + REST])
    out_ref[:, :MAIN] = first
    out_ref[:, MAIN:] = second


def hidden_row(main, side):
    return pl.pallas_call(
        hidden_kernel,
        out_shape=jax.ShapeDtypeStruct((SEQ, FFL), BF),
        compiler_params=params(),
        name="hidden_row",
    )(main, side)


def from_ahead(x, k):
    return lax.ppermute(x, "gx", [(i, (i - k) % ROWS) for i in range(ROWS)])


def order_kernel(at_ref, *refs):
    out_ref = refs[-1]
    for k, ref in enumerate(refs[:-1]):
        out_ref[lax.rem(at_ref[0] + k, ROWS)] = ref[...]


def all_rows(at, x):
    ahead = {0: x}
    for k in (1, 7, 3, 5):
        ahead[k] = from_ahead(x, k)
    ahead[2] = from_ahead(ahead[1], 1)
    ahead[6] = from_ahead(ahead[7], 7)
    ahead[4] = from_ahead(ahead[3], 1)
    vmem = pl.BlockSpec(memory_space=pltpu.VMEM)
    return pl.pallas_call(
        order_kernel,
        in_specs=[pl.BlockSpec(memory_space=pltpu.SMEM)] + [vmem] * ROWS,
        out_specs=vmem,
        out_shape=jax.ShapeDtypeStruct((ROWS,) + x.shape, x.dtype),
        compiler_params=params(),
        name="order_rows",
    )(at, *[ahead[k] for k in range(ROWS)])


def rope_table():
    inv_freq = np.power(
        np.float32(ROPE_BASE), -(np.arange(64, dtype=np.float32) * np.float32(2.0 / HEAD_DIM))
    ).astype(np.float32)
    angles = (np.arange(SEQ, dtype=np.float32)[:, None] * inv_freq[None, :]).astype(np.float64)
    cos, sin = np.cos(angles), np.sin(angles)
    table = np.zeros((2, LANE, LANE), np.float32)
    table[0, :SEQ] = np.concatenate([cos, cos], axis=1)
    table[1, :SEQ] = np.concatenate([-sin, sin], axis=1)
    return table


def per_device(
    tokens,
    norm_attn,
    w_query,
    w_key,
    w_value,
    w_out,
    norm_ffn,
    w_gate,
    w_up,
    w_down,
    lengths,
    segments,
):
    core, at = lax.axis_index("gy") % 2, jnp.reshape(lax.axis_index("gx"), (1,))
    mine, theirs = jnp.reshape(core, (1,)), jnp.reshape(1 - core, (1,))
    place = jnp.reshape(lax.axis_index("gy"), (1,))

    keep, give = cut_tokens(mine, theirs, at, place, tokens.T, norm_attn, norm_ffn)
    base = join_cores(mine, keep, swap(give))
    first = from_chips(place, base)
    other = swap(first)
    held, gains = qkv_half(mine, first, first, w_query, w_key.T, w_value.T)
    parts, _ = qkv_half(theirs, other, first, w_query, w_key.T, w_value.T, held)
    q, kv = qkv_sum(over_rows(parts))
    kv = lax.all_to_all(kv, "gy", 0, 0, axis_index_groups=KV_GROUPS, tiled=True)
    attended = over_rows(attend(lengths, q, kv, segments)).reshape(TOK, 256)
    residual = residual_sum(base, project_out(mine, theirs, attended, w_out))

    own = from_chips(place, residual)
    other = swap(own)
    weights = (w_gate.T, w_up.T)
    held, _ = gate_up_main(mine, own, gains, *weights)
    main, made = gate_up_main(theirs, other, gains, *weights, held)
    side = gate_up_side(mine, own, other, gains, *weights, made)
    main = lax.psum_scatter(main, "gx", scatter_dimension=0, tiled=True)
    side = over_rows(side.reshape(ROWS, SEQ, SIDE))
    hidden = all_rows(at, hidden_row(main, side)).reshape(TOK, FFL)
    keep, give = final_sum(mine, residual, project_out(mine, theirs, hidden, w_down))
    return place_halves(mine, keep, swap(give))


def solution(mesh):
    in_specs = (
        P(None, ("gx", "gy")),
        P(("gx", "gy")),
        P("gx", "gy"),
        P("gx", "gy"),
        P("gx", "gy"),
        P("gy", "gx"),
        P(("gx", "gy")),
        P("gx", "gy"),
        P("gx", "gy"),
        P("gy", "gx"),
        P("gx"),
        P("gx"),
    )
    out_specs = P(None, ("gx", "gy"))
    return jax.shard_map(
        per_device, mesh=mesh, in_specs=in_specs, out_specs=out_specs, check_vma=False
    )
```

```python
import functools
import math

import jax
import jax.numpy as jnp
import numpy as np
from jax import lax
from jax.experimental import pallas as pl
from jax.experimental.pallas import tpu as pltpu
from jax.sharding import PartitionSpec as P

D = 16384
HEADS = 64
KV_HEADS = 4
HEAD_DIM = 128
SEQ = 96
EPS = 1e-05
ROPE_BASE = 500000.0

BF = jnp.bfloat16
F32 = jnp.float32

TOK = 768
HALF = 384
CHIPS = 16
LANE = 128
ROWS = 8
KSTEP = 4
FFL = 832
MAIN = 768
REST = FFL - MAIN
SIDE = 256
CHIP_GROUPS = [[2 * i + c for i in range(CHIPS)] for c in range(2)]
KV_GROUPS = [list(range(8 * i, 8 * i + 8)) for i in range(4)]


def swap(x):
    return lax.ppermute(x, "gy", [(i, i ^ 1) for i in range(32)])


def over_chips(x):
    return lax.all_to_all(x, "gy", 0, 0, axis_index_groups=CHIP_GROUPS, tiled=True)


def over_ring(x, k, stage):
    pairs = []
    for i in range(32):
        y, across, core = i // 8, i // 2 % 4, i % 2
        if (core == 0) == (stage == 0):
            across = (across + k) % 4
        else:
            y = (y + k) % 4
        pairs.append((y * 8 + across * 2 + core, i))
    return lax.ppermute(x, "gy", pairs)


def stack_kernel(*refs):
    for j, ref in enumerate(refs[:-1]):
        refs[-1][j] = ref[...]


def order_chips_kernel(of_other, g_ref, *refs):
    out_ref = refs[-1]
    core = lax.rem(g_ref[0], 2)
    core = 1 - core if of_other else core
    across, y = lax.rem(lax.div(g_ref[0], 2), 4), lax.div(g_ref[0], 8)
    for a in range(4):
        for b in range(4):
            here_y = lax.rem(y + jnp.where(core == 0, a, b), 4)
            here_x = lax.rem(across + jnp.where(core == 0, b, a), 4)
            out_ref[here_y * 4 + here_x] = refs[a][b]


def from_chips(g, x):
    vmem = pl.BlockSpec(memory_space=pltpu.VMEM)
    line = pl.pallas_call(
        stack_kernel,
        in_specs=[vmem] * 4,
        out_specs=vmem,
        out_shape=jax.ShapeDtypeStruct((4,) + x.shape, x.dtype),
        compiler_params=params(),
        name="stack_line",
    )(x, *[over_ring(x, k, 0) for k in (1, 2, 3)])
    pieces = [line] + [over_ring(line, k, 1) for k in (1, 2, 3)]

    def ordered(of_other, pieces):
        return pl.pallas_call(
            functools.partial(order_chips_kernel, of_other),
            in_specs=[pl.BlockSpec(memory_space=pltpu.SMEM)] + [vmem] * 4,
            out_specs=vmem,
            out_shape=jax.ShapeDtypeStruct((CHIPS,) + x.shape, x.dtype),
            compiler_params=params(),
            name="order_chips",
        )(g, *pieces)

    return ordered(False, pieces), ordered(True, [swap(piece) for piece in pieces])


def over_rows(x):
    return lax.all_to_all(x, "gx", 0, 0, tiled=True)


def params(mib=16):
    return pltpu.CompilerParams(vmem_limit_bytes=mib * 1024 * 1024)


def nt(a, b):
    return lax.dot_general(a, b, (((1,), (1,)), ((), ())), preferred_element_type=F32)


def nn(a, b):
    return jnp.dot(a, b, preferred_element_type=F32)


def fold_squares(wide):
    total = None
    for j in range(wide.shape[1] // LANE):
        part = wide[:, j * LANE : (j + 1) * LANE]
        total = part * part if total is None else total + part * part
    return total


def split_two(total):
    high = total.astype(BF).astype(F32)
    return high, total - high


def gained_block(x_ref, g_ref, row):
    chips = range(x_ref.shape[0])
    wide = jnp.concatenate([x_ref[j, :HALF] for j in chips], axis=1).astype(F32)
    gain = jnp.concatenate([g_ref[j, row : row + 1] for j in chips], axis=1).astype(F32)
    return wide, (wide * gain).astype(BF)


def qkv_kernel(h_ref, x_ref, g_ref, wq_ref, wk_ref, wv_ref, *rest):
    out_ref, gains_ref, acc_q, acc_kv, acc_sq = rest[-5:]
    k = pl.program_id(0)
    gains_ref[...] = g_ref[...]

    @pl.when(k == 0)
    def _():
        acc_q[...] = jnp.zeros_like(acc_q)
        acc_kv[...] = jnp.zeros_like(acc_kv)
        acc_sq[...] = jnp.zeros_like(acc_sq)

    wide, gained = gained_block(x_ref, g_ref, 0)
    acc_sq[...] += fold_squares(wide)
    acc_q[...] += nn(gained, wq_ref[...])
    acc_kv[...] += nt(jnp.concatenate([wk_ref[...], wv_ref[...]], axis=0), gained)

    @pl.when(k == pl.num_programs(0) - 1)
    def _():
        high, low = split_two(jnp.sum(jnp.transpose(acc_sq[...]), axis=0, keepdims=True))
        def squeezed(row):
            cuts = [row[:, j * 32 : (j + 1) * 32] for j in range(SEQ // 32)]
            return jnp.concatenate(cuts + [jnp.zeros((16 - SEQ // 32, 32), F32)], axis=0)

        for r in range(HALF // SEQ):
            here = slice(r * SEQ, (r + 1) * SEQ)
            kv = acc_kv[:, here]
            out_ref[r, :SEQ] = acc_q[here].astype(BF)
            below = [kv[:16], squeezed(high[:, here]), kv[16:], squeezed(low[:, here])]
            out_ref[r, SEQ:] = jnp.concatenate(below, axis=1).astype(BF)


def qkv_half(h, x, gains, wq, wk_t, wv_t, held=None):
    depth = 2048 // KSTEP
    chips = CHIPS // KSTEP
    in_specs = [
        pl.BlockSpec((chips, HALF, LANE), lambda k, h: (k, 0, 0)),
        pl.BlockSpec((chips, 16, LANE), lambda k, h: (k, HALF // 16, 0)),
        pl.BlockSpec((depth, 256), lambda k, h: (k, 0)),
        pl.BlockSpec((16, depth), lambda k, h: (0, k)),
        pl.BlockSpec((16, depth), lambda k, h: (0, k)),
    ]
    operands = [h, x, gains, wq, wk_t, wv_t]
    aliases = {}
    if held is not None:
        in_specs.append(pl.BlockSpec(memory_space=pl.ANY))
        operands.append(held)
        aliases = {6: 0}
    return pl.pallas_call(
        qkv_kernel,
        grid_spec=pltpu.PrefetchScalarGridSpec(
            num_scalar_prefetch=1,
            grid=(KSTEP,),
            in_specs=in_specs,
            out_specs=(
                pl.BlockSpec((HALF // SEQ, SEQ + 16, 256), lambda k, h: (h[0], 0, 0)),
                pl.BlockSpec((chips, 16, LANE), lambda k, h: (k, 0, 0)),
            ),
            scratch_shapes=[
                pltpu.VMEM((HALF, 256), F32),
                pltpu.VMEM((32, HALF), F32),
                pltpu.VMEM((HALF, LANE), F32),
            ],
        ),
        out_shape=(
            jax.ShapeDtypeStruct((ROWS, SEQ + 16, 256), BF),
            jax.ShapeDtypeStruct((CHIPS, 16, LANE), BF),
        ),
        input_output_aliases=aliases,
        compiler_params=params(),
        cost_estimate=pl.CostEstimate(
            flops=2 * HALF * 2048 * 384, bytes_accessed=4 * 1024 * 1024, transcendentals=0
        ),
        name="qkv_half",
    )(*operands)


def qkv_sum_kernel(p_ref, q_ref, kv_ref):
    total = p_ref[0].astype(F32)
    for j in range(1, ROWS):
        total = total + p_ref[j].astype(F32)
    extra = total[SEQ:, SEQ:LANE] + total[SEQ:, LANE + SEQ :]
    squares = jnp.concatenate([extra[j : j + 1] for j in range(3)] + [extra[3:4]], axis=1)
    inv = lax.rsqrt(squares / D + EPS)
    down = jnp.transpose(jnp.broadcast_to(inv, (LANE, LANE)))[:SEQ]
    q_ref[...] = total[:SEQ] * jnp.concatenate([down, down], axis=1)
    kv = jnp.concatenate([total[96:112, :SEQ], total[96:112, LANE : LANE + SEQ]], axis=0)
    kv = kv * inv[:, :SEQ]
    for j in range(8):
        kv_ref[j] = kv


def qkv_sum(parts):
    return pl.pallas_call(
        qkv_sum_kernel,
        out_shape=(
            jax.ShapeDtypeStruct((SEQ, 256), F32),
            jax.ShapeDtypeStruct((8, 32, SEQ), F32),
        ),
        compiler_params=params(),
        name="qkv_sum",
    )(parts)


def attend_kernel(len_ref, q_ref, kv_ref, seg_ref, table_ref, out_ref):
    cos, sin = table_ref[0], table_ref[1]
    cos_t, sin_t = jnp.transpose(cos)[:, :SEQ], jnp.transpose(sin)[:, :SEQ]
    cos, sin = cos[:SEQ], sin[:SEQ]
    keys = jnp.concatenate([kv_ref[j, :16] for j in range(8)], axis=0)
    turned = jnp.concatenate([keys[64:], keys[:64]], axis=0)
    keys = (keys * cos_t + turned * sin_t).astype(BF)
    values = jnp.concatenate([kv_ref[j, 16:] for j in range(8)], axis=0).astype(BF)
    seg = jnp.concatenate([seg_ref[...].astype(F32), jnp.zeros((1, LANE - SEQ), F32)], axis=1)
    seg = jnp.broadcast_to(seg, (LANE, LANE))
    same = (seg == jnp.transpose(seg))[:SEQ, :SEQ]
    q_at = lax.broadcasted_iota(jnp.int32, (SEQ, SEQ), 0)
    k_at = lax.broadcasted_iota(jnp.int32, (SEQ, SEQ), 1)
    allowed = same & (k_at <= q_at) & (k_at < len_ref[0])
    allowed = allowed | (k_at == q_at)
    for head in range(2):
        query = q_ref[:, head * HEAD_DIM : (head + 1) * HEAD_DIM]
        query = (query * cos + pltpu.roll(query, 64, 1) * sin).astype(BF)
        scores = nn(query, keys) * (1.0 / math.sqrt(HEAD_DIM))
        scores = jnp.where(allowed, scores, F32(-1e30))
        expo = jnp.exp(scores - jnp.max(scores, axis=1, keepdims=True))
        soft = (expo / jnp.sum(expo, axis=1, keepdims=True)).astype(BF)
        attended = nt(soft, values).astype(BF)
        for j in range(ROWS):
            out_ref[j, :, head * HEAD_DIM : (head + 1) * HEAD_DIM] = attended


def attend(lengths, q, kv, segments):
    vmem = pl.BlockSpec(memory_space=pltpu.VMEM)
    return pl.pallas_call(
        attend_kernel,
        in_specs=[pl.BlockSpec(memory_space=pltpu.SMEM)] + [vmem] * 4,
        out_specs=vmem,
        out_shape=jax.ShapeDtypeStruct((ROWS, SEQ, 256), BF),
        compiler_params=params(),
        name="attend",
    )(lengths, q, kv, segments.reshape(1, SEQ), rope_table())


def proj_kernel(h_ref, x_ref, w_ref, out_ref):
    result = nn(x_ref[...], w_ref[...]).astype(out_ref.dtype)
    for j in range(out_ref.shape[0]):
        out_ref[j] = result[:, j * LANE : (j + 1) * LANE]


def proj_half(h, x, w, dtype):
    depth = x.shape[1]
    steps = 2
    wide = 2048 // steps
    return pl.pallas_call(
        proj_kernel,
        grid_spec=pltpu.PrefetchScalarGridSpec(
            num_scalar_prefetch=1,
            grid=(steps,),
            in_specs=[
                pl.BlockSpec((HALF, depth), lambda i, h: (h[0], 0)),
                pl.BlockSpec((depth, wide), lambda i, h: (0, i)),
            ],
            out_specs=pl.BlockSpec((wide // LANE, HALF, LANE), lambda i, h: (i, 0, 0)),
        ),
        out_shape=jax.ShapeDtypeStruct((CHIPS, HALF, LANE), dtype),
        compiler_params=params(),
        cost_estimate=pl.CostEstimate(
            flops=2 * HALF * 2048 * depth, bytes_accessed=4 * 1024 * 1024, transcendentals=0
        ),
        name="proj_half",
    )(h, x, w)


def project_out(mine, theirs, x, w):
    given = proj_half(theirs, x, w, BF)
    got = swap(given)
    kept = proj_half(mine, x, w, F32)
    return over_chips((kept + got.astype(F32)).astype(BF))


def residual_kernel(base_ref, p_ref, out_ref):
    total = p_ref[0].astype(F32)
    for j in range(1, CHIPS):
        total = total + p_ref[j].astype(F32)
    out_ref[...] = (base_ref[:HALF].astype(F32) + total).astype(BF)


def residual_sum(base, parts):
    return pl.pallas_call(
        residual_kernel,
        out_shape=jax.ShapeDtypeStruct((HALF, LANE), BF),
        compiler_params=params(),
        name="residual_sum",
    )(base, parts)


def final_kernel(h_ref, base_ref, p_ref, keep_ref, give_ref):
    total = p_ref[0].astype(F32)
    for j in range(1, CHIPS):
        total = total + p_ref[j].astype(F32)
    done = (base_ref[...].astype(F32) + total).astype(BF)
    first, second = done[:, :64], done[:, 64:]
    keep_ref[...] = jnp.where(h_ref[0] == 0, first, second)
    give_ref[...] = jnp.where(h_ref[0] == 0, second, first)


def final_sum(h, base, parts):
    vmem = pl.BlockSpec(memory_space=pltpu.VMEM)
    return pl.pallas_call(
        final_kernel,
        in_specs=[pl.BlockSpec(memory_space=pltpu.SMEM), vmem, vmem],
        out_specs=(vmem, vmem),
        out_shape=(jax.ShapeDtypeStruct((HALF, 64), BF),) * 2,
        compiler_params=params(),
        name="final_sum",
    )(h, base, parts)


def place_kernel(h_ref, keep_ref, got_ref, out_ref):
    keep, got = keep_ref[...], got_ref[...]
    out_ref[:, :HALF] = jnp.transpose(jnp.where(h_ref[0] == 0, keep, got))
    out_ref[:, HALF:] = jnp.transpose(jnp.where(h_ref[0] == 0, got, keep))


def place_halves(h, keep, got):
    vmem = pl.BlockSpec(memory_space=pltpu.VMEM)
    return pl.pallas_call(
        place_kernel,
        in_specs=[pl.BlockSpec(memory_space=pltpu.SMEM), vmem, vmem],
        out_specs=vmem,
        out_shape=jax.ShapeDtypeStruct((64, TOK), BF),
        compiler_params=params(),
        name="place_halves",
    )(h, keep, got).T


def cut_kernel(h_ref, other_ref, at_ref, place_ref, t_ref, ga_ref, gf_ref, keep_ref, give_ref):
    row = lax.broadcasted_iota(jnp.int32, (16, 64), 0)
    ga, gf = ga_ref[...].astype(F32), gf_ref[...].astype(F32)
    gains = jnp.where(row == 0, ga, jnp.where(row == 1, gf, 0.0)).astype(BF)
    keep_ref[HALF:] = gains
    give_ref[HALF:] = gains
    first = jnp.transpose(t_ref[:, :HALF])
    second = jnp.transpose(t_ref[:, HALF:])
    keep_ref[:HALF] = jnp.where(h_ref[0] == 0, first, second)
    give_ref[:HALF] = jnp.where(h_ref[0] == 0, second, first)


def cut_tokens(h, other, at, place, tokens_t, norm_attn, norm_ffn):
    whole = lambda *shape: pl.BlockSpec(shape, lambda i: (0, 0))
    return pl.pallas_call(
        cut_kernel,
        grid=(1,),
        in_specs=[
            pl.BlockSpec(memory_space=pltpu.SMEM),
            pl.BlockSpec(memory_space=pltpu.SMEM),
            pl.BlockSpec(memory_space=pltpu.SMEM),
            pl.BlockSpec(memory_space=pltpu.SMEM),
            whole(64, TOK),
            whole(1, 64),
            whole(1, 64),
        ],
        out_specs=(whole(HALF + 16, 64), whole(HALF + 16, 64)),
        out_shape=(jax.ShapeDtypeStruct((HALF + 16, 64), BF),) * 2,
        compiler_params=params(),
        name="cut_tokens",
    )(h, other, at, place, tokens_t, norm_attn.reshape(1, 64), norm_ffn.reshape(1, 64))


def join_kernel(h_ref, keep_ref, got_ref, out_ref):
    keep, got = keep_ref[...], got_ref[...]
    mine_first = jnp.concatenate([keep, got], axis=1)
    mine_last = jnp.concatenate([got, keep], axis=1)
    out_ref[...] = jnp.where(h_ref[0] == 0, mine_first, mine_last)


def join_cores(h, keep, got):
    vmem = pl.BlockSpec(memory_space=pltpu.VMEM)
    return pl.pallas_call(
        join_kernel,
        in_specs=[pl.BlockSpec(memory_space=pltpu.SMEM), vmem, vmem],
        out_specs=vmem,
        out_shape=jax.ShapeDtypeStruct((HALF + 16, LANE), BF),
        compiler_params=params(),
        name="join_cores",
    )(h, keep, got)


def gained_rows(x_ref, g_ref, xs):
    for j in range(CHIPS):
        gain = g_ref[j, 1:2].astype(F32)
        xs[:, j * LANE : (j + 1) * LANE] = (x_ref[j].astype(F32) * gain).astype(BF)


def gate_up_main_kernel(h_ref, x_ref, g_ref, wg_ref, wu_ref, *rest):
    out_ref, made_ref, xs = rest[-3:]
    step = pl.program_id(0)
    made_ref[0] = step

    @pl.when(step == 0)
    def _():
        gained_rows(x_ref, g_ref, xs)

    wide = wg_ref.shape[0]
    at = pl.multiple_of(step * wide, wide)
    out_ref[:, pl.ds(at, wide)] = nt(xs[...], wg_ref[...]).astype(BF)
    out_ref[:, pl.ds(MAIN + at, wide)] = nt(xs[...], wu_ref[...]).astype(BF)


def gate_up_main(h, x, gains, wg_t, wu_t, held=None):
    steps = 1
    wide = MAIN // steps
    in_specs = [
        pl.BlockSpec((CHIPS, HALF, LANE), lambda i, h: (0, 0, 0)),
        pl.BlockSpec((CHIPS, 16, LANE), lambda i, h: (0, 0, 0)),
        pl.BlockSpec((wide, 2048), lambda i, h: (i, 0)),
        pl.BlockSpec((wide, 2048), lambda i, h: (i, 0)),
    ]
    operands = [h, x, gains, wg_t, wu_t]
    aliases = {}
    if held is not None:
        in_specs.append(pl.BlockSpec(memory_space=pl.ANY))
        operands.append(held)
        aliases = {5: 0}
    return pl.pallas_call(
        gate_up_main_kernel,
        grid_spec=pltpu.PrefetchScalarGridSpec(
            num_scalar_prefetch=1,
            grid=(steps,),
            in_specs=in_specs,
            out_specs=(
                pl.BlockSpec((HALF, 2 * MAIN), lambda i, h: (h[0], 0)),
                pl.BlockSpec(memory_space=pltpu.SMEM),
            ),
            scratch_shapes=[pltpu.VMEM((HALF, 2048), BF)],
        ),
        out_shape=(
            jax.ShapeDtypeStruct((TOK, 2 * MAIN), BF),
            jax.ShapeDtypeStruct((1,), jnp.int32),
        ),
        input_output_aliases=aliases,
        compiler_params=params(24),
        cost_estimate=pl.CostEstimate(
            flops=4 * HALF * 2048 * MAIN,
            bytes_accessed=8 * 1024 * 1024,
            transcendentals=0,
        ),
        name="gate_up_main",
    )(*operands)


def gate_up_side_kernel(h_ref, own_ref, other_ref, g_ref, wg_ref, wu_ref, _, out_ref, xs):
    lane = lax.broadcasted_iota(jnp.int32, (HALF, SIDE // 2 - REST), 1)
    for x_ref, half in ((own_ref, h_ref[0]), (other_ref, 1 - h_ref[0])):
        gained_rows(x_ref, g_ref, xs)
        squares = None
        for j in range(CHIPS):
            wide = x_ref[j].astype(F32)
            squares = wide * wide if squares is None else squares + wide * wide
        high, low = split_two(jnp.sum(squares, axis=1, keepdims=True))
        extra = jnp.where(lane == 0, high, jnp.where(lane == 1, low, 0.0))
        rows = pl.ds(pl.multiple_of(half * HALF, HALF), HALF)
        gate = jnp.concatenate([nt(xs[...], wg_ref[...]), extra], axis=1)
        out_ref[rows, : SIDE // 2] = gate.astype(BF)
        up = jnp.concatenate([nt(xs[...], wu_ref[...]), jnp.zeros_like(extra)], axis=1)
        out_ref[rows, SIDE // 2 :] = up.astype(BF)


def gate_up_side(h, own, other, gains, wg_t, wu_t, made):
    x_spec = pl.BlockSpec((CHIPS, HALF, LANE), lambda i, h: (0, 0, 0))
    w_spec = pl.BlockSpec((pl.Element(REST), pl.Element(2048)), lambda i, h: (MAIN, 0))
    return pl.pallas_call(
        gate_up_side_kernel,
        grid_spec=pltpu.PrefetchScalarGridSpec(
            num_scalar_prefetch=1,
            grid=(1,),
            in_specs=[
                x_spec,
                x_spec,
                pl.BlockSpec((CHIPS, 16, LANE), lambda i, h: (0, 0, 0)),
                w_spec,
                w_spec,
                pl.BlockSpec(memory_space=pltpu.SMEM),
            ],
            out_specs=pl.BlockSpec((TOK, SIDE), lambda i, h: (0, 0)),
            scratch_shapes=[pltpu.VMEM((HALF, 2048), BF)],
        ),
        out_shape=jax.ShapeDtypeStruct((TOK, SIDE), BF),
        compiler_params=params(58),
        cost_estimate=pl.CostEstimate(
            flops=4 * TOK * 2048 * REST, bytes_accessed=6 * 1024 * 1024, transcendentals=0
        ),
        name="gate_up_side",
    )(h, own, other, gains, wg_t, wu_t, made)


def hidden_kernel(main_ref, side_ref, out_ref):
    side = side_ref[0].astype(F32)
    for j in range(1, ROWS):
        side = side + side_ref[j].astype(F32)
    squares = side[:, REST : REST + 1] + side[:, REST + 1 : REST + 2]
    inv = lax.rsqrt(squares / D + EPS)

    def gated(gate, up):
        gate, up = gate * inv, up * inv
        return (gate / (1.0 + jnp.exp(-gate)) * up).astype(BF)

    first = gated(main_ref[:, :MAIN].astype(F32), main_ref[:, MAIN:].astype(F32))
    second = gated(side[:, :REST], side[:, SIDE // 2 : SIDE // 2 + REST])
    out_ref[:, :MAIN] = first
    out_ref[:, MAIN:] = second


def hidden_row(main, side):
    return pl.pallas_call(
        hidden_kernel,
        out_shape=jax.ShapeDtypeStruct((SEQ, FFL), BF),
        compiler_params=params(),
        name="hidden_row",
    )(main, side)


def from_ahead(x, k):
    return lax.ppermute(x, "gx", [(i, (i - k) % ROWS) for i in range(ROWS)])


def order_kernel(at_ref, *refs):
    out_ref = refs[-1]
    for k, ref in enumerate(refs[:-1]):
        out_ref[lax.rem(at_ref[0] + k, ROWS)] = ref[...]


def all_rows(at, x):
    ahead = {0: x}
    for k in (1, 7, 3, 5):
        ahead[k] = from_ahead(x, k)
    ahead[2] = from_ahead(ahead[1], 1)
    ahead[6] = from_ahead(ahead[7], 7)
    ahead[4] = from_ahead(ahead[3], 1)
    vmem = pl.BlockSpec(memory_space=pltpu.VMEM)
    return pl.pallas_call(
        order_kernel,
        in_specs=[pl.BlockSpec(memory_space=pltpu.SMEM)] + [vmem] * ROWS,
        out_specs=vmem,
        out_shape=jax.ShapeDtypeStruct((ROWS,) + x.shape, x.dtype),
        compiler_params=params(),
        name="order_rows",
    )(at, *[ahead[k] for k in range(ROWS)])


def rope_table():
    inv_freq = np.power(
        np.float32(ROPE_BASE), -(np.arange(64, dtype=np.float32) * np.float32(2.0 / HEAD_DIM))
    ).astype(np.float32)
    angles = (np.arange(SEQ, dtype=np.float32)[:, None] * inv_freq[None, :]).astype(np.float64)
    cos, sin = np.cos(angles), np.sin(angles)
    table = np.zeros((2, LANE, LANE), np.float32)
    table[0, :SEQ] = np.concatenate([cos, cos], axis=1)
    table[1, :SEQ] = np.concatenate([-sin, sin], axis=1)
    return table


def per_device(
    tokens,
    norm_attn,
    w_query,
    w_key,
    w_value,
    w_out,
    norm_ffn,
    w_gate,
    w_up,
    w_down,
    lengths,
    segments,
):
    core, at = lax.axis_index("gy") % 2, jnp.reshape(lax.axis_index("gx"), (1,))
    mine, theirs = jnp.reshape(core, (1,)), jnp.reshape(1 - core, (1,))
    place = jnp.reshape(lax.axis_index("gy"), (1,))

    keep, give = cut_tokens(mine, theirs, at, place, tokens.T, norm_attn, norm_ffn)
    base = join_cores(mine, keep, swap(give))
    first, other = from_chips(place, base)
    held, gains = qkv_half(mine, first, first, w_query, w_key.T, w_value.T)
    parts, _ = qkv_half(theirs, other, first, w_query, w_key.T, w_value.T, held)
    q, kv = qkv_sum(over_rows(parts))
    kv = lax.all_to_all(kv, "gy", 0, 0, axis_index_groups=KV_GROUPS, tiled=True)
    attended = over_rows(attend(lengths, q, kv, segments)).reshape(TOK, 256)
    residual = residual_sum(base, project_out(mine, theirs, attended, w_out))

    own, other = from_chips(place, residual)
    weights = (w_gate.T, w_up.T)
    held, _ = gate_up_main(mine, own, gains, *weights)
    main, made = gate_up_main(theirs, other, gains, *weights, held)
    side = gate_up_side(mine, own, other, gains, *weights, made)
    main = lax.psum_scatter(main, "gx", scatter_dimension=0, tiled=True)
    side = over_rows(side.reshape(ROWS, SEQ, SIDE))
    hidden = all_rows(at, hidden_row(main, side)).reshape(TOK, FFL)
    keep, give = final_sum(mine, residual, project_out(mine, theirs, hidden, w_down))
    return place_halves(mine, keep, swap(give))


def solution(mesh):
    in_specs = (
        P(None, ("gx", "gy")),
        P(("gx", "gy")),
        P("gx", "gy"),
        P("gx", "gy"),
        P("gx", "gy"),
        P("gy", "gx"),
        P(("gx", "gy")),
        P("gx", "gy"),
        P("gx", "gy"),
        P("gy", "gx"),
        P("gx"),
        P("gx"),
    )
    out_specs = P(None, ("gx", "gy"))
    return jax.shard_map(
        per_device, mesh=mesh, in_specs=in_specs, out_specs=out_specs, check_vma=False
    )
```

```python
import functools
import math

import jax
import jax.numpy as jnp
import numpy as np
from jax import lax
from jax.experimental import pallas as pl
from jax.experimental.pallas import tpu as pltpu
from jax.sharding import PartitionSpec as P

D = 16384
HEADS = 64
KV_HEADS = 4
HEAD_DIM = 128
SEQ = 96
EPS = 1e-05
ROPE_BASE = 500000.0

BF = jnp.bfloat16
F32 = jnp.float32

TOK = 768
HALF = 384
CHIPS = 16
LANE = 128
ROWS = 8
KSTEP = 4
FFL = 832
MAIN = 768
REST = FFL - MAIN
SIDE = 256
CHIP_GROUPS = [[2 * i + c for i in range(CHIPS)] for c in range(2)]
KV_GROUPS = [list(range(8 * i, 8 * i + 8)) for i in range(4)]


def swap(x):
    return lax.ppermute(x, "gy", [(i, i ^ 1) for i in range(32)])


def over_chips(x):
    return lax.all_to_all(x, "gy", 0, 0, axis_index_groups=CHIP_GROUPS, tiled=True)


def over_ring(x, k, stage):
    pairs = []
    for i in range(32):
        y, across, core = i // 8, i // 2 % 4, i % 2
        if (core == 0) == (stage == 0):
            across = (across + k) % 4
        else:
            y = (y + k) % 4
        pairs.append((y * 8 + across * 2 + core, i))
    return lax.ppermute(x, "gy", pairs)


def stack_kernel(*refs):
    for j, ref in enumerate(refs[:-1]):
        refs[-1][j] = ref[...]


def order_chips_kernel(of_other, g_ref, *refs):
    out_ref = refs[-1]
    core = lax.rem(g_ref[0], 2)
    core = 1 - core if of_other else core
    across, y = lax.rem(lax.div(g_ref[0], 2), 4), lax.div(g_ref[0], 8)
    for a in range(4):
        for b in range(4):
            here_y = lax.rem(y + jnp.where(core == 0, a, b), 4)
            here_x = lax.rem(across + jnp.where(core == 0, b, a), 4)
            out_ref[here_y * 4 + here_x] = refs[a][b]


def from_chips(g, x):
    vmem = pl.BlockSpec(memory_space=pltpu.VMEM)
    line = pl.pallas_call(
        stack_kernel,
        in_specs=[vmem] * 4,
        out_specs=vmem,
        out_shape=jax.ShapeDtypeStruct((4,) + x.shape, x.dtype),
        compiler_params=params(),
        name="stack_line",
    )(x, *[over_ring(x, k, 0) for k in (1, 2, 3)])
    pieces = [line] + [over_ring(line, k, 1) for k in (1, 2, 3)]

    def ordered(of_other, pieces):
        return pl.pallas_call(
            functools.partial(order_chips_kernel, of_other),
            in_specs=[pl.BlockSpec(memory_space=pltpu.SMEM)] + [vmem] * 4,
            out_specs=vmem,
            out_shape=jax.ShapeDtypeStruct((CHIPS,) + x.shape, x.dtype),
            compiler_params=params(),
            name="order_chips",
        )(g, *pieces)

    return ordered(False, pieces), ordered(True, [swap(piece) for piece in pieces])


def over_rows(x):
    return lax.all_to_all(x, "gx", 0, 0, tiled=True)


def params(mib=16):
    return pltpu.CompilerParams(vmem_limit_bytes=mib * 1024 * 1024)


def nt(a, b):
    return lax.dot_general(a, b, (((1,), (1,)), ((), ())), preferred_element_type=F32)


def nn(a, b):
    return jnp.dot(a, b, preferred_element_type=F32)


def fold_squares(wide):
    total = None
    for j in range(wide.shape[1] // LANE):
        part = wide[:, j * LANE : (j + 1) * LANE]
        total = part * part if total is None else total + part * part
    return total


def split_two(total):
    high = total.astype(BF).astype(F32)
    return high, total - high


def gained_block(x_ref, g_ref, row):
    chips = range(x_ref.shape[0])
    wide = jnp.concatenate([x_ref[j, :HALF] for j in chips], axis=1).astype(F32)
    gain = jnp.concatenate([g_ref[j, row : row + 1] for j in chips], axis=1).astype(F32)
    return wide, (wide * gain).astype(BF)


def qkv_kernel(h_ref, x_ref, g_ref, wq_ref, wk_ref, wv_ref, *rest):
    out_ref, gains_ref, acc_q, acc_kv, acc_sq = rest[-5:]
    k = pl.program_id(0)
    gains_ref[...] = g_ref[...]

    @pl.when(k == 0)
    def _():
        acc_q[...] = jnp.zeros_like(acc_q)
        acc_kv[...] = jnp.zeros_like(acc_kv)
        acc_sq[...] = jnp.zeros_like(acc_sq)

    wide, gained = gained_block(x_ref, g_ref, 0)
    acc_sq[...] += fold_squares(wide)
    acc_q[...] += nn(gained, wq_ref[...])
    acc_kv[...] += nt(jnp.concatenate([wk_ref[...], wv_ref[...]], axis=0), gained)

    @pl.when(k == pl.num_programs(0) - 1)
    def _():
        high, low = split_two(jnp.sum(jnp.transpose(acc_sq[...]), axis=0, keepdims=True))
        def squeezed(row):
            cuts = [row[:, j * 32 : (j + 1) * 32] for j in range(SEQ // 32)]
            return jnp.concatenate(cuts + [jnp.zeros((16 - SEQ // 32, 32), F32)], axis=0)

        for r in range(HALF // SEQ):
            here = slice(r * SEQ, (r + 1) * SEQ)
            kv = acc_kv[:, here]
            out_ref[r, :SEQ] = acc_q[here].astype(BF)
            below = [kv[:16], squeezed(high[:, here]), kv[16:], squeezed(low[:, here])]
            out_ref[r, SEQ:] = jnp.concatenate(below, axis=1).astype(BF)


def qkv_half(h, x, gains, wq, wk_t, wv_t, held=None):
    depth = 2048 // KSTEP
    chips = CHIPS // KSTEP
    in_specs = [
        pl.BlockSpec((chips, HALF, LANE), lambda k, h: (k, 0, 0)),
        pl.BlockSpec((chips, 16, LANE), lambda k, h: (k, HALF // 16, 0)),
        pl.BlockSpec((depth, 256), lambda k, h: (k, 0)),
        pl.BlockSpec((16, depth), lambda k, h: (0, k)),
        pl.BlockSpec((16, depth), lambda k, h: (0, k)),
    ]
    operands = [h, x, gains, wq, wk_t, wv_t]
    aliases = {}
    if held is not None:
        in_specs.append(pl.BlockSpec(memory_space=pl.ANY))
        operands.append(held)
        aliases = {6: 0}
    return pl.pallas_call(
        qkv_kernel,
        grid_spec=pltpu.PrefetchScalarGridSpec(
            num_scalar_prefetch=1,
            grid=(KSTEP,),
            in_specs=in_specs,
            out_specs=(
                pl.BlockSpec((HALF // SEQ, SEQ + 16, 256), lambda k, h: (h[0], 0, 0)),
                pl.BlockSpec((chips, 16, LANE), lambda k, h: (k, 0, 0)),
            ),
            scratch_shapes=[
                pltpu.VMEM((HALF, 256), F32),
                pltpu.VMEM((32, HALF), F32),
                pltpu.VMEM((HALF, LANE), F32),
            ],
        ),
        out_shape=(
            jax.ShapeDtypeStruct((ROWS, SEQ + 16, 256), BF),
            jax.ShapeDtypeStruct((CHIPS, 16, LANE), BF),
        ),
        input_output_aliases=aliases,
        compiler_params=params(),
        cost_estimate=pl.CostEstimate(
            flops=2 * HALF * 2048 * 384, bytes_accessed=4 * 1024 * 1024, transcendentals=0
        ),
        name="qkv_half",
    )(*operands)


def qkv_sum_kernel(p_ref, q_ref, kv_ref):
    total = p_ref[0].astype(F32)
    for j in range(1, ROWS):
        total = total + p_ref[j].astype(F32)
    extra = total[SEQ:, SEQ:LANE] + total[SEQ:, LANE + SEQ :]
    squares = jnp.concatenate([extra[j : j + 1] for j in range(3)] + [extra[3:4]], axis=1)
    inv = lax.rsqrt(squares / D + EPS)
    down = jnp.transpose(jnp.broadcast_to(inv, (LANE, LANE)))[:SEQ]
    q_ref[...] = total[:SEQ] * jnp.concatenate([down, down], axis=1)
    kv = jnp.concatenate([total[96:112, :SEQ], total[96:112, LANE : LANE + SEQ]], axis=0)
    kv = kv * inv[:, :SEQ]
    for j in range(8):
        kv_ref[j] = kv


def qkv_sum(parts):
    return pl.pallas_call(
        qkv_sum_kernel,
        out_shape=(
            jax.ShapeDtypeStruct((SEQ, 256), F32),
            jax.ShapeDtypeStruct((8, 32, SEQ), F32),
        ),
        compiler_params=params(),
        name="qkv_sum",
    )(parts)


def attend_kernel(len_ref, q_ref, kv_ref, seg_ref, table_ref, out_ref):
    cos, sin = table_ref[0], table_ref[1]
    cos_t, sin_t = jnp.transpose(cos)[:, :SEQ], jnp.transpose(sin)[:, :SEQ]
    cos, sin = cos[:SEQ], sin[:SEQ]
    keys = jnp.concatenate([kv_ref[j, :16] for j in range(8)], axis=0)
    turned = jnp.concatenate([keys[64:], keys[:64]], axis=0)
    keys = (keys * cos_t + turned * sin_t).astype(BF)
    values = jnp.concatenate([kv_ref[j, 16:] for j in range(8)], axis=0).astype(BF)
    seg = jnp.concatenate([seg_ref[...].astype(F32), jnp.zeros((1, LANE - SEQ), F32)], axis=1)
    seg = jnp.broadcast_to(seg, (LANE, LANE))
    same = (seg == jnp.transpose(seg))[:SEQ, :SEQ]
    q_at = lax.broadcasted_iota(jnp.int32, (SEQ, SEQ), 0)
    k_at = lax.broadcasted_iota(jnp.int32, (SEQ, SEQ), 1)
    allowed = same & (k_at <= q_at) & (k_at < len_ref[0])
    allowed = allowed | (k_at == q_at)
    for head in range(2):
        query = q_ref[:, head * HEAD_DIM : (head + 1) * HEAD_DIM]
        query = (query * cos + pltpu.roll(query, 64, 1) * sin).astype(BF)
        scores = nn(query, keys) * (1.0 / math.sqrt(HEAD_DIM))
        scores = jnp.where(allowed, scores, F32(-1e30))
        expo = jnp.exp(scores - jnp.max(scores, axis=1, keepdims=True))
        soft = (expo / jnp.sum(expo, axis=1, keepdims=True)).astype(BF)
        attended = nt(soft, values).astype(BF)
        out_ref[:, head * HEAD_DIM : (head + 1) * HEAD_DIM] = attended


def attend(lengths, q, kv, segments):
    vmem = pl.BlockSpec(memory_space=pltpu.VMEM)
    return pl.pallas_call(
        attend_kernel,
        in_specs=[pl.BlockSpec(memory_space=pltpu.SMEM)] + [vmem] * 4,
        out_specs=vmem,
        out_shape=jax.ShapeDtypeStruct((SEQ, 256), BF),
        compiler_params=params(),
        name="attend",
    )(lengths, q, kv, segments.reshape(1, SEQ), rope_table())


def proj_kernel(h_ref, x_ref, w_ref, out_ref):
    result = nn(x_ref[...], w_ref[...]).astype(out_ref.dtype)
    for j in range(out_ref.shape[0]):
        out_ref[j] = result[:, j * LANE : (j + 1) * LANE]


def proj_half(h, x, w, dtype):
    depth = x.shape[1]
    steps = 2
    wide = 2048 // steps
    return pl.pallas_call(
        proj_kernel,
        grid_spec=pltpu.PrefetchScalarGridSpec(
            num_scalar_prefetch=1,
            grid=(steps,),
            in_specs=[
                pl.BlockSpec((HALF, depth), lambda i, h: (h[0], 0)),
                pl.BlockSpec((depth, wide), lambda i, h: (0, i)),
            ],
            out_specs=pl.BlockSpec((wide // LANE, HALF, LANE), lambda i, h: (i, 0, 0)),
        ),
        out_shape=jax.ShapeDtypeStruct((CHIPS, HALF, LANE), dtype),
        compiler_params=params(),
        cost_estimate=pl.CostEstimate(
            flops=2 * HALF * 2048 * depth, bytes_accessed=4 * 1024 * 1024, transcendentals=0
        ),
        name="proj_half",
    )(h, x, w)


def project_out(mine, theirs, x, w):
    given = proj_half(theirs, x, w, BF)
    got = swap(given)
    kept = proj_half(mine, x, w, F32)
    return over_chips((kept + got.astype(F32)).astype(BF))


def residual_kernel(base_ref, p_ref, out_ref):
    total = p_ref[0].astype(F32)
    for j in range(1, CHIPS):
        total = total + p_ref[j].astype(F32)
    out_ref[...] = (base_ref[:HALF].astype(F32) + total).astype(BF)


def residual_sum(base, parts):
    return pl.pallas_call(
        residual_kernel,
        out_shape=jax.ShapeDtypeStruct((HALF, LANE), BF),
        compiler_params=params(),
        name="residual_sum",
    )(base, parts)


def final_kernel(h_ref, base_ref, p_ref, keep_ref, give_ref):
    total = p_ref[0].astype(F32)
    for j in range(1, CHIPS):
        total = total + p_ref[j].astype(F32)
    done = (base_ref[...].astype(F32) + total).astype(BF)
    first, second = done[:, :64], done[:, 64:]
    keep_ref[...] = jnp.where(h_ref[0] == 0, first, second)
    give_ref[...] = jnp.where(h_ref[0] == 0, second, first)


def final_sum(h, base, parts):
    vmem = pl.BlockSpec(memory_space=pltpu.VMEM)
    return pl.pallas_call(
        final_kernel,
        in_specs=[pl.BlockSpec(memory_space=pltpu.SMEM), vmem, vmem],
        out_specs=(vmem, vmem),
        out_shape=(jax.ShapeDtypeStruct((HALF, 64), BF),) * 2,
        compiler_params=params(),
        name="final_sum",
    )(h, base, parts)


def place_kernel(h_ref, keep_ref, got_ref, out_ref):
    keep, got = keep_ref[...], got_ref[...]
    out_ref[:, :HALF] = jnp.transpose(jnp.where(h_ref[0] == 0, keep, got))
    out_ref[:, HALF:] = jnp.transpose(jnp.where(h_ref[0] == 0, got, keep))


def place_halves(h, keep, got):
    vmem = pl.BlockSpec(memory_space=pltpu.VMEM)
    return pl.pallas_call(
        place_kernel,
        in_specs=[pl.BlockSpec(memory_space=pltpu.SMEM), vmem, vmem],
        out_specs=vmem,
        out_shape=jax.ShapeDtypeStruct((64, TOK), BF),
        compiler_params=params(),
        name="place_halves",
    )(h, keep, got).T


def cut_kernel(h_ref, other_ref, at_ref, place_ref, t_ref, ga_ref, gf_ref, keep_ref, give_ref):
    row = lax.broadcasted_iota(jnp.int32, (16, 64), 0)
    ga, gf = ga_ref[...].astype(F32), gf_ref[...].astype(F32)
    gains = jnp.where(row == 0, ga, jnp.where(row == 1, gf, 0.0)).astype(BF)
    keep_ref[HALF:] = gains
    give_ref[HALF:] = gains
    first = jnp.transpose(t_ref[:, :HALF])
    second = jnp.transpose(t_ref[:, HALF:])
    keep_ref[:HALF] = jnp.where(h_ref[0] == 0, first, second)
    give_ref[:HALF] = jnp.where(h_ref[0] == 0, second, first)


def cut_tokens(h, other, at, place, tokens_t, norm_attn, norm_ffn):
    whole = lambda *shape: pl.BlockSpec(shape, lambda i: (0, 0))
    return pl.pallas_call(
        cut_kernel,
        grid=(1,),
        in_specs=[
            pl.BlockSpec(memory_space=pltpu.SMEM),
            pl.BlockSpec(memory_space=pltpu.SMEM),
            pl.BlockSpec(memory_space=pltpu.SMEM),
            pl.BlockSpec(memory_space=pltpu.SMEM),
            whole(64, TOK),
            whole(1, 64),
            whole(1, 64),
        ],
        out_specs=(whole(HALF + 16, 64), whole(HALF + 16, 64)),
        out_shape=(jax.ShapeDtypeStruct((HALF + 16, 64), BF),) * 2,
        compiler_params=params(),
        name="cut_tokens",
    )(h, other, at, place, tokens_t, norm_attn.reshape(1, 64), norm_ffn.reshape(1, 64))


def join_kernel(h_ref, keep_ref, got_ref, out_ref):
    keep, got = keep_ref[...], got_ref[...]
    mine_first = jnp.concatenate([keep, got], axis=1)
    mine_last = jnp.concatenate([got, keep], axis=1)
    out_ref[...] = jnp.where(h_ref[0] == 0, mine_first, mine_last)


def join_cores(h, keep, got):
    vmem = pl.BlockSpec(memory_space=pltpu.VMEM)
    return pl.pallas_call(
        join_kernel,
        in_specs=[pl.BlockSpec(memory_space=pltpu.SMEM), vmem, vmem],
        out_specs=vmem,
        out_shape=jax.ShapeDtypeStruct((HALF + 16, LANE), BF),
        compiler_params=params(),
        name="join_cores",
    )(h, keep, got)


def gained_rows(x_ref, g_ref, xs):
    for j in range(CHIPS):
        gain = g_ref[j, 1:2].astype(F32)
        xs[:, j * LANE : (j + 1) * LANE] = (x_ref[j].astype(F32) * gain).astype(BF)


def gate_up_main_kernel(h_ref, x_ref, g_ref, wg_ref, wu_ref, *rest):
    out_ref, made_ref, xs = rest[-3:]
    step = pl.program_id(0)
    made_ref[0] = step

    @pl.when(step == 0)
    def _():
        gained_rows(x_ref, g_ref, xs)

    wide = wg_ref.shape[0]
    at = pl.multiple_of(step * wide, wide)
    out_ref[:, pl.ds(at, wide)] = nt(xs[...], wg_ref[...]).astype(BF)
    out_ref[:, pl.ds(MAIN + at, wide)] = nt(xs[...], wu_ref[...]).astype(BF)


def gate_up_main(h, x, gains, wg_t, wu_t, held=None):
    steps = 1
    wide = MAIN // steps
    in_specs = [
        pl.BlockSpec((CHIPS, HALF, LANE), lambda i, h: (0, 0, 0)),
        pl.BlockSpec((CHIPS, 16, LANE), lambda i, h: (0, 0, 0)),
        pl.BlockSpec((wide, 2048), lambda i, h: (i, 0)),
        pl.BlockSpec((wide, 2048), lambda i, h: (i, 0)),
    ]
    operands = [h, x, gains, wg_t, wu_t]
    aliases = {}
    if held is not None:
        in_specs.append(pl.BlockSpec(memory_space=pl.ANY))
        operands.append(held)
        aliases = {5: 0}
    return pl.pallas_call(
        gate_up_main_kernel,
        grid_spec=pltpu.PrefetchScalarGridSpec(
            num_scalar_prefetch=1,
            grid=(steps,),
            in_specs=in_specs,
            out_specs=(
                pl.BlockSpec((HALF, 2 * MAIN), lambda i, h: (h[0], 0)),
                pl.BlockSpec(memory_space=pltpu.SMEM),
            ),
            scratch_shapes=[pltpu.VMEM((HALF, 2048), BF)],
        ),
        out_shape=(
            jax.ShapeDtypeStruct((TOK, 2 * MAIN), BF),
            jax.ShapeDtypeStruct((1,), jnp.int32),
        ),
        input_output_aliases=aliases,
        compiler_params=params(24),
        cost_estimate=pl.CostEstimate(
            flops=4 * HALF * 2048 * MAIN,
            bytes_accessed=8 * 1024 * 1024,
            transcendentals=0,
        ),
        name="gate_up_main",
    )(*operands)


def gate_up_side_kernel(h_ref, own_ref, other_ref, g_ref, wg_ref, wu_ref, _, out_ref, xs):
    lane = lax.broadcasted_iota(jnp.int32, (HALF, SIDE // 2 - REST), 1)
    for x_ref, half in ((own_ref, h_ref[0]), (other_ref, 1 - h_ref[0])):
        gained_rows(x_ref, g_ref, xs)
        squares = None
        for j in range(CHIPS):
            wide = x_ref[j].astype(F32)
            squares = wide * wide if squares is None else squares + wide * wide
        high, low = split_two(jnp.sum(squares, axis=1, keepdims=True))
        extra = jnp.where(lane == 0, high, jnp.where(lane == 1, low, 0.0))
        rows = pl.ds(pl.multiple_of(half * HALF, HALF), HALF)
        gate = jnp.concatenate([nt(xs[...], wg_ref[...]), extra], axis=1)
        out_ref[rows, : SIDE // 2] = gate.astype(BF)
        up = jnp.concatenate([nt(xs[...], wu_ref[...]), jnp.zeros_like(extra)], axis=1)
        out_ref[rows, SIDE // 2 :] = up.astype(BF)


def gate_up_side(h, own, other, gains, wg_t, wu_t, made):
    x_spec = pl.BlockSpec((CHIPS, HALF, LANE), lambda i, h: (0, 0, 0))
    w_spec = pl.BlockSpec((pl.Element(REST), pl.Element(2048)), lambda i, h: (MAIN, 0))
    return pl.pallas_call(
        gate_up_side_kernel,
        grid_spec=pltpu.PrefetchScalarGridSpec(
            num_scalar_prefetch=1,
            grid=(1,),
            in_specs=[
                x_spec,
                x_spec,
                pl.BlockSpec((CHIPS, 16, LANE), lambda i, h: (0, 0, 0)),
                w_spec,
                w_spec,
                pl.BlockSpec(memory_space=pltpu.SMEM),
            ],
            out_specs=pl.BlockSpec((TOK, SIDE), lambda i, h: (0, 0)),
            scratch_shapes=[pltpu.VMEM((HALF, 2048), BF)],
        ),
        out_shape=jax.ShapeDtypeStruct((TOK, SIDE), BF),
        compiler_params=params(58),
        cost_estimate=pl.CostEstimate(
            flops=4 * TOK * 2048 * REST, bytes_accessed=6 * 1024 * 1024, transcendentals=0
        ),
        name="gate_up_side",
    )(h, own, other, gains, wg_t, wu_t, made)


def hidden_kernel(main_ref, side_ref, out_ref):
    side = side_ref[0].astype(F32)
    for j in range(1, ROWS):
        side = side + side_ref[j].astype(F32)
    squares = side[:, REST : REST + 1] + side[:, REST + 1 : REST + 2]
    inv = lax.rsqrt(squares / D + EPS)

    def gated(gate, up):
        gate, up = gate * inv, up * inv
        return (gate / (1.0 + jnp.exp(-gate)) * up).astype(BF)

    first = gated(main_ref[:, :MAIN].astype(F32), main_ref[:, MAIN:].astype(F32))
    second = gated(side[:, :REST], side[:, SIDE // 2 : SIDE // 2 + REST])
    out_ref[:, :MAIN] = first
    out_ref[:, MAIN:] = second


def hidden_row(main, side):
    return pl.pallas_call(
        hidden_kernel,
        out_shape=jax.ShapeDtypeStruct((SEQ, FFL), BF),
        compiler_params=params(),
        name="hidden_row",
    )(main, side)


def from_ahead(x, k):
    return lax.ppermute(x, "gx", [(i, (i - k) % ROWS) for i in range(ROWS)])


def order_kernel(at_ref, *refs):
    out_ref = refs[-1]
    for k, ref in enumerate(refs[:-1]):
        out_ref[lax.rem(at_ref[0] + k, ROWS)] = ref[...]


def all_rows(at, x):
    ahead = {0: x}
    for k in (1, 7, 3, 5):
        ahead[k] = from_ahead(x, k)
    ahead[2] = from_ahead(ahead[1], 1)
    ahead[6] = from_ahead(ahead[7], 7)
    ahead[4] = from_ahead(ahead[3], 1)
    vmem = pl.BlockSpec(memory_space=pltpu.VMEM)
    return pl.pallas_call(
        order_kernel,
        in_specs=[pl.BlockSpec(memory_space=pltpu.SMEM)] + [vmem] * ROWS,
        out_specs=vmem,
        out_shape=jax.ShapeDtypeStruct((ROWS,) + x.shape, x.dtype),
        compiler_params=params(),
        name="order_rows",
    )(at, *[ahead[k] for k in range(ROWS)])


def rope_table():
    inv_freq = np.power(
        np.float32(ROPE_BASE), -(np.arange(64, dtype=np.float32) * np.float32(2.0 / HEAD_DIM))
    ).astype(np.float32)
    angles = (np.arange(SEQ, dtype=np.float32)[:, None] * inv_freq[None, :]).astype(np.float64)
    cos, sin = np.cos(angles), np.sin(angles)
    table = np.zeros((2, LANE, LANE), np.float32)
    table[0, :SEQ] = np.concatenate([cos, cos], axis=1)
    table[1, :SEQ] = np.concatenate([-sin, sin], axis=1)
    return table


def per_device(
    tokens,
    norm_attn,
    w_query,
    w_key,
    w_value,
    w_out,
    norm_ffn,
    w_gate,
    w_up,
    w_down,
    lengths,
    segments,
):
    core, at = lax.axis_index("gy") % 2, jnp.reshape(lax.axis_index("gx"), (1,))
    mine, theirs = jnp.reshape(core, (1,)), jnp.reshape(1 - core, (1,))
    place = jnp.reshape(lax.axis_index("gy"), (1,))

    keep, give = cut_tokens(mine, theirs, at, place, tokens.T, norm_attn, norm_ffn)
    base = join_cores(mine, keep, swap(give))
    first, other = from_chips(place, base)
    held, gains = qkv_half(mine, first, first, w_query, w_key.T, w_value.T)
    parts, _ = qkv_half(theirs, other, first, w_query, w_key.T, w_value.T, held)
    q, kv = qkv_sum(over_rows(parts))
    kv = lax.all_to_all(kv, "gy", 0, 0, axis_index_groups=KV_GROUPS, tiled=True)
    attended = all_rows(at, attend(lengths, q, kv, segments)).reshape(TOK, 256)
    residual = residual_sum(base, project_out(mine, theirs, attended, w_out))

    own, other = from_chips(place, residual)
    weights = (w_gate.T, w_up.T)
    held, _ = gate_up_main(mine, own, gains, *weights)
    main, made = gate_up_main(theirs, other, gains, *weights, held)
    side = gate_up_side(mine, own, other, gains, *weights, made)
    main = lax.psum_scatter(main, "gx", scatter_dimension=0, tiled=True)
    side = over_rows(side.reshape(ROWS, SEQ, SIDE))
    hidden = all_rows(at, hidden_row(main, side)).reshape(TOK, FFL)
    keep, give = final_sum(mine, residual, project_out(mine, theirs, hidden, w_down))
    return place_halves(mine, keep, swap(give))


def solution(mesh):
    in_specs = (
        P(None, ("gx", "gy")),
        P(("gx", "gy")),
        P("gx", "gy"),
        P("gx", "gy"),
        P("gx", "gy"),
        P("gy", "gx"),
        P(("gx", "gy")),
        P("gx", "gy"),
        P("gx", "gy"),
        P("gy", "gx"),
        P("gx"),
        P("gx"),
    )
    out_specs = P(None, ("gx", "gy"))
    return jax.shard_map(
        per_device, mesh=mesh, in_specs=in_specs, out_specs=out_specs, check_vma=False
    )
```
